256 devices in a mesh: batch: 16 (over y_hi, z), seq: 16 (over x, y_lo, core).
Axes of the slice: x: 4, y: 4 (y_hi: 2, y_lo: 2; y = y_hi * 2 + y_lo), z: 8, core: 2. Of those that a mesh axis runs over, the one named last changes fastest.
Arguments:
- forward_embed: bfloat16 [98304, 1536], P(('batch', 'seq')), parts along dimension 0, may hold values from -6 to 6
- reverse_embed: bfloat16 [98304, 1536], P(('batch', 'seq')), parts along dimension 0, may hold values from -6 to 6
- conv_weight: bfloat16 [1, 3, 1536, 1536], P(None, None, 'seq'), may hold values from -0.09375 to 0.09375
- conv_bias: float32 [1, 1536], replicated, may hold values from -0.5 to 0.5
- head_weight: bfloat16 [1536, 1024], replicated, may hold values from -0.15625 to 0.15625
- head_bias: float32 [1024], replicated, may hold values from -1 to 1
Outputs:
- averaged: bfloat16 [98304, 1024], P(('batch', 'seq')), parts along dimension 0
The draws below stay inside these ranges and needn't reach their ends.
There are 16 independent parts, one for each index of `batch`. The reference program is written for one: setup_inputs(seed, part) draws one part's arguments, and reference() takes and returns one part's arrays. A program takes and returns all parts, laid end to end along the dimension named above; an argument that names none is the same for every part. Nothing has to cross between parts.
All inputs are finite; a program needn't handle non-finite values.
Results may differ from the reference program's by a relative error of at most 0.008.
Values may be sent and summed in bfloat16 or wider, within the bound.
No kernel may reach another device: no remote copies, remote signals or barrier semaphores. Data moves between devices by JAX's collectives and lax.ppermute only.
A program may use at most 128 MiB of HBM per device.

```python
import jax
import jax.numpy as jnp

CHANNELS = 1536
TRACKS = 1024
LAYERS = 1
BINS = 6144


def level_of(stream_key, shape, cuts, low, high):
    level, own = 1.0, jax.random.fold_in(stream_key, 6)
    for dim, shards_of in cuts:
        heights = jnp.exp(jax.random.uniform(jax.random.fold_in(own, dim), (shards_of,), jnp.float32, low / len(cuts), high / len(cuts)))
        level = level * jnp.repeat(heights, shape[dim] // shards_of).reshape([-1 if axis == dim else 1 for axis in range(len(shape))])
    return level


def normal_values(key, extent, spread, limit, cuts=(), dtype=jnp.bfloat16):
    result = spread * jax.random.normal(key, extent, jnp.float32)
    if cuts:
        result = result * level_of(key, extent, cuts, -0.22, 0.18)
    return jnp.clip(result, -limit, limit).astype(dtype)


def setup_inputs(seed: int = 0, part: int = 0) -> dict:
    streams_of = jax.random.split(jax.random.key(seed), 7)
    own_keys = jax.random.split(jax.random.fold_in(streams_of[6], part), 7)
    forward_embed = normal_values(own_keys[0], (BINS, CHANNELS), 1.0, 6.0, ((0, 16),))
    reverse_embed = normal_values(own_keys[1], (BINS, CHANNELS), 1.0, 6.0, ((0, 16),))
    conv_weight = normal_values(streams_of[2], (LAYERS, 3, CHANNELS, CHANNELS), (3 * CHANNELS) ** -0.5, 0.09375, ((2, 16),))
    conv_bias = jnp.clip(jax.random.uniform(streams_of[3], (LAYERS, CHANNELS), jnp.float32, -0.5, 0.5), -0.5, 0.5)
    head_weight = normal_values(streams_of[4], (CHANNELS, TRACKS), CHANNELS ** -0.5, 0.15625)
    head_bias = jnp.clip(jax.random.uniform(streams_of[5], (TRACKS,), jnp.float32, -1.0, 1.0), -1.0, 1.0)
    return dict(forward_embed=forward_embed, reverse_embed=reverse_embed, conv_weight=conv_weight, conv_bias=conv_bias, head_weight=head_weight, head_bias=head_bias)


def convolve(hidden, kernel, bias):
    count = hidden.shape[0]
    padded = jnp.pad(hidden, ((1, 1), (0, 0)))
    acc = jnp.zeros((count, kernel.shape[2]), jnp.float32)
    for tap in range(3):
        acc = acc + jnp.dot(padded[tap:tap + count], kernel[tap], preferred_element_type=jnp.float32)
    return jax.nn.gelu(acc + bias, approximate=False).astype(jnp.bfloat16)


def strand_tracks(embed, conv_weight, conv_bias, head_weight, head_bias):
    hidden = embed
    for layer in range(LAYERS):
        hidden = convolve(hidden, conv_weight[layer], conv_bias[layer])
    logits = jnp.dot(hidden, head_weight, preferred_element_type=jnp.float32) + head_bias
    return jax.nn.softplus(logits).astype(jnp.bfloat16)


def reference(forward_embed, reverse_embed, conv_weight, conv_bias, head_weight, head_bias):
    forward_tracks = strand_tracks(forward_embed, conv_weight, conv_bias, head_weight, head_bias)
    reverse_tracks = strand_tracks(reverse_embed, conv_weight, conv_bias, head_weight, head_bias)
    mean = 0.5 * (forward_tracks.astype(jnp.float32) + reverse_tracks[::-1].astype(jnp.float32))
    return mean.astype(jnp.bfloat16)
```

```python
import functools

import jax
import jax.numpy as jnp
from jax import lax
from jax.experimental import pallas as pl
from jax.experimental.pallas import tpu as pltpu
from jax.sharding import Mesh
from jax.sharding import PartitionSpec as P

AXES = ("y_hi", "z", "x", "y_lo", "core")
SEQ = ("x", "y_lo", "core")
XN, YN, CN = 4, 4, 2
CHUNKS = (512, 512, 512)
VMEM_LIMIT = 56 * 1024 * 1024
EDGE = 16
INV_SQRT2 = 0.7071067811865476


def core_swap(value):
    return lax.ppermute(value, "core", [(0, 1), (1, 0)])


def x_shift(value):
    route = []
    for x in range(XN):
        route += [(x * 2, (x + 1) % XN * 2), (x * 2 + 1, (x - 1) % XN * 2 + 1)]
    return lax.ppermute(value, ("x", "core"), route)


def y_shift(value):
    route = []
    for y in range(YN):
        route += [(y * 2, (y + 1) % YN * 2), (y * 2 + 1, (y - 1) % YN * 2 + 1)]
    return lax.ppermute(value, ("y_hi", "y_lo", "core"), route)


def prepare_kernel(forward_ref, reverse_ref, low_ref, high_ref, out_ref):
    rows = forward_ref.shape[0]
    out_ref[0, :rows, :] = forward_ref[...]
    row = lax.broadcasted_iota(jnp.int32, (rows, rows), 0)
    column = lax.broadcasted_iota(jnp.int32, (rows, rows), 1)
    flip = jnp.where(row + column == rows - 1, 1.0, 0.0).astype(jnp.bfloat16)
    out_ref[1, :rows, :] = jnp.dot(
        flip, reverse_ref[...], preferred_element_type=jnp.float32
    ).astype(jnp.bfloat16)
    width = forward_ref.shape[1]
    edge = lax.broadcasted_iota(jnp.int32, (EDGE, width), 0)
    low = low_ref[...].astype(jnp.float32)
    high = high_ref[...].astype(jnp.float32)
    for strand, after, before in ((0, high[0:1], low[0:1]), (1, low[1:2], high[1:2])):
        tile = jnp.where(edge == 0, after, jnp.where(edge == EDGE - 1, before, 0.0))
        out_ref[strand, rows:, :] = tile.astype(jnp.bfloat16)


def prepare(forward_embed, reverse_embed, low, high):
    rows, width = forward_embed.shape
    return pl.pallas_call(
        prepare_kernel,
        out_shape=jax.ShapeDtypeStruct((2, rows + EDGE, width), jnp.bfloat16),
        compiler_params=pltpu.CompilerParams(vmem_limit_bytes=VMEM_LIMIT),
        cost_estimate=pl.CostEstimate(
            flops=2 * rows * rows * width, bytes_accessed=8 * rows * width, transcendentals=0
        ),
        name="prepare",
    )(forward_embed, reverse_embed, low, high)


def chunk_kernel(strands, start, size, blocks, first, last, *refs):
    place_ref, refs = refs[0], refs[1:]
    sources, refs = refs[: len(blocks)], refs[len(blocks) :]
    x_hbm, bias_ref, head_hbm, head_bias_ref = refs[:4]
    refs = refs[4:]
    if not first:
        prev_hbm, refs = refs[0], refs[1:]
    out_ref, refs = refs[0], refs[1:]
    w_ref, x_ref, head_ref, before_ref, here_ref, after_ref, h_ref = refs[:7]
    refs = refs[7:]
    if not first:
        prev_ref, refs = refs[0], refs[1:]
    w_sem, x_sem, head_sem, prev_sem = refs
    channels = w_ref.shape[1]
    part = channels // 16
    rows = x_ref.shape[1] - EDGE

    x_copies = []
    for slot, strand in enumerate(strands):
        copy = pltpu.make_async_copy(x_hbm.at[strand], x_ref.at[slot], x_sem.at[slot])
        copy.start()
        x_copies.append(copy)
    w_copies = []
    for tap in range(3):
        group = []
        number = 0
        for source, (count, whole) in zip(sources, blocks):
            for index in range(count):
                place = pl.multiple_of(place_ref[number] * part, part)
                piece = source.at[index, tap] if count > 1 else source.at[tap]
                if whole:
                    piece = piece.at[:, pl.ds(start, size)]
                copy = pltpu.make_async_copy(
                    piece, w_ref.at[tap, pl.ds(place, part), :], w_sem.at[tap, number]
                )
                copy.start()
                group.append(copy)
                number += 1
        w_copies.append(group)
    head_copy = pltpu.make_async_copy(head_hbm.at[pl.ds(start, size), :], head_ref, head_sem)
    head_copy.start()
    prev_copies = []
    if not first:
        for slot, strand in enumerate(strands):
            copy = pltpu.make_async_copy(prev_hbm.at[strand], prev_ref.at[slot], prev_sem.at[slot])
            copy.start()
            prev_copies.append(copy)

    bias = bias_ref[...]
    for slot, strand in enumerate(strands):
        x_copies[slot].wait()
        order = (0, 1, 2) if strand == 0 else (2, 1, 0)
        for target, tap in zip((before_ref, here_ref, after_ref), order):
            if slot == 0:
                for copy in w_copies[tap]:
                    copy.wait()
            value = jnp.dot(x_ref[slot], w_ref[tap], preferred_element_type=jnp.float32)
            target[pl.ds(8, rows + EDGE), :] = value
        before_ref[pl.ds(7, 1), :] = before_ref[pl.ds(8 + rows + EDGE - 1, 1), :]
        acc = (
            before_ref[pl.ds(7, rows), :]
            + here_ref[pl.ds(8, rows), :]
            + after_ref[pl.ds(9, rows), :]
            + bias
        )
        hidden = 0.5 * acc * (1.0 + lax.erf(acc * INV_SQRT2))
        h_ref[slot] = hidden.astype(jnp.bfloat16)
        if slot == 0:
            head_copy.wait()
        logits = jnp.dot(h_ref[slot], head_ref[...], preferred_element_type=jnp.float32)
        if not first:
            prev_copies[slot].wait()
            logits = logits + prev_ref[slot]
        if last:
            logits = logits + head_bias_ref[...]
            tracks = jnp.maximum(logits, 0.0) + jnp.log1p(jnp.exp(-jnp.abs(logits)))
            out_ref[slot] = tracks.astype(jnp.bfloat16)
        else:
            out_ref[slot] = logits


def run_chunk(strands, start, size, blocks, place, sources, x, bias, head, head_bias, prev, last):
    rows, channels = x.shape[1] - EDGE, x.shape[2]
    tracks = head.shape[1]
    first = prev is None
    count = len(strands)
    held = pl.BlockSpec(memory_space=pl.ANY)
    inside = pl.BlockSpec(memory_space=pltpu.VMEM)
    scratch = [
        pltpu.VMEM((3, channels, size), jnp.bfloat16),
        pltpu.VMEM((count, rows + EDGE, channels), jnp.bfloat16),
        pltpu.VMEM((size, tracks), jnp.bfloat16),
        pltpu.VMEM((rows + EDGE + 16, size), jnp.float32),
        pltpu.VMEM((rows + EDGE + 16, size), jnp.float32),
        pltpu.VMEM((rows + EDGE + 16, size), jnp.float32),
        pltpu.VMEM((count, rows, size), jnp.bfloat16),
    ]
    if not first:
        scratch.append(pltpu.VMEM((count, rows, tracks), jnp.float32))
    scratch += [
        pltpu.SemaphoreType.DMA((3, 16)),
        pltpu.SemaphoreType.DMA((count,)),
        pltpu.SemaphoreType.DMA,
        pltpu.SemaphoreType.DMA((count,)),
    ]
    operands = [place, *sources, x, bias[:, start : start + size], head, head_bias[None]]
    specs = (
        [pl.BlockSpec(memory_space=pltpu.SMEM)]
        + [held] * len(sources)
        + [held, inside, held, inside]
    )
    if not first:
        operands.append(prev)
        specs.append(held)
    return pl.pallas_call(
        functools.partial(chunk_kernel, strands, start, size, blocks, first, last),
        out_shape=jax.ShapeDtypeStruct(
            (count, rows, tracks), jnp.bfloat16 if last else jnp.float32
        ),
        in_specs=specs,
        out_specs=inside,
        scratch_shapes=scratch,
        compiler_params=pltpu.CompilerParams(vmem_limit_bytes=VMEM_LIMIT),
        cost_estimate=pl.CostEstimate(
            flops=2 * count * rows * size * (3 * channels + tracks),
            bytes_accessed=6 * channels * size + 4 * count * rows * tracks,
            transcendentals=count * rows * size,
        ),
        name="chunk_last" if last else "chunk",
    )(*operands)


def per_device(forward_embed, reverse_embed, conv_weight, conv_bias, head_weight, head_bias):
    own = conv_weight[0]
    channels = own.shape[2]
    x, y, core = lax.axis_index("x"), lax.axis_index("y_lo"), lax.axis_index("core")

    sibling = core_swap(own)
    starts = [sum(CHUNKS[:i]) for i in range(len(CHUNKS))]
    pairs = [
        jnp.stack([own[:, :, s : s + n], sibling[:, :, s : s + n]])
        for s, n in zip(starts, CHUNKS)
    ]
    across = y_shift(own)

    ends = lax.axis_size("x") * lax.axis_size("y_lo") * lax.axis_size("core")
    up = [(i, i + 1) for i in range(ends - 1)]
    down = [(b, a) for a, b in up]
    low = lax.ppermute(jnp.stack([forward_embed[-1], reverse_embed[-1]]), SEQ, up)
    high = lax.ppermute(jnp.stack([forward_embed[0], reverse_embed[0]]), SEQ, down)
    strands = prepare(forward_embed, reverse_embed, low, high)

    across_other = core_swap(across)

    def seq(x_of, y_of, core_of):
        return (x_of % XN) * 4 + y_of * 2 + core_of

    step = 1 - 2 * core
    back, fore, far = x - step + XN, x + step + XN, x + 2
    other, over = 1 - core, 1 - y
    place = jnp.stack(
        [
            seq(x, y, core), seq(x, y, other),
            seq(x, over, core), seq(x, over, other),
            seq(back, y, core), seq(back, y, other),
            seq(fore, y, other), seq(fore, y, core),
            seq(far, y, core), seq(far, y, other),
            seq(back, over, core), seq(back, over, other),
            seq(fore, over, other), seq(fore, over, core),
            seq(far, over, core), seq(far, over, other),
        ]
    ).astype(jnp.int32)
    blocks = (
        (2, False), (1, True), (1, True), (2, False), (2, False), (1, False), (1, False),
        (2, False), (2, False), (1, False), (1, False),
    )

    logits = None
    for number, (start, size) in enumerate(zip(starts, CHUNKS)):
        pair = pairs[number]
        near = x_shift(pair)
        distant = x_shift(near[0])
        near_over = y_shift(near)
        distant_over = y_shift(distant)
        moved = [near, distant, near_over, distant_over]
        near_2, distant_2, near_over_2, distant_over_2 = [core_swap(value) for value in moved]
        sources = [
            pair, across, across_other, near, near_2, distant, distant_2,
            near_over, near_over_2, distant_over, distant_over_2,
        ]
        call = functools.partial(
            run_chunk, start=start, size=size, blocks=blocks, place=place, sources=sources,
            x=strands, bias=conv_bias, head=head_weight, head_bias=head_bias, prev=logits,
        )
        if number < len(CHUNKS) - 1:
            logits = call((0, 1), last=False)
        else:
            reverse_tracks = call((1,), last=True)[0]
            forward_tracks = call((0,), last=True)[0]
    mirror = [(i, ends - 1 - i) for i in range(ends)]
    mirrored = lax.ppermute(reverse_tracks, SEQ, mirror)
    mean = 0.5 * (forward_tracks.astype(jnp.float32) + mirrored.astype(jnp.float32))
    return mean.astype(jnp.bfloat16)


def solution(mesh):
    fine = Mesh(mesh.devices.reshape(2, 8, XN, 2, CN), AXES)
    return jax.shard_map(
        per_device,
        mesh=fine,
        in_specs=(
            P(AXES, None),
            P(AXES, None),
            P(None, None, SEQ, None),
            P(),
            P(),
            P(),
        ),
        out_specs=P(AXES, None),
        check_vma=False,
    )
```

```python
import functools

import jax
import jax.numpy as jnp
from jax import lax
from jax.experimental import pallas as pl
from jax.experimental.pallas import tpu as pltpu
from jax.sharding import Mesh
from jax.sharding import PartitionSpec as P

AXES = ("y_hi", "z", "x", "y_lo", "core")
SEQ = ("x", "y_lo", "core")
XN, YN, CN = 4, 4, 2
VMEM_LIMIT = 48 * 1024 * 1024
EDGE = 16
TILE = 256
PARTS = (8, 6, 2)
INV_SQRT2 = 0.7071067811865476


def core_swap(value):
    return lax.ppermute(value, "core", [(0, 1), (1, 0)])


def x_shift(value):
    route = []
    for x in range(XN):
        route += [(x * 2, (x + 1) % XN * 2), (x * 2 + 1, (x - 1) % XN * 2 + 1)]
    return lax.ppermute(value, ("x", "core"), route)


def y_shift(value):
    route = []
    for y in range(YN):
        route += [(y * 2, (y + 1) % YN * 2), (y * 2 + 1, (y - 1) % YN * 2 + 1)]
    return lax.ppermute(value, ("y_hi", "y_lo", "core"), route)


def fence(*values):
    return pl.pallas_call(
        lambda *refs: None,
        out_shape=[jax.ShapeDtypeStruct(v.shape, v.dtype) for v in values],
        in_specs=[pl.BlockSpec(memory_space=pl.ANY)] * len(values),
        out_specs=[pl.BlockSpec(memory_space=pl.ANY)] * len(values),
        input_output_aliases={i: i for i in range(len(values))},
        name="fence",
    )(*values)


def prepare_kernel(place_ref, forward_ref, reverse_ref, low_ref, high_ref, *refs):
    out_refs, full_ref = refs[:3], refs[3]
    rows, width = forward_ref.shape
    part = width // 16
    full_ref[0, :rows, :] = forward_ref[...]
    row = lax.broadcasted_iota(jnp.int32, (rows, rows), 0)
    column = lax.broadcasted_iota(jnp.int32, (rows, rows), 1)
    flip = jnp.where(row + column == rows - 1, 1.0, 0.0).astype(jnp.bfloat16)
    full_ref[1, :rows, :] = jnp.dot(
        flip, reverse_ref[...], preferred_element_type=jnp.float32
    ).astype(jnp.bfloat16)
    edge = lax.broadcasted_iota(jnp.int32, (EDGE, width), 0)
    low = low_ref[...].astype(jnp.float32)
    high = high_ref[...].astype(jnp.float32)
    for strand, after, before in ((0, high[0:1], low[0:1]), (1, low[1:2], high[1:2])):
        tile = jnp.where(edge == 0, after, jnp.where(edge == EDGE - 1, before, 0.0))
        full_ref[strand, rows:, :] = tile.astype(jnp.bfloat16)
    begin = 0
    for out_ref, count in zip(out_refs, PARTS):
        size = count * part
        lane = lax.broadcasted_iota(jnp.int32, (1, size), 1)
        wanted = jnp.zeros((1, size), jnp.int32)
        for block in range(count):
            inside = (lane >= block * part) & (lane < (block + 1) * part)
            wanted = jnp.where(inside, lane + (place_ref[begin + block] - block) * part, wanted)
        source = lax.broadcasted_iota(jnp.int32, (width, size), 0)
        move = jnp.where(source == wanted, 1.0, 0.0).astype(jnp.bfloat16)
        for strand in range(2):
            out_ref[strand] = jnp.dot(
                full_ref[strand], move, preferred_element_type=jnp.float32
            ).astype(jnp.bfloat16)
        begin += count


def prepare(place, forward_embed, reverse_embed, low, high):
    rows, width = forward_embed.shape
    part = width // 16
    inside = pl.BlockSpec(memory_space=pltpu.VMEM)
    return pl.pallas_call(
        prepare_kernel,
        out_shape=[
            jax.ShapeDtypeStruct((2, rows + EDGE, count * part), jnp.bfloat16) for count in PARTS
        ],
        in_specs=[pl.BlockSpec(memory_space=pltpu.SMEM)] + [inside] * 4,
        out_specs=[inside] * 3,
        scratch_shapes=[pltpu.VMEM((2, rows + EDGE, width), jnp.bfloat16)],
        compiler_params=pltpu.CompilerParams(vmem_limit_bytes=VMEM_LIMIT),
        cost_estimate=pl.CostEstimate(
            flops=4 * rows * width * width, bytes_accessed=8 * rows * width, transcendentals=0
        ),
        name="prepare",
    )(place, forward_embed, reverse_embed, low, high)


def convolve(x_ref, slot, flipped, blocks, taps):
    rows = x_ref.shape[1] - EDGE
    order = (2, 1, 0) if flipped else (0, 1, 2)
    for target, tap in zip(taps, order):
        weight = jnp.concatenate([block[tap] for block in blocks], axis=0)
        target[pl.ds(8, rows + EDGE), :] = jnp.dot(
            x_ref[slot], weight, preferred_element_type=jnp.float32
        )
    before, here, after = taps
    before[pl.ds(7, 1), :] = before[pl.ds(8 + rows + EDGE - 1, 1), :]
    return before[pl.ds(7, rows), :] + here[pl.ds(8, rows), :] + after[pl.ds(9, rows), :]


def partial_kernel(count, first, x_ref, *refs):
    blocks, refs = refs[:count], refs[count:]
    if not first:
        prev_ref, refs = refs[0], refs[1:]
    out_ref, taps = refs[0], refs[1:]
    for strand in range(2):
        acc = convolve(x_ref, strand, strand == 1, blocks, taps)
        if not first:
            acc = acc + prev_ref[strand]
        out_ref[strand] = acc


def partial_sum(x, sources, prev):
    rows, depth = x.shape[1] - EDGE, x.shape[2]
    part, channels = sources[0].shape[1:]
    acc_spec = pl.BlockSpec((2, rows, TILE), lambda n: (0, 0, n))
    operands, specs = [x, *sources], [pl.BlockSpec((2, rows + EDGE, depth), lambda n: (0, 0, 0))]
    specs += [pl.BlockSpec((3, part, TILE), lambda n: (0, 0, n))] * len(sources)
    if prev is not None:
        operands.append(prev)
        specs.append(acc_spec)
    return pl.pallas_call(
        functools.partial(partial_kernel, len(sources), prev is None),
        out_shape=jax.ShapeDtypeStruct((2, rows, channels), jnp.float32),
        grid=(channels // TILE,),
        in_specs=specs,
        out_specs=acc_spec,
        scratch_shapes=[pltpu.VMEM((rows + EDGE + 16, TILE), jnp.float32)] * 3,
        compiler_params=pltpu.CompilerParams(vmem_limit_bytes=VMEM_LIMIT),
        cost_estimate=pl.CostEstimate(
            flops=12 * rows * depth * channels,
            bytes_accessed=6 * depth * channels + 8 * rows * channels,
            transcendentals=0,
        ),
        name="partial_sum",
    )(*operands)


def finish_kernel(count, flipped, x_ref, *refs):
    blocks, refs = refs[:count], refs[count:]
    prev_ref, bias_ref, head_ref, head_bias_ref, out_ref, logits_ref = refs[:6]
    taps = refs[6:]
    step = pl.program_id(0)
    acc = convolve(x_ref, 0, flipped, blocks, taps) + prev_ref[0] + bias_ref[...]
    hidden = (0.5 * acc * (1.0 + lax.erf(acc * INV_SQRT2))).astype(jnp.bfloat16)
    value = jnp.dot(hidden, head_ref[...], preferred_element_type=jnp.float32)

    @pl.when(step == 0)
    def _():
        logits_ref[...] = value

    @pl.when(step > 0)
    def _():
        logits_ref[...] += value

    @pl.when(step == pl.num_programs(0) - 1)
    def _():
        logits = logits_ref[...] + head_bias_ref[...]
        tracks = jnp.maximum(logits, 0.0) + jnp.log1p(jnp.exp(-jnp.abs(logits)))
        out_ref[...] = tracks.astype(jnp.bfloat16)


def finish(strand, x, sources, prev, bias, head, head_bias):
    rows, depth = x.shape[1] - EDGE, x.shape[2]
    part, channels = sources[0].shape[1:]
    tracks = head.shape[1]
    return pl.pallas_call(
        functools.partial(finish_kernel, len(sources), strand == 1),
        out_shape=jax.ShapeDtypeStruct((rows, tracks), jnp.bfloat16),
        grid=(channels // TILE,),
        in_specs=[pl.BlockSpec((1, rows + EDGE, depth), lambda n: (strand, 0, 0))]
        + [pl.BlockSpec((3, part, TILE), lambda n: (0, 0, n))] * len(sources)
        + [
            pl.BlockSpec((1, rows, TILE), lambda n: (strand, 0, n)),
            pl.BlockSpec((1, TILE), lambda n: (0, n)),
            pl.BlockSpec((TILE, tracks), lambda n: (n, 0)),
            pl.BlockSpec((1, tracks), lambda n: (0, 0)),
        ],
        out_specs=pl.BlockSpec((rows, tracks), lambda n: (0, 0)),
        scratch_shapes=[pltpu.VMEM((rows, tracks), jnp.float32)]
        + [pltpu.VMEM((rows + EDGE + 16, TILE), jnp.float32)] * 3,
        compiler_params=pltpu.CompilerParams(vmem_limit_bytes=VMEM_LIMIT),
        cost_estimate=pl.CostEstimate(
            flops=2 * rows * channels * (3 * depth + tracks),
            bytes_accessed=6 * depth * channels + 2 * channels * tracks,
            transcendentals=rows * channels,
        ),
        name="finish",
    )(x, *sources, prev, bias, head, head_bias[None])


def per_device(forward_embed, reverse_embed, conv_weight, conv_bias, head_weight, head_bias):
    own = conv_weight[0]
    x, y, core = lax.axis_index("x"), lax.axis_index("y_lo"), lax.axis_index("core")
    ends = XN * 2 * CN

    def seq(x_of, y_of, core_of):
        return (x_of % XN) * 4 + y_of * 2 + core_of

    step = 1 - 2 * core
    back, fore, far = x - step + XN, x + step + XN, x + 2
    other, over = 1 - core, 1 - y
    place = jnp.stack(
        [
            seq(x, y, core), seq(x, y, other), seq(x, over, core), seq(x, over, other),
            seq(back, y, core), seq(fore, y, other), seq(back, over, core), seq(fore, over, other),
            seq(far, y, core), seq(far, y, other), seq(back, y, other), seq(fore, y, core),
            seq(far, over, core), seq(far, over, other),
            seq(back, over, other), seq(fore, over, core),
        ]
    ).astype(jnp.int32)

    across = y_shift(own)
    near = x_shift(own)
    sibling = core_swap(own)
    up = [(i, i + 1) for i in range(ends - 1)]
    down = [(b, a) for a, b in up]
    low = lax.ppermute(jnp.stack([forward_embed[-1], reverse_embed[-1]]), SEQ, up)
    high = lax.ppermute(jnp.stack([forward_embed[0], reverse_embed[0]]), SEQ, down)
    x_1, x_2, x_3 = prepare(place, forward_embed, reverse_embed, low, high)
    near, across, sibling, x_1 = fence(near, across, sibling, x_1)

    distant = x_shift(near)
    near_over = y_shift(near)
    across_b = core_swap(across)
    near_b = core_swap(near)
    distant, near_over, sibling, across_b, near_b = fence(
        distant, near_over, sibling, across_b, near_b
    )

    second = x_shift(sibling)
    distant_over = y_shift(distant)
    near_over_b = core_swap(near_over)
    distant_b = core_swap(distant)
    acc = partial_sum(
        x_1, [own, sibling, across, across_b, near, near_b, near_over, near_over_b], None
    )
    second, distant_over, distant_b, acc = fence(second, distant_over, distant_b, acc)

    second_over = y_shift(second)
    second_b = core_swap(second)
    distant_over_b = core_swap(distant_over)
    acc = partial_sum(
        x_2, [distant, distant_b, second, second_b, distant_over, distant_over_b], acc
    )
    second_over, acc = fence(second_over, acc)
    second_over_b = core_swap(second_over)

    last = [second_over, second_over_b]
    reverse_tracks = finish(1, x_3, last, acc, conv_bias, head_weight, head_bias)
    forward_tracks = finish(0, x_3, last, acc, conv_bias, head_weight, head_bias)
    mirrored = lax.ppermute(reverse_tracks, SEQ, [(i, ends - 1 - i) for i in range(ends)])
    mean = 0.5 * (forward_tracks.astype(jnp.float32) + mirrored.astype(jnp.float32))
    return mean.astype(jnp.bfloat16)


def solution(mesh):
    fine = Mesh(mesh.devices.reshape(2, 8, XN, 2, CN), AXES)
    return jax.shard_map(
        per_device,
        mesh=fine,
        in_specs=(
            P(AXES, None),
            P(AXES, None),
            P(None, None, SEQ, None),
            P(),
            P(),
            P(),
        ),
        out_specs=P(AXES, None),
        check_vma=False,
    )
```

```python
import functools

import jax
import jax.numpy as jnp
from jax import lax
from jax.experimental import pallas as pl
from jax.experimental.pallas import tpu as pltpu
from jax.sharding import Mesh
from jax.sharding import PartitionSpec as P

AXES = ("y_hi", "z", "x", "y_lo", "core")
SEQ = ("x", "y_lo", "core")
XN, YN, CN = 4, 4, 2
VMEM_LIMIT = 24 * 1024 * 1024
EDGE = 16
TILE = 512
PARTS = (8, 6, 2)
ROWS = 128
TOKEN = jax.ShapeDtypeStruct((8, 128), jnp.float32)
INV_SQRT2 = 0.7071067811865476


def core_swap(value):
    return lax.ppermute(value, "core", [(0, 1), (1, 0)])


def x_shift(value):
    route = []
    for x in range(XN):
        route += [(x * 2, (x + 1) % XN * 2), (x * 2 + 1, (x - 1) % XN * 2 + 1)]
    return lax.ppermute(value, ("x", "core"), route)


def y_shift(value):
    route = []
    for y in range(YN):
        route += [(y * 2, (y + 1) % YN * 2), (y * 2 + 1, (y - 1) % YN * 2 + 1)]
    return lax.ppermute(value, ("y_hi", "y_lo", "core"), route)


def fence_kernel(count, *refs):
    for source, target in zip(refs[:count], refs[-count:]):
        target[...] = source[...]


def fence(token, *values):
    inside = pl.BlockSpec(memory_space=pltpu.VMEM)
    operands = values if token is None else (*values, token)
    return pl.pallas_call(
        functools.partial(fence_kernel, len(values)),
        out_shape=[jax.ShapeDtypeStruct(v.shape, v.dtype) for v in values],
        in_specs=[inside] * len(operands),
        out_specs=[inside] * len(values),
        input_output_aliases={i: i for i in range(len(values))},
        compiler_params=pltpu.CompilerParams(vmem_limit_bytes=8 * 1024 * 1024),
        name="fence",
    )(*operands)


def prepare_kernel(place_ref, forward_ref, reverse_ref, low_ref, high_ref, *refs):
    out_refs, (token_ref, full_ref, reverse_vmem, sem) = refs[:3], refs[3:]
    token_ref[...] = jnp.zeros_like(token_ref)
    rows, width = forward_ref.shape
    part = width // 16
    forward_copy = pltpu.make_async_copy(forward_ref, full_ref.at[0, pl.ds(0, rows), :], sem.at[0])
    forward_copy.start()
    reverse_copy = pltpu.make_async_copy(reverse_ref, reverse_vmem, sem.at[1])
    reverse_copy.start()
    row = lax.broadcasted_iota(jnp.int32, (rows, rows), 0)
    column = lax.broadcasted_iota(jnp.int32, (rows, rows), 1)
    flip = jnp.where(row + column == rows - 1, 1.0, 0.0).astype(jnp.bfloat16)
    reverse_copy.wait()
    full_ref[1, :rows, :] = jnp.dot(
        flip, reverse_vmem[...], preferred_element_type=jnp.float32
    ).astype(jnp.bfloat16)
    edge = lax.broadcasted_iota(jnp.int32, (EDGE, width), 0)
    low = low_ref[...].astype(jnp.float32)
    high = high_ref[...].astype(jnp.float32)
    for strand, after, before in ((0, high[0:1], low[0:1]), (1, low[1:2], high[1:2])):
        tile = jnp.where(edge == 0, after, jnp.where(edge == EDGE - 1, before, 0.0))
        full_ref[strand, rows:, :] = tile.astype(jnp.bfloat16)
    forward_copy.wait()
    begin = 0
    for out_ref, count in zip(out_refs, PARTS):
        size = count * part
        lane = lax.broadcasted_iota(jnp.int32, (1, size), 1)
        wanted = jnp.zeros((1, size), jnp.int32)
        for block in range(count):
            inside = (lane >= block * part) & (lane < (block + 1) * part)
            wanted = jnp.where(inside, lane + (place_ref[begin + block] - block) * part, wanted)
        source = lax.broadcasted_iota(jnp.int32, (width, size), 0)
        move = jnp.where(source == wanted, 1.0, 0.0).astype(jnp.bfloat16)
        for strand in range(2):
            out_ref[strand] = jnp.dot(
                full_ref[strand], move, preferred_element_type=jnp.float32
            ).astype(jnp.bfloat16)
        begin += count


def prepare(place, forward_embed, reverse_embed, low, high):
    rows, width = forward_embed.shape
    part = width // 16
    inside = pl.BlockSpec(memory_space=pltpu.VMEM)
    return pl.pallas_call(
        prepare_kernel,
        out_shape=[
            jax.ShapeDtypeStruct((2, rows + EDGE, count * part), jnp.bfloat16) for count in PARTS
        ]
        + [TOKEN],
        in_specs=[pl.BlockSpec(memory_space=pltpu.SMEM)]
        + [pl.BlockSpec(memory_space=pltpu.HBM)] * 2
        + [inside] * 2,
        out_specs=[inside] * 4,
        scratch_shapes=[
            pltpu.VMEM((2, rows + EDGE, width), jnp.bfloat16),
            pltpu.VMEM((rows, width), jnp.bfloat16),
            pltpu.SemaphoreType.DMA((2,)),
        ],
        compiler_params=pltpu.CompilerParams(vmem_limit_bytes=VMEM_LIMIT),
        cost_estimate=pl.CostEstimate(
            flops=4 * rows * width * width, bytes_accessed=8 * rows * width, transcendentals=0
        ),
        name="prepare",
    )(place, forward_embed, reverse_embed, low, high)


def convolve(x, flipped, blocks, columns):
    rows = x.shape[0] - EDGE
    total = None
    for tap in range(3):
        weight = jnp.concatenate([block[tap, :, columns] for block in blocks], axis=0)
        value = jnp.dot(x, weight, preferred_element_type=jnp.float32)
        shift = tap - 1 if flipped else 1 - tap
        if shift:
            value = pltpu.roll(value, shift % (rows + EDGE), 0)
        value = value[:rows]
        total = value if total is None else total + value
    return total


def partial_kernel(count, first, x_ref, *refs):
    blocks, refs = refs[:count], refs[count:]
    out_ref, token_ref = refs[-2:]
    token_ref[...] = jnp.zeros_like(token_ref)
    channels = out_ref.shape[2]
    for start in range(0, channels, TILE):
        columns = pl.ds(start, TILE)
        for strand in range(2):
            acc = convolve(x_ref[strand], strand == 1, blocks, columns)
            if not first:
                acc = acc + refs[0][strand, :, columns]
            out_ref[strand, :, columns] = acc


def partial_sum(x, sources, prev):
    rows, depth = x.shape[1] - EDGE, x.shape[2]
    channels = sources[0].shape[2]
    operands = [x, *sources] + ([] if prev is None else [prev])
    inside = pl.BlockSpec(memory_space=pltpu.VMEM)
    return pl.pallas_call(
        functools.partial(partial_kernel, len(sources), prev is None),
        out_shape=[jax.ShapeDtypeStruct((2, rows, channels), jnp.float32), TOKEN],
        in_specs=[inside] * len(operands),
        out_specs=[inside] * 2,
        input_output_aliases={} if prev is None else {len(operands) - 1: 0},
        compiler_params=pltpu.CompilerParams(vmem_limit_bytes=VMEM_LIMIT),
        cost_estimate=pl.CostEstimate(
            flops=12 * rows * depth * channels,
            bytes_accessed=6 * depth * channels,
            transcendentals=0,
        ),
        name="partial_sum",
    )(*operands)


def finish_kernel(strand, groups, x_ref, *refs):
    count = sum(groups)
    sources, refs = refs[:count], refs[count:]
    prev_ref, bias_ref, head_ref, head_bias_ref, out_ref, hidden_ref = refs
    rows = out_ref.shape[0]
    start = 0
    for count in groups:
        blocks, sources = sources[:count], sources[count:]
        width = blocks[0].shape[2]
        here = pl.ds(start, width)
        acc = convolve(x_ref[strand], strand == 1, blocks, pl.ds(0, width))
        acc = acc + prev_ref[strand, :, here] + bias_ref[:, here]
        hidden = 0.5 * acc * (1.0 + lax.erf(acc * INV_SQRT2))
        hidden_ref[:, here] = hidden.astype(jnp.bfloat16)
        start += width
    for row in range(0, rows, ROWS):
        logits = jnp.dot(
            hidden_ref[pl.ds(row, ROWS), :], head_ref[...], preferred_element_type=jnp.float32
        )
        logits = logits + head_bias_ref[...]
        tracks = jnp.maximum(logits, 0.0) + jnp.log1p(jnp.exp(-jnp.abs(logits)))
        out_ref[pl.ds(row, ROWS), :] = tracks.astype(jnp.bfloat16)


def finish(strand, x, groups, prev, bias, head, head_bias):
    rows, depth = x.shape[1] - EDGE, x.shape[2]
    channels, tracks = head.shape
    sources = [value for group in groups for value in group]
    inside = pl.BlockSpec(memory_space=pltpu.VMEM)
    return pl.pallas_call(
        functools.partial(finish_kernel, strand, tuple(len(group) for group in groups)),
        out_shape=jax.ShapeDtypeStruct((rows, tracks), jnp.bfloat16),
        in_specs=[inside] * (len(sources) + 5),
        out_specs=inside,
        scratch_shapes=[pltpu.VMEM((rows, channels), jnp.bfloat16)],
        compiler_params=pltpu.CompilerParams(vmem_limit_bytes=VMEM_LIMIT),
        cost_estimate=pl.CostEstimate(
            flops=2 * rows * channels * (3 * depth + tracks),
            bytes_accessed=6 * depth * channels + 2 * channels * tracks,
            transcendentals=rows * channels,
        ),
        name="finish",
    )(x, *sources, prev, bias, head, head_bias[None])


def per_device(forward_embed, reverse_embed, conv_weight, conv_bias, head_weight, head_bias):
    own = conv_weight[0]
    x, y, core = lax.axis_index("x"), lax.axis_index("y_lo"), lax.axis_index("core")
    ends = XN * 2 * CN

    def seq(x_of, y_of, core_of):
        return (x_of % XN) * 4 + y_of * 2 + core_of

    step = 1 - 2 * core
    back, fore, far = x - step + XN, x + step + XN, x + 2
    other, over = 1 - core, 1 - y
    place = jnp.stack(
        [
            seq(x, y, core), seq(x, y, other), seq(x, over, core), seq(x, over, other),
            seq(back, y, core), seq(fore, y, other), seq(back, over, core), seq(fore, over, other),
            seq(far, y, core), seq(far, y, other), seq(back, y, other), seq(fore, y, core),
            seq(far, over, core), seq(far, over, other),
            seq(back, over, other), seq(fore, over, core),
        ]
    ).astype(jnp.int32)

    near = x_shift(own)
    across = y_shift(own)
    sibling = core_swap(own)
    up = [(i, i + 1) for i in range(ends - 1)]
    down = [(b, a) for a, b in up]
    low = lax.ppermute(jnp.stack([forward_embed[-1], reverse_embed[-1]]), SEQ, up)
    high = lax.ppermute(jnp.stack([forward_embed[0], reverse_embed[0]]), SEQ, down)
    near, across, low, high = fence(None, near, across, low, high)

    distant = x_shift(near)
    near_over = y_shift(near)
    across_b = core_swap(across)
    near_b = core_swap(near)
    x_1, x_2, x_3, token = prepare(place, forward_embed, reverse_embed, low, high)
    distant, near_over, sibling = fence(token, distant, near_over, sibling)

    second = x_shift(sibling)
    distant_over = y_shift(distant)
    near_over_b = core_swap(near_over)
    distant_b = core_swap(distant)
    half = own.shape[2] // 2
    across_half = across_b[:, :, :half]
    acc, token = partial_sum(
        x_1, [own, sibling, across, across_b, near, near_b, near_over, near_over_b], None
    )
    second, distant_over, across_half = fence(token, second, distant_over, across_half)

    over_low = x_shift(across_half)
    over_high = y_shift(second[:, :, half:])
    second_b = core_swap(second)
    distant_over_b = core_swap(distant_over)
    acc, token = partial_sum(
        x_2, [distant, distant_b, second, second_b, distant_over, distant_over_b], acc
    )
    over_low, over_high = fence(token, over_low, over_high)

    last = [[over_low, core_swap(over_low)], [over_high, core_swap(over_high)]]
    reverse_tracks = finish(1, x_3, last, acc, conv_bias, head_weight, head_bias)
    forward_tracks = finish(0, x_3, last, acc, conv_bias, head_weight, head_bias)
    mirrored = lax.ppermute(reverse_tracks, SEQ, [(i, ends - 1 - i) for i in range(ends)])
    mean = 0.5 * (forward_tracks.astype(jnp.float32) + mirrored.astype(jnp.float32))
    return mean.astype(jnp.bfloat16)


def solution(mesh):
    fine = Mesh(mesh.devices.reshape(2, 8, XN, 2, CN), AXES)
    return jax.shard_map(
        per_device,
        mesh=fine,
        in_specs=(
            P(AXES, None),
            P(AXES, None),
            P(None, None, SEQ, None),
            P(),
            P(),
            P(),
        ),
        out_specs=P(AXES, None),
        check_vma=False,
    )
```

```python
import functools

import jax
import jax.numpy as jnp
from jax import lax
from jax.experimental import pallas as pl
from jax.experimental.pallas import tpu as pltpu
from jax.sharding import Mesh
from jax.sharding import PartitionSpec as P

AXES = ("y_hi", "z", "x", "y_lo", "core")
SEQ = ("x", "y_lo", "core")
XN, YN, CN = 4, 4, 2
VMEM_LIMIT = 24 * 1024 * 1024
EDGE = 16
TILE = 512
PARTS = (8, 4, 4)
ROWS = 128
TOKEN = jax.ShapeDtypeStruct((8, 128), jnp.float32)
INV_SQRT2 = 0.7071067811865476


def core_swap(value):
    return lax.ppermute(value, "core", [(0, 1), (1, 0)])


def x_shift(value):
    route = []
    for x in range(XN):
        route += [(x * 2, (x + 1) % XN * 2), (x * 2 + 1, (x - 1) % XN * 2 + 1)]
    return lax.ppermute(value, ("x", "core"), route)


def y_shift(value):
    route = []
    for y in range(YN):
        route += [(y * 2, (y + 1) % YN * 2), (y * 2 + 1, (y - 1) % YN * 2 + 1)]
    return lax.ppermute(value, ("y_hi", "y_lo", "core"), route)


def fence_kernel(count, *refs):
    for source, target in zip(refs[:count], refs[-count:]):
        target[...] = source[...]


def fence(token, *values):
    inside = pl.BlockSpec(memory_space=pltpu.VMEM)
    operands = values if token is None else (*values, token)
    return pl.pallas_call(
        functools.partial(fence_kernel, len(values)),
        out_shape=[jax.ShapeDtypeStruct(v.shape, v.dtype) for v in values],
        in_specs=[inside] * len(operands),
        out_specs=[inside] * len(values),
        input_output_aliases={i: i for i in range(len(values))},
        compiler_params=pltpu.CompilerParams(vmem_limit_bytes=8 * 1024 * 1024),
        name="fence",
    )(*operands)


def prepare_kernel(place_ref, forward_ref, reverse_ref, low_ref, high_ref, *refs):
    out_refs, (token_ref, full_ref, reverse_vmem, sem) = refs[:3], refs[3:]
    token_ref[...] = jnp.zeros_like(token_ref)
    rows, width = forward_ref.shape
    part = width // 16
    forward_copy = pltpu.make_async_copy(forward_ref, full_ref.at[0, pl.ds(0, rows), :], sem.at[0])
    forward_copy.start()
    reverse_copy = pltpu.make_async_copy(reverse_ref, reverse_vmem, sem.at[1])
    reverse_copy.start()
    row = lax.broadcasted_iota(jnp.int32, (rows, rows), 0)
    column = lax.broadcasted_iota(jnp.int32, (rows, rows), 1)
    flip = jnp.where(row + column == rows - 1, 1.0, 0.0).astype(jnp.bfloat16)
    reverse_copy.wait()
    full_ref[1, :rows, :] = jnp.dot(
        flip, reverse_vmem[...], preferred_element_type=jnp.float32
    ).astype(jnp.bfloat16)
    edge = lax.broadcasted_iota(jnp.int32, (EDGE, width), 0)
    low = low_ref[...].astype(jnp.float32)
    high = high_ref[...].astype(jnp.float32)
    for strand, after, before in ((0, high[0:1], low[0:1]), (1, low[1:2], high[1:2])):
        tile = jnp.where(edge == 0, after, jnp.where(edge == EDGE - 1, before, 0.0))
        full_ref[strand, rows:, :] = tile.astype(jnp.bfloat16)
    forward_copy.wait()
    begin = 0
    for out_ref, count in zip(out_refs, PARTS):
        size = count * part
        lane = lax.broadcasted_iota(jnp.int32, (1, size), 1)
        wanted = jnp.zeros((1, size), jnp.int32)
        for block in range(count):
            inside = (lane >= block * part) & (lane < (block + 1) * part)
            wanted = jnp.where(inside, lane + (place_ref[begin + block] - block) * part, wanted)
        source = lax.broadcasted_iota(jnp.int32, (width, size), 0)
        move = jnp.where(source == wanted, 1.0, 0.0).astype(jnp.bfloat16)
        for strand in range(2):
            out_ref[strand] = jnp.dot(
                full_ref[strand], move, preferred_element_type=jnp.float32
            ).astype(jnp.bfloat16)
        begin += count


def prepare(place, forward_embed, reverse_embed, low, high):
    rows, width = forward_embed.shape
    part = width // 16
    inside = pl.BlockSpec(memory_space=pltpu.VMEM)
    return pl.pallas_call(
        prepare_kernel,
        out_shape=[
            jax.ShapeDtypeStruct((2, rows + EDGE, count * part), jnp.bfloat16) for count in PARTS
        ]
        + [TOKEN],
        in_specs=[pl.BlockSpec(memory_space=pltpu.SMEM)]
        + [pl.BlockSpec(memory_space=pltpu.HBM)] * 2
        + [inside] * 2,
        out_specs=[inside] * 4,
        scratch_shapes=[
            pltpu.VMEM((2, rows + EDGE, width), jnp.bfloat16),
            pltpu.VMEM((rows, width), jnp.bfloat16),
            pltpu.SemaphoreType.DMA((2,)),
        ],
        compiler_params=pltpu.CompilerParams(vmem_limit_bytes=VMEM_LIMIT),
        cost_estimate=pl.CostEstimate(
            flops=4 * rows * width * width, bytes_accessed=8 * rows * width, transcendentals=0
        ),
        name="prepare",
    )(place, forward_embed, reverse_embed, low, high)


def convolve(x, flipped, blocks, columns):
    rows = x.shape[0] - EDGE
    total = None
    for tap in range(3):
        weight = jnp.concatenate([block[tap, :, columns] for block in blocks], axis=0)
        value = jnp.dot(x, weight, preferred_element_type=jnp.float32)
        shift = tap - 1 if flipped else 1 - tap
        if shift:
            value = pltpu.roll(value, shift % (rows + EDGE), 0)
        value = value[:rows]
        total = value if total is None else total + value
    return total


def partial_kernel(count, first, x_ref, *refs):
    blocks, refs = refs[:count], refs[count:]
    out_ref, token_ref = refs[-2:]
    token_ref[...] = jnp.zeros_like(token_ref)
    channels = out_ref.shape[2]
    for start in range(0, channels, TILE):
        columns = pl.ds(start, TILE)
        for strand in range(2):
            acc = convolve(x_ref[strand], strand == 1, blocks, columns)
            if not first:
                acc = acc + refs[0][strand, :, columns]
            out_ref[strand, :, columns] = acc


def partial_sum(x, sources, prev):
    rows, depth = x.shape[1] - EDGE, x.shape[2]
    channels = sources[0].shape[2]
    operands = [x, *sources] + ([] if prev is None else [prev])
    inside = pl.BlockSpec(memory_space=pltpu.VMEM)
    return pl.pallas_call(
        functools.partial(partial_kernel, len(sources), prev is None),
        out_shape=[jax.ShapeDtypeStruct((2, rows, channels), jnp.float32), TOKEN],
        in_specs=[inside] * len(operands),
        out_specs=[inside] * 2,
        input_output_aliases={} if prev is None else {len(operands) - 1: 0},
        compiler_params=pltpu.CompilerParams(vmem_limit_bytes=VMEM_LIMIT),
        cost_estimate=pl.CostEstimate(
            flops=12 * rows * depth * channels,
            bytes_accessed=6 * depth * channels,
            transcendentals=0,
        ),
        name="partial_sum",
    )(*operands)


def finish_kernel(strand, count, x_ref, *refs):
    sources, refs = refs[:count], refs[count:]
    prev_ref, bias_ref, head_ref, head_bias_ref, out_ref, hidden_ref = refs
    rows = out_ref.shape[0]
    for start in range(0, hidden_ref.shape[1], TILE):
        here = pl.ds(start, TILE)
        acc = convolve(x_ref[strand], strand == 1, sources, here)
        acc = acc + prev_ref[strand, :, here] + bias_ref[:, here]
        hidden = 0.5 * acc * (1.0 + lax.erf(acc * INV_SQRT2))
        hidden_ref[:, here] = hidden.astype(jnp.bfloat16)
    for row in range(0, rows, ROWS):
        logits = jnp.dot(
            hidden_ref[pl.ds(row, ROWS), :], head_ref[...], preferred_element_type=jnp.float32
        )
        logits = logits + head_bias_ref[...]
        tracks = jnp.maximum(logits, 0.0) + jnp.log1p(jnp.exp(-jnp.abs(logits)))
        out_ref[pl.ds(row, ROWS), :] = tracks.astype(jnp.bfloat16)


def finish(strand, x, sources, prev, bias, head, head_bias):
    rows, depth = x.shape[1] - EDGE, x.shape[2]
    channels, tracks = head.shape
    inside = pl.BlockSpec(memory_space=pltpu.VMEM)
    return pl.pallas_call(
        functools.partial(finish_kernel, strand, len(sources)),
        out_shape=jax.ShapeDtypeStruct((rows, tracks), jnp.bfloat16),
        in_specs=[inside] * (len(sources) + 5),
        out_specs=inside,
        scratch_shapes=[pltpu.VMEM((rows, channels), jnp.bfloat16)],
        compiler_params=pltpu.CompilerParams(vmem_limit_bytes=VMEM_LIMIT),
        cost_estimate=pl.CostEstimate(
            flops=2 * rows * channels * (3 * depth + tracks),
            bytes_accessed=6 * depth * channels + 2 * channels * tracks,
            transcendentals=rows * channels,
        ),
        name="finish",
    )(x, *sources, prev, bias, head, head_bias[None])


def per_device(forward_embed, reverse_embed, conv_weight, conv_bias, head_weight, head_bias):
    own = conv_weight[0]
    x, y, core = lax.axis_index("x"), lax.axis_index("y_lo"), lax.axis_index("core")
    ends = XN * 2 * CN

    def seq(x_of, y_of, core_of):
        return (x_of % XN) * 4 + y_of * 2 + core_of

    step = 1 - 2 * core
    back, fore, far = x - step + XN, x + step + XN, x + 2
    other, over = 1 - core, 1 - y
    place = jnp.stack(
        [
            seq(x, y, core), seq(x, y, other), seq(x, over, core), seq(x, over, other),
            seq(back, y, core), seq(fore, y, other), seq(back, over, core), seq(fore, over, other),
            seq(far, y, core), seq(far, y, other), seq(back, y, other), seq(fore, y, core),
            seq(back, over, other), seq(fore, over, core),
            seq(far, over, core), seq(far, over, other),
        ]
    ).astype(jnp.int32)

    near = x_shift(own)
    across = y_shift(own)
    sibling = core_swap(own)
    up = [(i, i + 1) for i in range(ends - 1)]
    down = [(b, a) for a, b in up]
    low = lax.ppermute(jnp.stack([forward_embed[-1], reverse_embed[-1]]), SEQ, up)
    high = lax.ppermute(jnp.stack([forward_embed[0], reverse_embed[0]]), SEQ, down)
    near, across, sibling, low, high = fence(None, near, across, sibling, low, high)

    distant = x_shift(near)
    near_over = y_shift(near)
    second = x_shift(sibling)
    across_b = core_swap(across)
    near_b = core_swap(near)
    x_1, x_2, x_3, token = prepare(place, forward_embed, reverse_embed, low, high)
    distant, second, across_b = fence(token, distant, second, across_b)

    second_over = x_shift(across_b)
    distant_over = y_shift(distant)
    distant_b = core_swap(distant)
    second_b = core_swap(second)
    near_over_b = core_swap(near_over)
    acc, _ = partial_sum(
        x_1, [own, sibling, across, across_b, near, near_b, near_over, near_over_b], None
    )
    acc, token = partial_sum(x_2, [distant, distant_b, second, second_b], acc)
    second_over, distant_over = fence(token, second_over, distant_over)

    last = [second_over, core_swap(second_over), distant_over, core_swap(distant_over)]
    reverse_tracks = finish(1, x_3, last, acc, conv_bias, head_weight, head_bias)
    forward_tracks = finish(0, x_3, last, acc, conv_bias, head_weight, head_bias)
    mirrored = lax.ppermute(reverse_tracks, SEQ, [(i, ends - 1 - i) for i in range(ends)])
    mean = 0.5 * (forward_tracks.astype(jnp.float32) + mirrored.astype(jnp.float32))
    return mean.astype(jnp.bfloat16)


def solution(mesh):
    fine = Mesh(mesh.devices.reshape(2, 8, XN, 2, CN), AXES)
    return jax.shard_map(
        per_device,
        mesh=fine,
        in_specs=(
            P(AXES, None),
            P(AXES, None),
            P(None, None, SEQ, None),
            P(),
            P(),
            P(),
        ),
        out_specs=P(AXES, None),
        check_vma=False,
    )
```

```python
import functools

import jax
import jax.numpy as jnp
from jax import lax
from jax.experimental import pallas as pl
from jax.experimental.pallas import tpu as pltpu
from jax.sharding import Mesh
from jax.sharding import PartitionSpec as P

AXES = ("y_hi", "z", "x", "y_lo", "core")
SEQ = ("x", "y_lo", "core")
XN, YN, CN = 4, 4, 2
VMEM_LIMIT = 24 * 1024 * 1024
EDGE = 16
TILE = 512
PARTS = (8, 4, 4)
ROWS = 128
TOKEN = jax.ShapeDtypeStruct((8, 128), jnp.float32)
INV_SQRT2 = 0.7071067811865476


def core_swap(value):
    return lax.ppermute(value, "core", [(0, 1), (1, 0)])


def x_shift(value):
    route = []
    for x in range(XN):
        route += [(x * 2, (x + 1) % XN * 2), (x * 2 + 1, (x - 1) % XN * 2 + 1)]
    return lax.ppermute(value, ("x", "core"), route)


def y_shift(value):
    route = []
    for y in range(YN):
        route += [(y * 2, (y + 1) % YN * 2), (y * 2 + 1, (y - 1) % YN * 2 + 1)]
    return lax.ppermute(value, ("y_hi", "y_lo", "core"), route)


def fence_kernel(count, *refs):
    for source, target in zip(refs[:count], refs[-count:]):
        target[...] = source[...]


def fence(token, *values):
    inside = pl.BlockSpec(memory_space=pltpu.VMEM)
    operands = values if token is None else (*values, token)
    return pl.pallas_call(
        functools.partial(fence_kernel, len(values)),
        out_shape=[jax.ShapeDtypeStruct(v.shape, v.dtype) for v in values],
        in_specs=[inside] * len(operands),
        out_specs=[inside] * len(values),
        input_output_aliases={i: i for i in range(len(values))},
        compiler_params=pltpu.CompilerParams(vmem_limit_bytes=8 * 1024 * 1024),
        name="fence",
    )(*operands)


def prepare_kernel(place_ref, forward_ref, reverse_ref, low_ref, high_ref, *refs):
    out_refs, (token_ref, full_ref, reverse_vmem, sem) = refs[:3], refs[3:]
    token_ref[...] = jnp.zeros_like(token_ref)
    rows, width = forward_ref.shape
    part = width // 16
    forward_copy = pltpu.make_async_copy(forward_ref, full_ref.at[0, pl.ds(0, rows), :], sem.at[0])
    forward_copy.start()
    reverse_copy = pltpu.make_async_copy(reverse_ref, reverse_vmem, sem.at[1])
    reverse_copy.start()
    row = lax.broadcasted_iota(jnp.int32, (rows, rows), 0)
    column = lax.broadcasted_iota(jnp.int32, (rows, rows), 1)
    flip = jnp.where(row + column == rows - 1, 1.0, 0.0).astype(jnp.bfloat16)
    reverse_copy.wait()
    full_ref[1, :rows, :] = jnp.dot(
        flip, reverse_vmem[...], preferred_element_type=jnp.float32
    ).astype(jnp.bfloat16)
    edge = lax.broadcasted_iota(jnp.int32, (EDGE, width), 0)
    low = low_ref[...].astype(jnp.float32)
    high = high_ref[...].astype(jnp.float32)
    for strand, after, before in ((0, high[0:1], low[0:1]), (1, low[1:2], high[1:2])):
        tile = jnp.where(edge == 0, after, jnp.where(edge == EDGE - 1, before, 0.0))
        full_ref[strand, rows:, :] = tile.astype(jnp.bfloat16)
    forward_copy.wait()
    begin = 0
    for out_ref, count in zip(out_refs, PARTS):
        size = count * part
        lane = lax.broadcasted_iota(jnp.int32, (1, size), 1)
        wanted = jnp.zeros((1, size), jnp.int32)
        for block in range(count):
            inside = (lane >= block * part) & (lane < (block + 1) * part)
            wanted = jnp.where(inside, lane + (place_ref[begin + block] - block) * part, wanted)
        source = lax.broadcasted_iota(jnp.int32, (width, size), 0)
        move = jnp.where(source == wanted, 1.0, 0.0).astype(jnp.bfloat16)
        for strand in range(2):
            out_ref[strand] = jnp.dot(
                full_ref[strand], move, preferred_element_type=jnp.float32
            ).astype(jnp.bfloat16)
        begin += count


def prepare(place, forward_embed, reverse_embed, low, high):
    rows, width = forward_embed.shape
    part = width // 16
    inside = pl.BlockSpec(memory_space=pltpu.VMEM)
    return pl.pallas_call(
        prepare_kernel,
        out_shape=[
            jax.ShapeDtypeStruct((2, rows + EDGE, count * part), jnp.bfloat16) for count in PARTS
        ]
        + [TOKEN],
        in_specs=[pl.BlockSpec(memory_space=pltpu.SMEM)]
        + [pl.BlockSpec(memory_space=pltpu.HBM)] * 2
        + [inside] * 2,
        out_specs=[inside] * 4,
        scratch_shapes=[
            pltpu.VMEM((2, rows + EDGE, width), jnp.bfloat16),
            pltpu.VMEM((rows, width), jnp.bfloat16),
            pltpu.SemaphoreType.DMA((2,)),
        ],
        compiler_params=pltpu.CompilerParams(vmem_limit_bytes=VMEM_LIMIT),
        cost_estimate=pl.CostEstimate(
            flops=4 * rows * width * width, bytes_accessed=8 * rows * width, transcendentals=0
        ),
        name="prepare",
    )(place, forward_embed, reverse_embed, low, high)


def convolve(x, flipped, blocks, columns):
    rows = x.shape[0] - EDGE
    total = None
    for tap in range(3):
        weight = jnp.concatenate([block[tap, :, columns] for block in blocks], axis=0)
        value = jnp.dot(x, weight, preferred_element_type=jnp.float32)
        shift = tap - 1 if flipped else 1 - tap
        if shift:
            value = pltpu.roll(value, shift % (rows + EDGE), 0)
        value = value[:rows]
        total = value if total is None else total + value
    return total


def partial_kernel(count, first, x_ref, *refs):
    blocks, refs = refs[:count], refs[count:]
    out_ref, token_ref = refs[-2:]
    token_ref[...] = jnp.zeros_like(token_ref)
    channels = out_ref.shape[2]
    for start in range(0, channels, TILE):
        columns = pl.ds(start, TILE)
        for strand in range(2):
            acc = convolve(x_ref[strand], strand == 1, blocks, columns)
            if not first:
                acc = acc + refs[0][strand, :, columns]
            out_ref[strand, :, columns] = acc


def partial_sum(x, sources, prev):
    rows, depth = x.shape[1] - EDGE, x.shape[2]
    channels = sources[0].shape[2]
    operands = [x, *sources] + ([] if prev is None else [prev])
    inside = pl.BlockSpec(memory_space=pltpu.VMEM)
    return pl.pallas_call(
        functools.partial(partial_kernel, len(sources), prev is None),
        out_shape=[jax.ShapeDtypeStruct((2, rows, channels), jnp.float32), TOKEN],
        in_specs=[inside] * len(operands),
        out_specs=[inside] * 2,
        input_output_aliases={} if prev is None else {len(operands) - 1: 0},
        compiler_params=pltpu.CompilerParams(vmem_limit_bytes=VMEM_LIMIT),
        cost_estimate=pl.CostEstimate(
            flops=12 * rows * depth * channels,
            bytes_accessed=6 * depth * channels,
            transcendentals=0,
        ),
        name="partial_sum",
    )(*operands)


def finish_kernel(strand, count, x_ref, *refs):
    sources, refs = refs[:count], refs[count:]
    prev_ref, bias_ref, head_ref, head_bias_ref, out_ref, hidden_ref = refs
    rows = out_ref.shape[0]
    for start in range(0, hidden_ref.shape[1], TILE):
        here = pl.ds(start, TILE)
        acc = convolve(x_ref[strand], strand == 1, sources, here)
        acc = acc + prev_ref[strand, :, here] + bias_ref[:, here]
        hidden = 0.5 * acc * (1.0 + lax.erf(acc * INV_SQRT2))
        hidden_ref[:, here] = hidden.astype(jnp.bfloat16)
    for row in range(0, rows, ROWS):
        logits = jnp.dot(
            hidden_ref[pl.ds(row, ROWS), :], head_ref[...], preferred_element_type=jnp.float32
        )
        logits = logits + head_bias_ref[...]
        tracks = jnp.maximum(logits, 0.0) + jnp.log1p(jnp.exp(-jnp.abs(logits)))
        out_ref[pl.ds(row, ROWS), :] = tracks.astype(jnp.bfloat16)


def finish(strand, x, sources, prev, bias, head, head_bias):
    rows, depth = x.shape[1] - EDGE, x.shape[2]
    channels, tracks = head.shape
    inside = pl.BlockSpec(memory_space=pltpu.VMEM)
    return pl.pallas_call(
        functools.partial(finish_kernel, strand, len(sources)),
        out_shape=jax.ShapeDtypeStruct((rows, tracks), jnp.bfloat16),
        in_specs=[inside] * (len(sources) + 5),
        out_specs=inside,
        scratch_shapes=[pltpu.VMEM((rows, channels), jnp.bfloat16)],
        compiler_params=pltpu.CompilerParams(vmem_limit_bytes=VMEM_LIMIT),
        cost_estimate=pl.CostEstimate(
            flops=2 * rows * channels * (3 * depth + tracks),
            bytes_accessed=6 * depth * channels + 2 * channels * tracks,
            transcendentals=rows * channels,
        ),
        name="finish",
    )(x, *sources, prev, bias, head, head_bias[None])


def per_device(forward_embed, reverse_embed, conv_weight, conv_bias, head_weight, head_bias):
    own = conv_weight[0]
    x, y, core = lax.axis_index("x"), lax.axis_index("y_lo"), lax.axis_index("core")
    ends = XN * 2 * CN

    def seq(x_of, y_of, core_of):
        return (x_of % XN) * 4 + y_of * 2 + core_of

    step = 1 - 2 * core
    back, fore, far = x - step + XN, x + step + XN, x + 2
    other, over = 1 - core, 1 - y
    place = jnp.stack(
        [
            seq(x, y, core), seq(x, y, other), seq(x, over, core), seq(x, over, other),
            seq(back, y, core), seq(fore, y, other), seq(back, y, other), seq(fore, y, core),
            seq(back, over, core), seq(fore, over, other), seq(far, y, core), seq(far, y, other),
            seq(back, over, other), seq(fore, over, core),
            seq(far, over, core), seq(far, over, other),
        ]
    ).astype(jnp.int32)

    near = x_shift(own)
    across = y_shift(own)
    sibling = core_swap(own)
    second = x_shift(sibling)
    up = [(i, i + 1) for i in range(ends - 1)]
    down = [(b, a) for a, b in up]
    low = lax.ppermute(jnp.stack([forward_embed[-1], reverse_embed[-1]]), SEQ, up)
    high = lax.ppermute(jnp.stack([forward_embed[0], reverse_embed[0]]), SEQ, down)
    x_1, x_2, x_3, token = prepare(place, forward_embed, reverse_embed, low, high)
    near, across = fence(token, near, across)

    distant = x_shift(near)
    near_over = y_shift(near)
    across_b = core_swap(across)
    near_b = core_swap(near)
    second_b = core_swap(second)
    acc, token = partial_sum(
        x_1, [own, sibling, across, across_b, near, near_b, second, second_b], None
    )
    distant, near_over, across_b = fence(token, distant, near_over, across_b)

    second_over = x_shift(across_b)
    distant_over = y_shift(distant)
    near_over_b = core_swap(near_over)
    distant_b = core_swap(distant)
    acc, token = partial_sum(x_2, [near_over, near_over_b, distant, distant_b], acc)
    second_over, distant_over = fence(token, second_over, distant_over)

    last = [second_over, core_swap(second_over), distant_over, core_swap(distant_over)]
    reverse_tracks = finish(1, x_3, last, acc, conv_bias, head_weight, head_bias)
    forward_tracks = finish(0, x_3, last, acc, conv_bias, head_weight, head_bias)
    mirrored = lax.ppermute(reverse_tracks, SEQ, [(i, ends - 1 - i) for i in range(ends)])
    mean = 0.5 * (forward_tracks.astype(jnp.float32) + mirrored.astype(jnp.float32))
    return mean.astype(jnp.bfloat16)


def solution(mesh):
    fine = Mesh(mesh.devices.reshape(2, 8, XN, 2, CN), AXES)
    return jax.shard_map(
        per_device,
        mesh=fine,
        in_specs=(
            P(AXES, None),
            P(AXES, None),
            P(None, None, SEQ, None),
            P(),
            P(),
            P(),
        ),
        out_specs=P(AXES, None),
        check_vma=False,
    )
```

```python
import functools

import jax
import jax.numpy as jnp
from jax import lax
from jax.experimental import pallas as pl
from jax.experimental.pallas import tpu as pltpu
from jax.sharding import Mesh
from jax.sharding import PartitionSpec as P

AXES = ("y_hi", "z", "x", "y_lo", "core")
SEQ = ("x", "y_lo", "core")
XN, YN, CN = 4, 4, 2
VMEM_LIMIT = 24 * 1024 * 1024
EDGE = 16
TILE = 512
PARTS = (8, 4, 4)
ROWS = 128
AWAY = 128
TOKEN = jax.ShapeDtypeStruct((8, 128), jnp.float32)
INV_SQRT2 = 0.7071067811865476


def core_swap(value):
    return lax.ppermute(value, "core", [(0, 1), (1, 0)])


def x_shift(value):
    route = []
    for x in range(XN):
        route += [(x * 2, (x + 1) % XN * 2), (x * 2 + 1, (x - 1) % XN * 2 + 1)]
    return lax.ppermute(value, ("x", "core"), route)


def y_shift(value):
    route = []
    for y in range(YN):
        route += [(y * 2, (y + 1) % YN * 2), (y * 2 + 1, (y - 1) % YN * 2 + 1)]
    return lax.ppermute(value, ("y_hi", "y_lo", "core"), route)


def fence_kernel(count, *refs):
    for source, target in zip(refs[:count], refs[-count:]):
        target[...] = source[...]


def fence(token, *values):
    inside = pl.BlockSpec(memory_space=pltpu.VMEM)
    operands = values if token is None else (*values, token)
    return pl.pallas_call(
        functools.partial(fence_kernel, len(values)),
        out_shape=[jax.ShapeDtypeStruct(v.shape, v.dtype) for v in values],
        in_specs=[inside] * len(operands),
        out_specs=[inside] * len(values),
        input_output_aliases={i: i for i in range(len(values))},
        compiler_params=pltpu.CompilerParams(vmem_limit_bytes=8 * 1024 * 1024),
        name="fence",
    )(*operands)


def edge_tile(after, before):
    width = after.shape[1]
    edge = lax.broadcasted_iota(jnp.int32, (EDGE, width), 0)
    tile = jnp.where(edge == 0, after, jnp.where(edge == EDGE - 1, before, 0.0))
    return tile.astype(jnp.bfloat16)


def prepare_kernel(place_ref, forward_ref, reverse_ref, low_ref, high_ref, *refs):
    x_refs, y_refs, move_refs, away_ref, token_ref = refs[:3], refs[3:6], refs[6:9], *refs[9:11]
    full_ref, flip_ref, reverse_vmem, sem = refs[11:]
    token_ref[...] = jnp.zeros_like(token_ref)
    rows, width = forward_ref.shape
    kept = rows - AWAY
    part = width // 16
    forward_copy = pltpu.make_async_copy(forward_ref, full_ref.at[pl.ds(0, rows), :], sem.at[0])
    forward_copy.start()
    reverse_copy = pltpu.make_async_copy(reverse_ref, reverse_vmem, sem.at[1])
    reverse_copy.start()
    begin = 0
    for move_ref, count in zip(move_refs, PARTS):
        size = count * part
        lane = lax.broadcasted_iota(jnp.int32, (1, size), 1)
        wanted = jnp.zeros((1, size), jnp.int32)
        for block in range(count):
            inside = (lane >= block * part) & (lane < (block + 1) * part)
            wanted = jnp.where(inside, lane + (place_ref[begin + block] - block) * part, wanted)
        source = lax.broadcasted_iota(jnp.int32, (width, size), 0)
        move_ref[...] = jnp.where(source == wanted, 1.0, 0.0).astype(jnp.bfloat16)
        begin += count
    low = low_ref[...].astype(jnp.float32)
    high = high_ref[...].astype(jnp.float32)
    row = lax.broadcasted_iota(jnp.int32, (rows, rows), 0)
    column = lax.broadcasted_iota(jnp.int32, (rows, rows), 1)
    flip = jnp.where(row + column == rows - 1, 1.0, 0.0).astype(jnp.bfloat16)
    reverse_copy.wait()
    flipped = jnp.dot(flip, reverse_vmem[...], preferred_element_type=jnp.float32)
    flip_ref[:kept, :] = flipped[:kept].astype(jnp.bfloat16)
    flip_ref[kept:, :] = edge_tile(flipped[kept : kept + 1], high[1:2])
    away_ref[:AWAY, :] = flipped[kept:].astype(jnp.bfloat16)
    away_ref[AWAY:, :] = edge_tile(low[1:2], flipped[kept - 1 : kept])
    full_ref[rows:, :] = edge_tile(high[0:1], low[0:1])
    forward_copy.wait()
    for x_ref, y_ref, move_ref in zip(x_refs, y_refs, move_refs):
        for source_ref, target_ref in ((full_ref, x_ref), (flip_ref, y_ref)):
            target_ref[...] = jnp.dot(
                source_ref[...], move_ref[...], preferred_element_type=jnp.float32
            ).astype(jnp.bfloat16)


def prepare(place, forward_embed, reverse_embed, low, high):
    rows, width = forward_embed.shape
    kept = rows - AWAY
    part = width // 16
    inside = pl.BlockSpec(memory_space=pltpu.VMEM)

    def stripes(height):
        return [jax.ShapeDtypeStruct((height, count * part), jnp.bfloat16) for count in PARTS]

    outs = pl.pallas_call(
        prepare_kernel,
        out_shape=stripes(rows + EDGE)
        + stripes(kept + EDGE)
        + stripes(width)
        + [jax.ShapeDtypeStruct((AWAY + EDGE, width), jnp.bfloat16), TOKEN],
        in_specs=[pl.BlockSpec(memory_space=pltpu.SMEM)]
        + [pl.BlockSpec(memory_space=pltpu.HBM)] * 2
        + [inside] * 2,
        out_specs=[inside] * 11,
        scratch_shapes=[
            pltpu.VMEM((rows + EDGE, width), jnp.bfloat16),
            pltpu.VMEM((kept + EDGE, width), jnp.bfloat16),
            pltpu.VMEM((rows, width), jnp.bfloat16),
            pltpu.SemaphoreType.DMA((2,)),
        ],
        compiler_params=pltpu.CompilerParams(vmem_limit_bytes=VMEM_LIMIT),
        cost_estimate=pl.CostEstimate(
            flops=4 * rows * width * width, bytes_accessed=8 * rows * width, transcendentals=0
        ),
        name="prepare",
    )(place, forward_embed, reverse_embed, low, high)
    return list(zip(outs[:3], outs[3:6])), outs[6:9], outs[9], outs[10]


def convolve(x, flipped, blocks, columns):
    rows = x.shape[0] - EDGE
    total = None
    for tap in range(3):
        weight = jnp.concatenate([block[tap, :, columns] for block in blocks], axis=0)
        value = jnp.dot(x, weight, preferred_element_type=jnp.float32)
        shift = tap - 1 if flipped else 1 - tap
        if shift:
            value = pltpu.roll(value, shift % (rows + EDGE), 0)
        value = value[:rows]
        total = value if total is None else total + value
    return total


def partial_kernel(count, first, *refs):
    strands, blocks, refs = refs[:2], refs[2 : 2 + count], refs[2 + count :]
    out_refs, token_ref = refs[-3:-1], refs[-1]
    token_ref[...] = jnp.zeros_like(token_ref)
    channels = out_refs[0].shape[1]
    for start in range(0, channels, TILE):
        columns = pl.ds(start, TILE)
        for strand in range(2):
            acc = convolve(strands[strand][...], strand == 1, blocks, columns)
            if not first:
                acc = acc + refs[strand][:, columns]
            out_refs[strand][:, columns] = acc


def partial_sum(strands, sources, prev):
    rows = [x.shape[0] - EDGE for x in strands]
    depth, channels = strands[0].shape[1], sources[0].shape[2]
    operands = [*strands, *sources] + ([] if prev is None else list(prev))
    inside = pl.BlockSpec(memory_space=pltpu.VMEM)
    last = len(operands)
    forward, reverse, token = pl.pallas_call(
        functools.partial(partial_kernel, len(sources), prev is None),
        out_shape=[jax.ShapeDtypeStruct((count, channels), jnp.float32) for count in rows]
        + [TOKEN],
        in_specs=[inside] * last,
        out_specs=[inside] * 3,
        input_output_aliases={} if prev is None else {last - 2: 0, last - 1: 1},
        compiler_params=pltpu.CompilerParams(vmem_limit_bytes=VMEM_LIMIT),
        cost_estimate=pl.CostEstimate(
            flops=6 * sum(rows) * depth * channels,
            bytes_accessed=6 * depth * channels,
            transcendentals=0,
        ),
        name="partial_sum",
    )(*operands)
    return (forward, reverse), token


def gelu(acc):
    return (0.5 * acc * (1.0 + lax.erf(acc * INV_SQRT2))).astype(jnp.bfloat16)


def predict(hidden_ref, head_ref, head_bias_ref, out_ref):
    rows = out_ref.shape[0]
    for row in range(0, rows, ROWS):
        here = pl.ds(row, ROWS)
        logits = jnp.dot(hidden_ref[here, :], head_ref[...], preferred_element_type=jnp.float32)
        logits = logits + head_bias_ref[...]
        tracks = jnp.maximum(logits, 0.0) + jnp.log1p(jnp.exp(-jnp.abs(logits)))
        out_ref[here, :] = tracks.astype(jnp.bfloat16)


def finish_kernel(flipped, count, x_ref, *refs):
    sources, refs = refs[:count], refs[count:]
    prev_ref, bias_ref, head_ref, head_bias_ref, out_ref, hidden_ref = refs
    for start in range(0, hidden_ref.shape[1], TILE):
        here = pl.ds(start, TILE)
        acc = convolve(x_ref[...], flipped, sources, here)
        hidden_ref[:, here] = gelu(acc + prev_ref[:, here] + bias_ref[:, here])
    predict(hidden_ref, head_ref, head_bias_ref, out_ref)


def finish(flipped, x, sources, prev, bias, head, head_bias):
    rows, depth = x.shape[0] - EDGE, x.shape[1]
    channels, tracks = head.shape
    inside = pl.BlockSpec(memory_space=pltpu.VMEM)
    return pl.pallas_call(
        functools.partial(finish_kernel, flipped, len(sources)),
        out_shape=jax.ShapeDtypeStruct((rows, tracks), jnp.bfloat16),
        in_specs=[inside] * (len(sources) + 5),
        out_specs=inside,
        scratch_shapes=[pltpu.VMEM((rows, channels), jnp.bfloat16)],
        compiler_params=pltpu.CompilerParams(vmem_limit_bytes=VMEM_LIMIT),
        cost_estimate=pl.CostEstimate(
            flops=2 * rows * channels * (3 * depth + tracks),
            bytes_accessed=6 * depth * channels + 2 * channels * tracks,
            transcendentals=rows * channels,
        ),
        name="finish",
    )(x, *sources, prev, bias, head, head_bias[None])


def whole_kernel(sizes, away_ref, *refs):
    moves, refs = refs[: len(sizes)], refs[len(sizes) :]
    sources, refs = refs[: sum(sizes)], refs[sum(sizes) :]
    bias_ref, head_ref, head_bias_ref, out_ref, hidden_ref = refs
    stripes = [
        jnp.dot(away_ref[...], move[...], preferred_element_type=jnp.float32).astype(jnp.bfloat16)
        for move in moves
    ]
    for start in range(0, hidden_ref.shape[1], TILE):
        here = pl.ds(start, TILE)
        acc, begin = bias_ref[:, here], 0
        for stripe, count in zip(stripes, sizes):
            acc = acc + convolve(stripe, True, sources[begin : begin + count], here)
            begin += count
        hidden_ref[:, here] = gelu(acc)
    predict(hidden_ref, head_ref, head_bias_ref, out_ref)


def whole(away, moves, sources, bias, head, head_bias):
    rows = away.shape[0] - EDGE
    channels, tracks = head.shape
    inside = pl.BlockSpec(memory_space=pltpu.VMEM)
    return pl.pallas_call(
        functools.partial(whole_kernel, PARTS),
        out_shape=jax.ShapeDtypeStruct((rows, tracks), jnp.bfloat16),
        in_specs=[inside] * (len(moves) + len(sources) + 4),
        out_specs=inside,
        scratch_shapes=[pltpu.VMEM((rows, channels), jnp.bfloat16)],
        compiler_params=pltpu.CompilerParams(vmem_limit_bytes=VMEM_LIMIT),
        cost_estimate=pl.CostEstimate(
            flops=2 * rows * channels * (4 * channels + tracks),
            bytes_accessed=6 * channels * channels,
            transcendentals=rows * channels,
        ),
        name="whole",
    )(away, *moves, *sources, bias, head, head_bias[None])


def per_device(forward_embed, reverse_embed, conv_weight, conv_bias, head_weight, head_bias):
    own = conv_weight[0]
    x, y, core = lax.axis_index("x"), lax.axis_index("y_lo"), lax.axis_index("core")
    ends = XN * 2 * CN

    def seq(x_of, y_of, core_of):
        return (x_of % XN) * 4 + y_of * 2 + core_of

    step = 1 - 2 * core
    back, fore, far = x - step + XN, x + step + XN, x + 2
    other, over = 1 - core, 1 - y
    place = jnp.stack(
        [
            seq(x, y, core), seq(x, y, other), seq(x, over, core), seq(x, over, other),
            seq(back, y, core), seq(fore, y, other), seq(back, y, other), seq(fore, y, core),
            seq(back, over, core), seq(fore, over, other), seq(far, y, core), seq(far, y, other),
            seq(back, over, other), seq(fore, over, core),
            seq(far, over, core), seq(far, over, other),
        ]
    ).astype(jnp.int32)

    near = x_shift(own)
    across = y_shift(own)
    sibling = core_swap(own)
    second = x_shift(sibling)
    up = [(i, i + 1) for i in range(ends - 1)]
    down = [(b, a) for a, b in up]
    low = lax.ppermute(jnp.stack([forward_embed[-1], reverse_embed[-1]]), SEQ, up)
    high = lax.ppermute(jnp.stack([forward_embed[0], reverse_embed[0]]), SEQ, down)
    (x_1, x_2, x_3), moves, away, token = prepare(place, forward_embed, reverse_embed, low, high)
    near, across = fence(token, near, across)

    distant = x_shift(near)
    near_over = y_shift(near)
    across_b = core_swap(across)
    near_b = core_swap(near)
    second_b = core_swap(second)
    shards_1 = [own, sibling, across, across_b, near, near_b, second, second_b]
    acc, token = partial_sum(x_1, shards_1, None)
    distant, near_over, across_b = fence(token, distant, near_over, across_b)
    shards_1[3] = across_b

    second_over = x_shift(across_b)
    distant_over = y_shift(distant)
    near_over_b = core_swap(near_over)
    distant_b = core_swap(distant)
    shards_2 = [near_over, near_over_b, distant, distant_b]
    acc, token = partial_sum(x_2, shards_2, acc)
    second_over, distant_over, away = fence(token, second_over, distant_over, away)

    mirror = [(i, ends - 1 - i) for i in range(ends)]
    away = lax.ppermute(away, SEQ, mirror)
    shards_3 = [second_over, core_swap(second_over), distant_over, core_swap(distant_over)]
    rest = (conv_bias, head_weight, head_bias)
    reverse_tracks = finish(True, x_3[1], shards_3, acc[1], *rest)
    mirrored = lax.ppermute(reverse_tracks, SEQ, mirror)
    forward_tracks = finish(False, x_3[0], shards_3, acc[0], *rest)
    away_tracks = whole(away, moves, shards_1 + shards_2 + shards_3, *rest)
    reverse = jnp.concatenate([mirrored, away_tracks])
    mean = 0.5 * (forward_tracks.astype(jnp.float32) + reverse.astype(jnp.float32))
    return mean.astype(jnp.bfloat16)


def solution(mesh):
    fine = Mesh(mesh.devices.reshape(2, 8, XN, 2, CN), AXES)
    return jax.shard_map(
        per_device,
        mesh=fine,
        in_specs=(
            P(AXES, None),
            P(AXES, None),
            P(None, None, SEQ, None),
            P(),
            P(),
            P(),
        ),
        out_specs=P(AXES, None),
        check_vma=False,
    )
```

```python
import functools

import jax
import jax.numpy as jnp
from jax import lax
from jax.experimental import pallas as pl
from jax.experimental.pallas import tpu as pltpu
from jax.sharding import Mesh
from jax.sharding import PartitionSpec as P

AXES = ("y_hi", "z", "x", "y_lo", "core")
SEQ = ("x", "y_lo", "core")
XN, YN, CN = 4, 4, 2
VMEM_LIMIT = 24 * 1024 * 1024
EDGE = 16
TILE = 512
PARTS = (8, 6, 2)
ROWS = 128
AWAY = 128
TOKEN = jax.ShapeDtypeStruct((8, 128), jnp.float32)
INV_SQRT2 = 0.7071067811865476


def core_swap(value):
    return lax.ppermute(value, "core", [(0, 1), (1, 0)])


def x_shift(value):
    route = []
    for x in range(XN):
        route += [(x * 2, (x + 1) % XN * 2), (x * 2 + 1, (x - 1) % XN * 2 + 1)]
    return lax.ppermute(value, ("x", "core"), route)


def y_shift(value):
    route = []
    for y in range(YN):
        route += [(y * 2, (y + 1) % YN * 2), (y * 2 + 1, (y - 1) % YN * 2 + 1)]
    return lax.ppermute(value, ("y_hi", "y_lo", "core"), route)


def fence_kernel(count, *refs):
    for source, target in zip(refs[:count], refs[-count:]):
        target[...] = source[...]


def fence(token, *values):
    inside = pl.BlockSpec(memory_space=pltpu.VMEM)
    operands = values if token is None else (*values, token)
    return pl.pallas_call(
        functools.partial(fence_kernel, len(values)),
        out_shape=[jax.ShapeDtypeStruct(v.shape, v.dtype) for v in values],
        in_specs=[inside] * len(operands),
        out_specs=[inside] * len(values),
        input_output_aliases={i: i for i in range(len(values))},
        compiler_params=pltpu.CompilerParams(vmem_limit_bytes=8 * 1024 * 1024),
        name="fence",
    )(*operands)


def edge_tile(after, before):
    width = after.shape[1]
    edge = lax.broadcasted_iota(jnp.int32, (EDGE, width), 0)
    tile = jnp.where(edge == 0, after, jnp.where(edge == EDGE - 1, before, 0.0))
    return tile.astype(jnp.bfloat16)


def prepare_kernel(place_ref, forward_ref, reverse_ref, low_ref, high_ref, *refs):
    x_refs, y_refs, move_refs, away_ref, token_ref = refs[:3], refs[3:6], refs[6:9], *refs[9:11]
    full_ref, flip_ref, reverse_vmem, sem = refs[11:]
    token_ref[...] = jnp.zeros_like(token_ref)
    rows, width = forward_ref.shape
    kept = rows - AWAY
    part = width // 16
    forward_copy = pltpu.make_async_copy(forward_ref, full_ref.at[pl.ds(0, rows), :], sem.at[0])
    forward_copy.start()
    reverse_copy = pltpu.make_async_copy(reverse_ref, reverse_vmem, sem.at[1])
    reverse_copy.start()
    begin = 0
    for move_ref, count in zip(move_refs, PARTS):
        size = count * part
        lane = lax.broadcasted_iota(jnp.int32, (1, size), 1)
        wanted = jnp.zeros((1, size), jnp.int32)
        for block in range(count):
            inside = (lane >= block * part) & (lane < (block + 1) * part)
            wanted = jnp.where(inside, lane + (place_ref[begin + block] - block) * part, wanted)
        source = lax.broadcasted_iota(jnp.int32, (width, size), 0)
        move_ref[...] = jnp.where(source == wanted, 1.0, 0.0).astype(jnp.bfloat16)
        begin += count
    low = low_ref[...].astype(jnp.float32)
    high = high_ref[...].astype(jnp.float32)
    row = lax.broadcasted_iota(jnp.int32, (rows, rows), 0)
    column = lax.broadcasted_iota(jnp.int32, (rows, rows), 1)
    flip = jnp.where(row + column == rows - 1, 1.0, 0.0).astype(jnp.bfloat16)
    reverse_copy.wait()
    flipped = jnp.dot(flip, reverse_vmem[...], preferred_element_type=jnp.float32)
    flip_ref[:kept, :] = flipped[:kept].astype(jnp.bfloat16)
    flip_ref[kept:, :] = edge_tile(flipped[kept : kept + 1], high[1:2])
    away_ref[:AWAY, :] = flipped[kept:].astype(jnp.bfloat16)
    away_ref[AWAY:, :] = edge_tile(low[1:2], flipped[kept - 1 : kept])
    full_ref[rows:, :] = edge_tile(high[0:1], low[0:1])
    forward_copy.wait()
    for x_ref, y_ref, move_ref in zip(x_refs, y_refs, move_refs):
        for source_ref, target_ref in ((full_ref, x_ref), (flip_ref, y_ref)):
            target_ref[...] = jnp.dot(
                source_ref[...], move_ref[...], preferred_element_type=jnp.float32
            ).astype(jnp.bfloat16)


def prepare(place, forward_embed, reverse_embed, low, high):
    rows, width = forward_embed.shape
    kept = rows - AWAY
    part = width // 16
    inside = pl.BlockSpec(memory_space=pltpu.VMEM)

    def stripes(height):
        return [jax.ShapeDtypeStruct((height, count * part), jnp.bfloat16) for count in PARTS]

    outs = pl.pallas_call(
        prepare_kernel,
        out_shape=stripes(rows + EDGE)
        + stripes(kept + EDGE)
        + stripes(width)
        + [jax.ShapeDtypeStruct((AWAY + EDGE, width), jnp.bfloat16), TOKEN],
        in_specs=[pl.BlockSpec(memory_space=pltpu.SMEM)]
        + [pl.BlockSpec(memory_space=pltpu.HBM)] * 2
        + [inside] * 2,
        out_specs=[inside] * 11,
        scratch_shapes=[
            pltpu.VMEM((rows + EDGE, width), jnp.bfloat16),
            pltpu.VMEM((kept + EDGE, width), jnp.bfloat16),
            pltpu.VMEM((rows, width), jnp.bfloat16),
            pltpu.SemaphoreType.DMA((2,)),
        ],
        compiler_params=pltpu.CompilerParams(vmem_limit_bytes=VMEM_LIMIT),
        cost_estimate=pl.CostEstimate(
            flops=4 * rows * width * width, bytes_accessed=8 * rows * width, transcendentals=0
        ),
        name="prepare",
    )(place, forward_embed, reverse_embed, low, high)
    return list(zip(outs[:3], outs[3:6])), outs[6:9], outs[9], outs[10]


def convolve(x, flipped, blocks, columns):
    rows = x.shape[0] - EDGE
    total = None
    for tap in range(3):
        weight = jnp.concatenate([block[tap, :, columns] for block in blocks], axis=0)
        value = jnp.dot(x, weight, preferred_element_type=jnp.float32)
        shift = tap - 1 if flipped else 1 - tap
        if shift:
            value = pltpu.roll(value, shift % (rows + EDGE), 0)
        value = value[:rows]
        total = value if total is None else total + value
    return total


def partial_kernel(count, first, *refs):
    strands, blocks, refs = refs[:2], refs[2 : 2 + count], refs[2 + count :]
    out_refs, token_ref = refs[-3:-1], refs[-1]
    token_ref[...] = jnp.zeros_like(token_ref)
    channels = out_refs[0].shape[1]
    for start in range(0, channels, TILE):
        columns = pl.ds(start, TILE)
        for strand in range(2):
            acc = convolve(strands[strand][...], strand == 1, blocks, columns)
            if not first:
                acc = acc + refs[strand][:, columns]
            out_refs[strand][:, columns] = acc


def partial_sum(strands, sources, prev):
    rows = [x.shape[0] - EDGE for x in strands]
    depth, channels = strands[0].shape[1], sources[0].shape[2]
    operands = [*strands, *sources] + ([] if prev is None else list(prev))
    inside = pl.BlockSpec(memory_space=pltpu.VMEM)
    last = len(operands)
    forward, reverse, token = pl.pallas_call(
        functools.partial(partial_kernel, len(sources), prev is None),
        out_shape=[jax.ShapeDtypeStruct((count, channels), jnp.float32) for count in rows]
        + [TOKEN],
        in_specs=[inside] * last,
        out_specs=[inside] * 3,
        input_output_aliases={} if prev is None else {last - 2: 0, last - 1: 1},
        compiler_params=pltpu.CompilerParams(vmem_limit_bytes=VMEM_LIMIT),
        cost_estimate=pl.CostEstimate(
            flops=6 * sum(rows) * depth * channels,
            bytes_accessed=6 * depth * channels,
            transcendentals=0,
        ),
        name="partial_sum",
    )(*operands)
    return (forward, reverse), token


def gelu(acc):
    return (0.5 * acc * (1.0 + lax.erf(acc * INV_SQRT2))).astype(jnp.bfloat16)


def predict(hidden_ref, head_ref, head_bias_ref, out_ref):
    rows = out_ref.shape[0]
    for row in range(0, rows, ROWS):
        here = pl.ds(row, ROWS)
        logits = jnp.dot(hidden_ref[here, :], head_ref[...], preferred_element_type=jnp.float32)
        logits = logits + head_bias_ref[...]
        tracks = jnp.maximum(logits, 0.0) + jnp.log1p(jnp.exp(-jnp.abs(logits)))
        out_ref[here, :] = tracks.astype(jnp.bfloat16)


def finish_kernel(flipped, count, x_ref, *refs):
    sources, refs = refs[:count], refs[count:]
    prev_ref, bias_ref, head_ref, head_bias_ref, out_ref, hidden_ref = refs
    for start in range(0, hidden_ref.shape[1], TILE):
        here = pl.ds(start, TILE)
        acc = convolve(x_ref[...], flipped, sources, here)
        hidden_ref[:, here] = gelu(acc + prev_ref[:, here] + bias_ref[:, here])
    predict(hidden_ref, head_ref, head_bias_ref, out_ref)


def finish(flipped, x, sources, prev, bias, head, head_bias):
    rows, depth = x.shape[0] - EDGE, x.shape[1]
    channels, tracks = head.shape
    inside = pl.BlockSpec(memory_space=pltpu.VMEM)
    return pl.pallas_call(
        functools.partial(finish_kernel, flipped, len(sources)),
        out_shape=jax.ShapeDtypeStruct((rows, tracks), jnp.bfloat16),
        in_specs=[inside] * (len(sources) + 5),
        out_specs=inside,
        scratch_shapes=[pltpu.VMEM((rows, channels), jnp.bfloat16)],
        compiler_params=pltpu.CompilerParams(vmem_limit_bytes=VMEM_LIMIT),
        cost_estimate=pl.CostEstimate(
            flops=2 * rows * channels * (3 * depth + tracks),
            bytes_accessed=6 * depth * channels + 2 * channels * tracks,
            transcendentals=rows * channels,
        ),
        name="finish",
    )(x, *sources, prev, bias, head, head_bias[None])


def whole_kernel(sizes, away_ref, *refs):
    moves, refs = refs[: len(sizes)], refs[len(sizes) :]
    sources, refs = refs[: sum(sizes)], refs[sum(sizes) :]
    bias_ref, head_ref, head_bias_ref, out_ref, hidden_ref = refs
    stripes = [
        jnp.dot(away_ref[...], move[...], preferred_element_type=jnp.float32).astype(jnp.bfloat16)
        for move in moves
    ]
    for start in range(0, hidden_ref.shape[1], TILE):
        here = pl.ds(start, TILE)
        acc, begin = bias_ref[:, here], 0
        for stripe, count in zip(stripes, sizes):
            acc = acc + convolve(stripe, True, sources[begin : begin + count], here)
            begin += count
        hidden_ref[:, here] = gelu(acc)
    predict(hidden_ref, head_ref, head_bias_ref, out_ref)


def whole(away, moves, sources, bias, head, head_bias):
    rows = away.shape[0] - EDGE
    channels, tracks = head.shape
    inside = pl.BlockSpec(memory_space=pltpu.VMEM)
    return pl.pallas_call(
        functools.partial(whole_kernel, PARTS),
        out_shape=jax.ShapeDtypeStruct((rows, tracks), jnp.bfloat16),
        in_specs=[inside] * (len(moves) + len(sources) + 4),
        out_specs=inside,
        scratch_shapes=[pltpu.VMEM((rows, channels), jnp.bfloat16)],
        compiler_params=pltpu.CompilerParams(vmem_limit_bytes=VMEM_LIMIT),
        cost_estimate=pl.CostEstimate(
            flops=2 * rows * channels * (4 * channels + tracks),
            bytes_accessed=6 * channels * channels,
            transcendentals=rows * channels,
        ),
        name="whole",
    )(away, *moves, *sources, bias, head, head_bias[None])


def per_device(forward_embed, reverse_embed, conv_weight, conv_bias, head_weight, head_bias):
    own = conv_weight[0]
    x, y, core = lax.axis_index("x"), lax.axis_index("y_lo"), lax.axis_index("core")
    ends = XN * 2 * CN

    def seq(x_of, y_of, core_of):
        return (x_of % XN) * 4 + y_of * 2 + core_of

    step = 1 - 2 * core
    back, fore, far = x - step + XN, x + step + XN, x + 2
    other, over = 1 - core, 1 - y
    place = jnp.stack(
        [
            seq(x, y, core), seq(x, y, other), seq(x, over, core), seq(x, over, other),
            seq(back, y, core), seq(fore, y, other), seq(back, y, other), seq(fore, y, core),
            seq(back, over, core), seq(fore, over, other), seq(far, y, core), seq(far, y, other),
            seq(back, over, other), seq(fore, over, core),
            seq(far, over, core), seq(far, over, other),
        ]
    ).astype(jnp.int32)

    near = x_shift(own)
    across = y_shift(own)
    sibling = core_swap(own)
    second = x_shift(sibling)
    up = [(i, i + 1) for i in range(ends - 1)]
    down = [(b, a) for a, b in up]
    low = lax.ppermute(jnp.stack([forward_embed[-1], reverse_embed[-1]]), SEQ, up)
    high = lax.ppermute(jnp.stack([forward_embed[0], reverse_embed[0]]), SEQ, down)
    near, across, low, high = fence(None, near, across, low, high)

    distant = x_shift(near)
    near_over = y_shift(near)
    across_b = core_swap(across)
    near_b = core_swap(near)
    across_b, low, high = fence(None, across_b, low, high)

    second_over = x_shift(across_b)
    second_b = core_swap(second)
    (x_1, x_2, x_3), moves, away, token = prepare(place, forward_embed, reverse_embed, low, high)
    shards_1 = [own, sibling, across, across_b, near, near_b, second, second_b]
    acc, token = partial_sum(x_1, shards_1, None)
    (distant,) = fence(token, distant)

    distant_over = y_shift(distant)
    near_over_b = core_swap(near_over)
    distant_b = core_swap(distant)
    second_over_b = core_swap(second_over)
    shards_2 = [near_over, near_over_b, distant, distant_b, second_over, second_over_b]
    acc, token = partial_sum(x_2, shards_2, acc)
    (away,) = fence(token, away)
    (distant_over,) = fence(token, distant_over)

    mirror = [(i, ends - 1 - i) for i in range(ends)]
    away = lax.ppermute(away, SEQ, mirror)
    shards_3 = [distant_over, core_swap(distant_over)]
    rest = (conv_bias, head_weight, head_bias)
    reverse_tracks = finish(True, x_3[1], shards_3, acc[1], *rest)
    mirrored = lax.ppermute(reverse_tracks, SEQ, mirror)
    forward_tracks = finish(False, x_3[0], shards_3, acc[0], *rest)
    away_tracks = whole(away, moves, shards_1 + shards_2 + shards_3, *rest)
    reverse = jnp.concatenate([mirrored, away_tracks])
    mean = 0.5 * (forward_tracks.astype(jnp.float32) + reverse.astype(jnp.float32))
    return mean.astype(jnp.bfloat16)


def solution(mesh):
    fine = Mesh(mesh.devices.reshape(2, 8, XN, 2, CN), AXES)
    return jax.shard_map(
        per_device,
        mesh=fine,
        in_specs=(
            P(AXES, None),
            P(AXES, None),
            P(None, None, SEQ, None),
            P(),
            P(),
            P(),
        ),
        out_specs=P(AXES, None),
        check_vma=False,
    )
```

```python
import functools

import jax
import jax.numpy as jnp
from jax import lax
from jax.experimental import pallas as pl
from jax.experimental.pallas import tpu as pltpu
from jax.sharding import Mesh
from jax.sharding import PartitionSpec as P

AXES = ("y_hi", "z", "x", "y_lo", "core")
SEQ = ("x", "y_lo", "core")
XN, YN, ZN, CN = 4, 4, 8, 2
VMEM_LIMIT = 24 * 1024 * 1024
EDGE = 16
TILE = 512
PARTS = (12, 10, 10)
SOURCES = (6, 6, 6)
PIECES = 32
ROWS = 128
AWAY = 128
TOKEN = jax.ShapeDtypeStruct((8, 128), jnp.float32)
INV_SQRT2 = 0.7071067811865476


def core_swap(value):
    return lax.ppermute(value, "core", [(0, 1), (1, 0)])


def x_shift(value):
    route = []
    for x in range(XN):
        route += [(x * 2, (x + 1) % XN * 2), (x * 2 + 1, (x - 1) % XN * 2 + 1)]
    return lax.ppermute(value, ("x", "core"), route)


def y_shift(value):
    route = []
    for y in range(YN):
        route += [(y * 2, (y + 1) % YN * 2), (y * 2 + 1, (y - 1) % YN * 2 + 1)]
    return lax.ppermute(value, ("y_hi", "y_lo", "core"), route)


def z_shift(value):
    route = []
    for z in range(ZN):
        route += [(z * 2, (z + 1) % ZN * 2), (z * 2 + 1, (z - 1) % ZN * 2 + 1)]
    return lax.ppermute(value, ("z", "core"), route)


def fence_kernel(count, *refs):
    for source, target in zip(refs[:count], refs[-count:]):
        target[...] = source[...]


def fence(token, *values):
    inside = pl.BlockSpec(memory_space=pltpu.VMEM)
    operands = values if token is None else (*values, token)
    return pl.pallas_call(
        functools.partial(fence_kernel, len(values)),
        out_shape=[jax.ShapeDtypeStruct(v.shape, v.dtype) for v in values],
        in_specs=[inside] * len(operands),
        out_specs=[inside] * len(values),
        input_output_aliases={i: i for i in range(len(values))},
        compiler_params=pltpu.CompilerParams(vmem_limit_bytes=8 * 1024 * 1024),
        name="fence",
    )(*operands)


def edge_tile(after, before):
    width = after.shape[1]
    edge = lax.broadcasted_iota(jnp.int32, (EDGE, width), 0)
    tile = jnp.where(edge == 0, after, jnp.where(edge == EDGE - 1, before, 0.0))
    return tile.astype(jnp.bfloat16)


def order_kernel(place_ref, reverse_ref, *refs):
    move_refs, flipped_ref, token_ref = refs[:3], refs[3], refs[4]
    token_ref[...] = jnp.zeros_like(token_ref)
    rows, width = reverse_ref.shape
    part = width // PIECES
    begin = 0
    for move_ref, count in zip(move_refs, PARTS):
        size = count * part
        lane = lax.broadcasted_iota(jnp.int32, (1, size), 1)
        wanted = jnp.zeros((1, size), jnp.int32)
        for block in range(count):
            inside = (lane >= block * part) & (lane < (block + 1) * part)
            wanted = jnp.where(inside, lane + (place_ref[begin + block] - block) * part, wanted)
        source = lax.broadcasted_iota(jnp.int32, (width, size), 0)
        move_ref[...] = jnp.where(source == wanted, 1.0, 0.0).astype(jnp.bfloat16)
        begin += count
    row = lax.broadcasted_iota(jnp.int32, (rows, rows), 0)
    column = lax.broadcasted_iota(jnp.int32, (rows, rows), 1)
    flip = jnp.where(row + column == rows - 1, 1.0, 0.0).astype(jnp.bfloat16)
    flipped = jnp.dot(flip, reverse_ref[...], preferred_element_type=jnp.float32)
    flipped_ref[...] = flipped.astype(jnp.bfloat16)


def order(place, reverse_embed):
    rows, width = reverse_embed.shape
    part = width // PIECES
    inside = pl.BlockSpec(memory_space=pltpu.VMEM)
    outs = pl.pallas_call(
        order_kernel,
        out_shape=[jax.ShapeDtypeStruct((width, count * part), jnp.bfloat16) for count in PARTS]
        + [jax.ShapeDtypeStruct((rows, width), jnp.bfloat16), TOKEN],
        in_specs=[pl.BlockSpec(memory_space=pltpu.SMEM), inside],
        out_specs=[inside] * 5,
        compiler_params=pltpu.CompilerParams(vmem_limit_bytes=VMEM_LIMIT),
        cost_estimate=pl.CostEstimate(
            flops=16 * rows * width * width, bytes_accessed=8 * rows * width, transcendentals=0
        ),
        name="order",
    )(place, reverse_embed)
    return outs[:3], outs[3], outs[4]


def edge_tile(after, before):
    width = after.shape[1]
    edge = lax.broadcasted_iota(jnp.int32, (EDGE, width), 0)
    tile = jnp.where(edge == 0, after, jnp.where(edge == EDGE - 1, before, 0.0))
    return tile.astype(jnp.bfloat16)


def prepare_kernel(forward_ref, flipped_ref, low_ref, high_ref, *refs):
    move_refs, x_refs, y_refs, (away_ref, token_ref, edge_ref) = (
        refs[:3], refs[3:6], refs[6:9], refs[9:],
    )
    token_ref[...] = jnp.zeros_like(token_ref)
    rows = forward_ref.shape[0]
    kept = rows - AWAY
    low = low_ref[...].astype(jnp.float32)
    high = high_ref[...].astype(jnp.float32)
    next_row = flipped_ref[pl.ds(kept, EDGE), :].astype(jnp.float32)[0:1]
    past_row = flipped_ref[pl.ds(kept - EDGE, EDGE), :].astype(jnp.float32)[EDGE - 1 :]
    away_ref[:AWAY, :] = flipped_ref[pl.ds(kept, AWAY), :]
    away_ref[AWAY:, :] = edge_tile(low[1:2], past_row)
    edge_ref[:EDGE, :] = edge_tile(high[0:1], low[0:1])
    edge_ref[EDGE:, :] = edge_tile(next_row, high[1:2])
    for x_ref, y_ref, move_ref in zip(x_refs, y_refs, move_refs):
        edges = jnp.dot(edge_ref[...], move_ref[...], preferred_element_type=jnp.float32)
        edges = edges.astype(jnp.bfloat16)
        x_ref[:rows, :] = jnp.dot(
            forward_ref[...], move_ref[...], preferred_element_type=jnp.float32
        ).astype(jnp.bfloat16)
        x_ref[rows:, :] = edges[:EDGE]
        y_ref[:kept, :] = jnp.dot(
            flipped_ref[pl.ds(0, kept), :], move_ref[...], preferred_element_type=jnp.float32
        ).astype(jnp.bfloat16)
        y_ref[kept:, :] = edges[EDGE:]


def prepare(forward_embed, flipped, low, high, moves):
    rows, width = forward_embed.shape
    kept = rows - AWAY
    part = width // PIECES
    inside = pl.BlockSpec(memory_space=pltpu.VMEM)

    def stripes(height):
        return [jax.ShapeDtypeStruct((height, count * part), jnp.bfloat16) for count in PARTS]

    outs = pl.pallas_call(
        prepare_kernel,
        out_shape=stripes(rows + EDGE)
        + stripes(kept + EDGE)
        + [jax.ShapeDtypeStruct((AWAY + EDGE, width), jnp.bfloat16), TOKEN],
        in_specs=[inside] * 7,
        out_specs=[inside] * 8,
        scratch_shapes=[pltpu.VMEM((2 * EDGE, width), jnp.bfloat16)],
        compiler_params=pltpu.CompilerParams(vmem_limit_bytes=VMEM_LIMIT),
        cost_estimate=pl.CostEstimate(flops=1000, bytes_accessed=1000, transcendentals=0),
        name="prepare",
    )(forward_embed, flipped, low, high, *moves)
    return list(zip(outs[:3], outs[3:6])), outs[6], outs[7]


def convolve(x, flipped, blocks, columns):
    rows = x.shape[0] - EDGE
    total = None
    for tap in range(3):
        weight = jnp.concatenate([block[tap, :, columns] for block in blocks], axis=0)
        value = jnp.dot(x, weight, preferred_element_type=jnp.float32)
        shift = tap - 1 if flipped else 1 - tap
        if shift:
            value = pltpu.roll(value, shift % (rows + EDGE), 0)
        value = value[:rows]
        total = value if total is None else total + value
    return total


def partial_kernel(count, first, *refs):
    strands, blocks, refs = refs[:2], refs[2 : 2 + count], refs[2 + count :]
    out_refs, token_ref = refs[-3:-1], refs[-1]
    token_ref[...] = jnp.zeros_like(token_ref)
    channels = out_refs[0].shape[1]
    for start in range(0, channels, TILE):
        columns = pl.ds(start, TILE)
        for strand in range(2):
            acc = convolve(strands[strand][...], strand == 1, blocks, columns)
            if not first:
                acc = acc + refs[strand][:, columns]
            out_refs[strand][:, columns] = acc


def partial_sum(strands, sources, prev):
    rows = [x.shape[0] - EDGE for x in strands]
    depth, channels = strands[0].shape[1], sources[0].shape[2]
    operands = [*strands, *sources] + ([] if prev is None else list(prev))
    inside = pl.BlockSpec(memory_space=pltpu.VMEM)
    last = len(operands)
    forward, reverse, token = pl.pallas_call(
        functools.partial(partial_kernel, len(sources), prev is None),
        out_shape=[jax.ShapeDtypeStruct((count, channels), jnp.float32) for count in rows]
        + [TOKEN],
        in_specs=[inside] * last,
        out_specs=[inside] * 3,
        input_output_aliases={} if prev is None else {last - 2: 0, last - 1: 1},
        compiler_params=pltpu.CompilerParams(vmem_limit_bytes=VMEM_LIMIT),
        cost_estimate=pl.CostEstimate(
            flops=6 * sum(rows) * depth * channels,
            bytes_accessed=6 * depth * channels,
            transcendentals=0,
        ),
        name="partial_sum",
    )(*operands)
    return (forward, reverse), token


def gelu(acc):
    return (0.5 * acc * (1.0 + lax.erf(acc * INV_SQRT2))).astype(jnp.bfloat16)


def predict(hidden_ref, head_ref, head_bias_ref, out_ref):
    rows = out_ref.shape[0]
    for row in range(0, rows, ROWS):
        here = pl.ds(row, ROWS)
        logits = jnp.dot(hidden_ref[here, :], head_ref[...], preferred_element_type=jnp.float32)
        logits = logits + head_bias_ref[...]
        tracks = jnp.maximum(logits, 0.0) + jnp.log1p(jnp.exp(-jnp.abs(logits)))
        out_ref[here, :] = tracks.astype(jnp.bfloat16)


def finish_kernel(flipped, count, x_ref, *refs):
    sources, refs = refs[:count], refs[count:]
    prev_ref, bias_ref, head_ref, head_bias_ref, out_ref, hidden_ref = refs
    for start in range(0, hidden_ref.shape[1], TILE):
        here = pl.ds(start, TILE)
        acc = convolve(x_ref[...], flipped, sources, here)
        hidden_ref[:, here] = gelu(acc + prev_ref[:, here] + bias_ref[:, here])
    predict(hidden_ref, head_ref, head_bias_ref, out_ref)


def finish(flipped, x, sources, prev, bias, head, head_bias):
    rows, depth = x.shape[0] - EDGE, x.shape[1]
    channels, tracks = head.shape
    inside = pl.BlockSpec(memory_space=pltpu.VMEM)
    return pl.pallas_call(
        functools.partial(finish_kernel, flipped, len(sources)),
        out_shape=jax.ShapeDtypeStruct((rows, tracks), jnp.bfloat16),
        in_specs=[inside] * (len(sources) + 5),
        out_specs=inside,
        scratch_shapes=[pltpu.VMEM((rows, channels), jnp.bfloat16)],
        compiler_params=pltpu.CompilerParams(vmem_limit_bytes=VMEM_LIMIT),
        cost_estimate=pl.CostEstimate(
            flops=2 * rows * channels * (3 * depth + tracks),
            bytes_accessed=6 * depth * channels + 2 * channels * tracks,
            transcendentals=rows * channels,
        ),
        name="finish",
    )(x, *sources, prev, bias, head, head_bias[None])


def whole_kernel(sizes, away_ref, *refs):
    moves, refs = refs[: len(sizes)], refs[len(sizes) :]
    sources, refs = refs[: sum(sizes)], refs[sum(sizes) :]
    bias_ref, head_ref, head_bias_ref, out_ref, hidden_ref = refs
    stripes = [
        jnp.dot(away_ref[...], move[...], preferred_element_type=jnp.float32).astype(jnp.bfloat16)
        for move in moves
    ]
    for start in range(0, hidden_ref.shape[1], TILE):
        here = pl.ds(start, TILE)
        acc, begin = bias_ref[:, here], 0
        for stripe, count in zip(stripes, sizes):
            acc = acc + convolve(stripe, True, sources[begin : begin + count], here)
            begin += count
        hidden_ref[:, here] = gelu(acc)
    predict(hidden_ref, head_ref, head_bias_ref, out_ref)


def whole(away, moves, sources, bias, head, head_bias):
    rows = away.shape[0] - EDGE
    channels, tracks = head.shape
    inside = pl.BlockSpec(memory_space=pltpu.VMEM)
    return pl.pallas_call(
        functools.partial(whole_kernel, SOURCES),
        out_shape=jax.ShapeDtypeStruct((rows, tracks), jnp.bfloat16),
        in_specs=[inside] * (len(moves) + len(sources) + 4),
        out_specs=inside,
        scratch_shapes=[pltpu.VMEM((rows, channels), jnp.bfloat16)],
        compiler_params=pltpu.CompilerParams(vmem_limit_bytes=VMEM_LIMIT),
        cost_estimate=pl.CostEstimate(
            flops=2 * rows * channels * (4 * channels + tracks),
            bytes_accessed=6 * channels * channels,
            transcendentals=rows * channels,
        ),
        name="whole",
    )(away, *moves, *sources, bias, head, head_bias[None])


def per_device(forward_embed, reverse_embed, conv_weight, conv_bias, head_weight, head_bias):
    own = conv_weight[0]
    x, y, core = lax.axis_index("x"), lax.axis_index("y_lo"), lax.axis_index("core")
    ends = XN * 2 * CN

    def seq(x_of, y_of, core_of):
        return (x_of % XN) * 4 + y_of * 2 + core_of

    step = 1 - 2 * core
    back, fore, far = x - step + XN, x + step + XN, x + 2
    other, over = 1 - core, 1 - y
    odd = lax.axis_index("z") % 2

    def both(*shards):
        return [2 * shard + half for shard in shards for half in range(2)]

    place = jnp.stack(
        both(
            seq(x, y, core), seq(x, y, other), seq(x, over, core), seq(x, over, other),
            seq(back, y, core), seq(fore, y, other),
            seq(back, over, core), seq(fore, over, other), seq(far, y, core), seq(far, y, other),
        )
        + [2 * seq(back, y, other) + odd, 2 * seq(fore, y, core) + odd]
        + [2 * seq(back, y, other) + 1 - odd, 2 * seq(fore, y, core) + 1 - odd]
        + both(
            seq(back, over, other), seq(fore, over, core),
            seq(far, over, core), seq(far, over, other),
        )
    ).astype(jnp.int32)

    with jax.named_scope("near"):
        near = x_shift(own)
    with jax.named_scope("across"):
        across = y_shift(own)
    with jax.named_scope("sibling"):
        sibling = core_swap(own)
    half = own.shape[1] // 2
    sibling_half = lax.dynamic_slice_in_dim(sibling, odd * half, half, 1)
    with jax.named_scope("second"):
        second = x_shift(sibling_half)
    up = [(i, i + 1) for i in range(ends - 1)]
    down = [(b, a) for a, b in up]
    with jax.named_scope("low"):
        low = lax.ppermute(jnp.stack([forward_embed[-1], reverse_embed[-1]]), SEQ, up)
    with jax.named_scope("high"):
        high = lax.ppermute(jnp.stack([forward_embed[0], reverse_embed[0]]), SEQ, down)
    moves, flipped, token = order(place, reverse_embed)
    near, across, low, high = fence(token, near, across, low, high)

    with jax.named_scope("distant"):
        distant = x_shift(near)
    with jax.named_scope("near_over"):
        near_over = y_shift(near)
    with jax.named_scope("across_b"):
        across_b = core_swap(across)
    with jax.named_scope("near_b"):
        near_b = core_swap(near)
    (x_1, x_2, x_3), away, token = prepare(forward_embed, flipped, low, high, moves)
    shards_1 = [own, sibling, across, across_b, near, near_b]
    acc, token = partial_sum(x_1, shards_1, None)
    distant, near_over, across_b, second = fence(token, distant, near_over, across_b, second)
    shards_1[3] = across_b

    with jax.named_scope("second_z"):
        second_z = z_shift(second)
    with jax.named_scope("second_over"):
        second_over = x_shift(across_b)
    with jax.named_scope("distant_over"):
        distant_over = y_shift(distant)
    with jax.named_scope("near_over_b"):
        near_over_b = core_swap(near_over)
    with jax.named_scope("distant_b"):
        distant_b = core_swap(distant)
    with jax.named_scope("second_b"):
        second_b = core_swap(second)
    shards_2 = [near_over, near_over_b, distant, distant_b, second, second_b]
    acc, token = partial_sum(x_2, shards_2, acc)
    second_over, distant_over, second_z, away = fence(
        token, second_over, distant_over, second_z, away
    )

    mirror = [(i, ends - 1 - i) for i in range(ends)]
    with jax.named_scope("away"):
        away = lax.ppermute(away, SEQ, mirror)
    with jax.named_scope("second_over_b"):
        second_over_b = core_swap(second_over)
    with jax.named_scope("distant_over_b"):
        distant_over_b = core_swap(distant_over)
    with jax.named_scope("second_z_b"):
        second_z_b = core_swap(second_z)
    shards_3 = [second_z, second_z_b, second_over, second_over_b, distant_over, distant_over_b]
    rest = (conv_bias, head_weight, head_bias)
    reverse_tracks = finish(True, x_3[1], shards_3, acc[1], *rest)
    with jax.named_scope("mirrored"):
        mirrored = lax.ppermute(reverse_tracks, SEQ, mirror)
    forward_tracks = finish(False, x_3[0], shards_3, acc[0], *rest)
    away_tracks = whole(away, moves, shards_1 + shards_2 + shards_3, *rest)
    reverse = jnp.concatenate([mirrored, away_tracks])
    mean = 0.5 * (forward_tracks.astype(jnp.float32) + reverse.astype(jnp.float32))
    return mean.astype(jnp.bfloat16)


def solution(mesh):
    fine = Mesh(mesh.devices.reshape(2, 8, XN, 2, CN), AXES)
    return jax.shard_map(
        per_device,
        mesh=fine,
        in_specs=(
            P(AXES, None),
            P(AXES, None),
            P(None, None, SEQ, None),
            P(),
            P(),
            P(),
        ),
        out_specs=P(AXES, None),
        check_vma=False,
    )
```

```python
import functools

import jax
import jax.numpy as jnp
from jax import lax
from jax.experimental import pallas as pl
from jax.experimental.pallas import tpu as pltpu
from jax.sharding import Mesh
from jax.sharding import PartitionSpec as P

AXES = ("y_hi", "z", "x", "y_lo", "core")
SEQ = ("x", "y_lo", "core")
XN, YN, ZN, CN = 4, 4, 8, 2
VMEM_LIMIT = 24 * 1024 * 1024
EDGE = 16
TILE = 512
PARTS = (12, 10, 10)
SOURCES = (6, 6, 6)
PIECES = 32
FIRST_HALF = 20
ROWS = 128
AWAY = 128
TOKEN = jax.ShapeDtypeStruct((8, 128), jnp.float32)
INV_SQRT2 = 0.7071067811865476


def core_swap(value):
    return lax.ppermute(value, "core", [(0, 1), (1, 0)])


def x_shift(value):
    route = []
    for x in range(XN):
        route += [(x * 2, (x + 1) % XN * 2), (x * 2 + 1, (x - 1) % XN * 2 + 1)]
    return lax.ppermute(value, ("x", "core"), route)


def y_shift(value):
    route = []
    for y in range(YN):
        route += [(y * 2, (y + 1) % YN * 2), (y * 2 + 1, (y - 1) % YN * 2 + 1)]
    return lax.ppermute(value, ("y_hi", "y_lo", "core"), route)


def z_shift(value):
    route = []
    for z in range(ZN):
        route += [(z * 2, (z + 1) % ZN * 2), (z * 2 + 1, (z - 1) % ZN * 2 + 1)]
    return lax.ppermute(value, ("z", "core"), route)


def fence_kernel(count, *refs):
    for source, target in zip(refs[:count], refs[-count:]):
        target[...] = source[...]


def fence(token, *values):
    inside = pl.BlockSpec(memory_space=pltpu.VMEM)
    operands = values if token is None else (*values, token)
    return pl.pallas_call(
        functools.partial(fence_kernel, len(values)),
        out_shape=[jax.ShapeDtypeStruct(v.shape, v.dtype) for v in values],
        in_specs=[inside] * len(operands),
        out_specs=[inside] * len(values),
        input_output_aliases={i: i for i in range(len(values))},
        compiler_params=pltpu.CompilerParams(vmem_limit_bytes=8 * 1024 * 1024),
        name="fence",
    )(*operands)


def edge_tile(after, before):
    width = after.shape[1]
    edge = lax.broadcasted_iota(jnp.int32, (EDGE, width), 0)
    tile = jnp.where(edge == 0, after, jnp.where(edge == EDGE - 1, before, 0.0))
    return tile.astype(jnp.bfloat16)


def halve_kernel(place_ref, shard_ref, out_ref):
    half = out_ref.shape[1]
    odd = lax.rem(place_ref[FIRST_HALF], 2)

    @pl.when(odd == 0)
    def _():
        out_ref[...] = shard_ref[:, pl.ds(0, half), :]

    @pl.when(odd == 1)
    def _():
        out_ref[...] = shard_ref[:, pl.ds(half, half), :]


def halve(place, shard):
    taps, rows, columns = shard.shape
    inside = pl.BlockSpec(memory_space=pltpu.VMEM)
    return pl.pallas_call(
        halve_kernel,
        out_shape=jax.ShapeDtypeStruct((taps, rows // 2, columns), shard.dtype),
        in_specs=[pl.BlockSpec(memory_space=pltpu.SMEM), inside],
        out_specs=inside,
        compiler_params=pltpu.CompilerParams(vmem_limit_bytes=8 * 1024 * 1024),
        name="halve",
    )(place, shard)


def order_kernel(place_ref, reverse_ref, *refs):
    move_refs, flipped_ref, token_ref = refs[:3], refs[3], refs[4]
    token_ref[...] = jnp.zeros_like(token_ref)
    rows, width = reverse_ref.shape
    part = width // PIECES
    begin = 0
    for move_ref, count in zip(move_refs, PARTS):
        size = count * part
        lane = lax.broadcasted_iota(jnp.int32, (1, size), 1)
        wanted = jnp.zeros((1, size), jnp.int32)
        for block in range(count):
            inside = (lane >= block * part) & (lane < (block + 1) * part)
            wanted = jnp.where(inside, lane + (place_ref[begin + block] - block) * part, wanted)
        source = lax.broadcasted_iota(jnp.int32, (width, size), 0)
        move_ref[...] = jnp.where(source == wanted, 1.0, 0.0).astype(jnp.bfloat16)
        begin += count
    row = lax.broadcasted_iota(jnp.int32, (rows, rows), 0)
    column = lax.broadcasted_iota(jnp.int32, (rows, rows), 1)
    flip = jnp.where(row + column == rows - 1, 1.0, 0.0).astype(jnp.bfloat16)
    flipped = jnp.dot(flip, reverse_ref[...], preferred_element_type=jnp.float32)
    flipped_ref[...] = flipped.astype(jnp.bfloat16)


def order(place, reverse_embed):
    rows, width = reverse_embed.shape
    part = width // PIECES
    inside = pl.BlockSpec(memory_space=pltpu.VMEM)
    outs = pl.pallas_call(
        order_kernel,
        out_shape=[jax.ShapeDtypeStruct((width, count * part), jnp.bfloat16) for count in PARTS]
        + [jax.ShapeDtypeStruct((rows, width), jnp.bfloat16), TOKEN],
        in_specs=[pl.BlockSpec(memory_space=pltpu.SMEM), inside],
        out_specs=[inside] * 5,
        compiler_params=pltpu.CompilerParams(vmem_limit_bytes=VMEM_LIMIT),
        cost_estimate=pl.CostEstimate(
            flops=16 * rows * width * width, bytes_accessed=8 * rows * width, transcendentals=0
        ),
        name="order",
    )(place, reverse_embed)
    return outs[:3], outs[3], outs[4]


def edge_tile(after, before):
    width = after.shape[1]
    edge = lax.broadcasted_iota(jnp.int32, (EDGE, width), 0)
    tile = jnp.where(edge == 0, after, jnp.where(edge == EDGE - 1, before, 0.0))
    return tile.astype(jnp.bfloat16)


def prepare_kernel(forward_ref, flipped_ref, low_ref, high_ref, *refs):
    move_refs, x_refs, y_refs, (away_ref, token_ref, edge_ref) = (
        refs[:3], refs[3:6], refs[6:9], refs[9:],
    )
    token_ref[...] = jnp.zeros_like(token_ref)
    rows = forward_ref.shape[0]
    kept = rows - AWAY
    low = low_ref[...].astype(jnp.float32)
    high = high_ref[...].astype(jnp.float32)
    next_row = flipped_ref[pl.ds(kept, EDGE), :].astype(jnp.float32)[0:1]
    past_row = flipped_ref[pl.ds(kept - EDGE, EDGE), :].astype(jnp.float32)[EDGE - 1 :]
    away_ref[:AWAY, :] = flipped_ref[pl.ds(kept, AWAY), :]
    away_ref[AWAY:, :] = edge_tile(low[1:2], past_row)
    edge_ref[:EDGE, :] = edge_tile(high[0:1], low[0:1])
    edge_ref[EDGE:, :] = edge_tile(next_row, high[1:2])
    for x_ref, y_ref, move_ref in zip(x_refs, y_refs, move_refs):
        edges = jnp.dot(edge_ref[...], move_ref[...], preferred_element_type=jnp.float32)
        edges = edges.astype(jnp.bfloat16)
        x_ref[:rows, :] = jnp.dot(
            forward_ref[...], move_ref[...], preferred_element_type=jnp.float32
        ).astype(jnp.bfloat16)
        x_ref[rows:, :] = edges[:EDGE]
        y_ref[:kept, :] = jnp.dot(
            flipped_ref[pl.ds(0, kept), :], move_ref[...], preferred_element_type=jnp.float32
        ).astype(jnp.bfloat16)
        y_ref[kept:, :] = edges[EDGE:]


def prepare(forward_embed, flipped, low, high, moves):
    rows, width = forward_embed.shape
    kept = rows - AWAY
    part = width // PIECES
    inside = pl.BlockSpec(memory_space=pltpu.VMEM)

    def stripes(height):
        return [jax.ShapeDtypeStruct((height, count * part), jnp.bfloat16) for count in PARTS]

    outs = pl.pallas_call(
        prepare_kernel,
        out_shape=stripes(rows + EDGE)
        + stripes(kept + EDGE)
        + [jax.ShapeDtypeStruct((AWAY + EDGE, width), jnp.bfloat16), TOKEN],
        in_specs=[inside] * 7,
        out_specs=[inside] * 8,
        scratch_shapes=[pltpu.VMEM((2 * EDGE, width), jnp.bfloat16)],
        compiler_params=pltpu.CompilerParams(vmem_limit_bytes=VMEM_LIMIT),
        cost_estimate=pl.CostEstimate(flops=1000, bytes_accessed=1000, transcendentals=0),
        name="prepare",
    )(forward_embed, flipped, low, high, *moves)
    return list(zip(outs[:3], outs[3:6])), outs[6], outs[7]


def convolve(x, flipped, blocks, columns):
    rows = x.shape[0] - EDGE
    total = None
    for tap in range(3):
        weight = jnp.concatenate([block[tap, :, columns] for block in blocks], axis=0)
        value = jnp.dot(x, weight, preferred_element_type=jnp.float32)
        shift = tap - 1 if flipped else 1 - tap
        if shift:
            value = pltpu.roll(value, shift % (rows + EDGE), 0)
        value = value[:rows]
        total = value if total is None else total + value
    return total


def partial_kernel(count, first, *refs):
    strands, blocks, refs = refs[:2], refs[2 : 2 + count], refs[2 + count :]
    out_refs, token_ref = refs[-3:-1], refs[-1]
    token_ref[...] = jnp.zeros_like(token_ref)
    channels = out_refs[0].shape[1]
    for start in range(0, channels, TILE):
        columns = pl.ds(start, TILE)
        for strand in range(2):
            acc = convolve(strands[strand][...], strand == 1, blocks, columns)
            if not first:
                acc = acc + refs[strand][:, columns]
            out_refs[strand][:, columns] = acc


def partial_sum(strands, sources, prev):
    rows = [x.shape[0] - EDGE for x in strands]
    depth, channels = strands[0].shape[1], sources[0].shape[2]
    operands = [*strands, *sources] + ([] if prev is None else list(prev))
    inside = pl.BlockSpec(memory_space=pltpu.VMEM)
    last = len(operands)
    forward, reverse, token = pl.pallas_call(
        functools.partial(partial_kernel, len(sources), prev is None),
        out_shape=[jax.ShapeDtypeStruct((count, channels), jnp.float32) for count in rows]
        + [TOKEN],
        in_specs=[inside] * last,
        out_specs=[inside] * 3,
        input_output_aliases={} if prev is None else {last - 2: 0, last - 1: 1},
        compiler_params=pltpu.CompilerParams(vmem_limit_bytes=VMEM_LIMIT),
        cost_estimate=pl.CostEstimate(
            flops=6 * sum(rows) * depth * channels,
            bytes_accessed=6 * depth * channels,
            transcendentals=0,
        ),
        name="partial_sum",
    )(*operands)
    return (forward, reverse), token


def gelu(acc):
    return (0.5 * acc * (1.0 + lax.erf(acc * INV_SQRT2))).astype(jnp.bfloat16)


def predict(hidden_ref, head_ref, head_bias_ref, out_ref):
    rows = out_ref.shape[0]
    for row in range(0, rows, ROWS):
        here = pl.ds(row, ROWS)
        logits = jnp.dot(hidden_ref[here, :], head_ref[...], preferred_element_type=jnp.float32)
        logits = logits + head_bias_ref[...]
        tracks = jnp.maximum(logits, 0.0) + jnp.log1p(jnp.exp(-jnp.abs(logits)))
        out_ref[here, :] = tracks.astype(jnp.bfloat16)


def finish_kernel(flipped, count, x_ref, *refs):
    sources, refs = refs[:count], refs[count:]
    prev_ref, bias_ref, head_ref, head_bias_ref, out_ref, hidden_ref = refs
    for start in range(0, hidden_ref.shape[1], TILE):
        here = pl.ds(start, TILE)
        acc = convolve(x_ref[...], flipped, sources, here)
        hidden_ref[:, here] = gelu(acc + prev_ref[:, here] + bias_ref[:, here])
    predict(hidden_ref, head_ref, head_bias_ref, out_ref)


def finish(flipped, x, sources, prev, bias, head, head_bias):
    rows, depth = x.shape[0] - EDGE, x.shape[1]
    channels, tracks = head.shape
    inside = pl.BlockSpec(memory_space=pltpu.VMEM)
    return pl.pallas_call(
        functools.partial(finish_kernel, flipped, len(sources)),
        out_shape=jax.ShapeDtypeStruct((rows, tracks), jnp.bfloat16),
        in_specs=[inside] * (len(sources) + 5),
        out_specs=inside,
        scratch_shapes=[pltpu.VMEM((rows, channels), jnp.bfloat16)],
        compiler_params=pltpu.CompilerParams(vmem_limit_bytes=VMEM_LIMIT),
        cost_estimate=pl.CostEstimate(
            flops=2 * rows * channels * (3 * depth + tracks),
            bytes_accessed=6 * depth * channels + 2 * channels * tracks,
            transcendentals=rows * channels,
        ),
        name="finish",
    )(x, *sources, prev, bias, head, head_bias[None])


def whole_kernel(sizes, away_ref, *refs):
    moves, refs = refs[: len(sizes)], refs[len(sizes) :]
    sources, refs = refs[: sum(sizes)], refs[sum(sizes) :]
    bias_ref, head_ref, head_bias_ref, out_ref, hidden_ref = refs
    stripes = [
        jnp.dot(away_ref[...], move[...], preferred_element_type=jnp.float32).astype(jnp.bfloat16)
        for move in moves
    ]
    for start in range(0, hidden_ref.shape[1], TILE):
        here = pl.ds(start, TILE)
        acc, begin = bias_ref[:, here], 0
        for stripe, count in zip(stripes, sizes):
            acc = acc + convolve(stripe, True, sources[begin : begin + count], here)
            begin += count
        hidden_ref[:, here] = gelu(acc)
    predict(hidden_ref, head_ref, head_bias_ref, out_ref)


def whole(away, moves, sources, bias, head, head_bias):
    rows = away.shape[0] - EDGE
    channels, tracks = head.shape
    inside = pl.BlockSpec(memory_space=pltpu.VMEM)
    return pl.pallas_call(
        functools.partial(whole_kernel, SOURCES),
        out_shape=jax.ShapeDtypeStruct((rows, tracks), jnp.bfloat16),
        in_specs=[inside] * (len(moves) + len(sources) + 4),
        out_specs=inside,
        scratch_shapes=[pltpu.VMEM((rows, channels), jnp.bfloat16)],
        compiler_params=pltpu.CompilerParams(vmem_limit_bytes=VMEM_LIMIT),
        cost_estimate=pl.CostEstimate(
            flops=2 * rows * channels * (4 * channels + tracks),
            bytes_accessed=6 * channels * channels,
            transcendentals=rows * channels,
        ),
        name="whole",
    )(away, *moves, *sources, bias, head, head_bias[None])


def per_device(forward_embed, reverse_embed, conv_weight, conv_bias, head_weight, head_bias):
    own = conv_weight[0]
    x, y, core = lax.axis_index("x"), lax.axis_index("y_lo"), lax.axis_index("core")
    ends = XN * 2 * CN

    def seq(x_of, y_of, core_of):
        return (x_of % XN) * 4 + y_of * 2 + core_of

    step = 1 - 2 * core
    back, fore, far = x - step + XN, x + step + XN, x + 2
    other, over = 1 - core, 1 - y
    odd = lax.axis_index("z") % 2

    def both(*shards):
        return [2 * shard + half for shard in shards for half in range(2)]

    place = jnp.stack(
        both(
            seq(x, y, core), seq(x, y, other), seq(x, over, core), seq(x, over, other),
            seq(back, y, core), seq(fore, y, other),
            seq(back, over, core), seq(fore, over, other), seq(far, y, core), seq(far, y, other),
        )
        + [2 * seq(back, y, other) + odd, 2 * seq(fore, y, core) + odd]
        + [2 * seq(back, y, other) + 1 - odd, 2 * seq(fore, y, core) + 1 - odd]
        + both(
            seq(back, over, other), seq(fore, over, core),
            seq(far, over, core), seq(far, over, other),
        )
    ).astype(jnp.int32)

    with jax.named_scope("near"):
        near = x_shift(own)
    with jax.named_scope("across"):
        across = y_shift(own)
    with jax.named_scope("sibling"):
        sibling = core_swap(own)
    sibling_half = halve(place, sibling)
    with jax.named_scope("second"):
        second = x_shift(sibling_half)
    up = [(i, i + 1) for i in range(ends - 1)]
    down = [(b, a) for a, b in up]
    with jax.named_scope("low"):
        low = lax.ppermute(jnp.stack([forward_embed[-1], reverse_embed[-1]]), SEQ, up)
    with jax.named_scope("high"):
        high = lax.ppermute(jnp.stack([forward_embed[0], reverse_embed[0]]), SEQ, down)
    moves, flipped, token = order(place, reverse_embed)
    near, across, low, high = fence(token, near, across, low, high)

    with jax.named_scope("distant"):
        distant = x_shift(near)
    with jax.named_scope("near_over"):
        near_over = y_shift(near)
    with jax.named_scope("across_b"):
        across_b = core_swap(across)
    with jax.named_scope("near_b"):
        near_b = core_swap(near)
    (x_1, x_2, x_3), away, token = prepare(forward_embed, flipped, low, high, moves)
    shards_1 = [own, sibling, across, across_b, near, near_b]
    acc, token = partial_sum(x_1, shards_1, None)
    distant, near_over, across_b, second = fence(token, distant, near_over, across_b, second)
    shards_1[3] = across_b

    with jax.named_scope("second_z"):
        second_z = z_shift(second)
    with jax.named_scope("second_over"):
        second_over = x_shift(across_b)
    with jax.named_scope("distant_over"):
        distant_over = y_shift(distant)
    with jax.named_scope("near_over_b"):
        near_over_b = core_swap(near_over)
    with jax.named_scope("distant_b"):
        distant_b = core_swap(distant)
    with jax.named_scope("second_b"):
        second_b = core_swap(second)
    shards_2 = [near_over, near_over_b, distant, distant_b, second, second_b]
    acc, token = partial_sum(x_2, shards_2, acc)
    second_over, distant_over, second_z, away = fence(
        token, second_over, distant_over, second_z, away
    )

    mirror = [(i, ends - 1 - i) for i in range(ends)]
    with jax.named_scope("away"):
        away = lax.ppermute(away, SEQ, mirror)
    with jax.named_scope("second_over_b"):
        second_over_b = core_swap(second_over)
    with jax.named_scope("distant_over_b"):
        distant_over_b = core_swap(distant_over)
    with jax.named_scope("second_z_b"):
        second_z_b = core_swap(second_z)
    shards_3 = [second_z, second_z_b, second_over, second_over_b, distant_over, distant_over_b]
    rest = (conv_bias, head_weight, head_bias)
    reverse_tracks = finish(True, x_3[1], shards_3, acc[1], *rest)
    with jax.named_scope("mirrored"):
        mirrored = lax.ppermute(reverse_tracks, SEQ, mirror)
    forward_tracks = finish(False, x_3[0], shards_3, acc[0], *rest)
    away_tracks = whole(away, moves, shards_1 + shards_2 + shards_3, *rest)
    reverse = jnp.concatenate([mirrored, away_tracks])
    mean = 0.5 * (forward_tracks.astype(jnp.float32) + reverse.astype(jnp.float32))
    return mean.astype(jnp.bfloat16)


def solution(mesh):
    fine = Mesh(mesh.devices.reshape(2, 8, XN, 2, CN), AXES)
    return jax.shard_map(
        per_device,
        mesh=fine,
        in_specs=(
            P(AXES, None),
            P(AXES, None),
            P(None, None, SEQ, None),
            P(),
            P(),
            P(),
        ),
        out_specs=P(AXES, None),
        check_vma=False,
    )
```

```python
import functools

import jax
import jax.numpy as jnp
from jax import lax
from jax.experimental import pallas as pl
from jax.experimental.pallas import tpu as pltpu
from jax.sharding import Mesh
from jax.sharding import PartitionSpec as P

AXES = ("y_hi", "z", "x", "y_lo", "core")
SEQ = ("x", "y_lo", "core")
XN, YN, ZN, CN = 4, 4, 8, 2
VMEM_LIMIT = 24 * 1024 * 1024
EDGE = 16
TILE = 512
PARTS = (12, 10, 10)
SOURCES = (6, 6, 6)
PIECES = 32
FIRST_HALF = 20
ROWS = 128
AWAY = 128
TOKEN = jax.ShapeDtypeStruct((8, 128), jnp.float32)
INV_SQRT2 = 0.7071067811865476


def core_swap(value):
    return lax.ppermute(value, "core", [(0, 1), (1, 0)])


def x_shift(value):
    route = []
    for x in range(XN):
        route += [(x * 2, (x + 1) % XN * 2), (x * 2 + 1, (x - 1) % XN * 2 + 1)]
    return lax.ppermute(value, ("x", "core"), route)


def y_shift(value):
    route = []
    for y in range(YN):
        route += [(y * 2, (y + 1) % YN * 2), (y * 2 + 1, (y - 1) % YN * 2 + 1)]
    return lax.ppermute(value, ("y_hi", "y_lo", "core"), route)


def z_shift(value):
    route = []
    for z in range(ZN):
        route += [(z * 2, (z + 1) % ZN * 2), (z * 2 + 1, (z - 1) % ZN * 2 + 1)]
    return lax.ppermute(value, ("z", "core"), route)


def fence_kernel(count, *refs):
    for source, target in zip(refs[:count], refs[-count:]):
        target[...] = source[...]


def fence(token, *values):
    inside = pl.BlockSpec(memory_space=pltpu.VMEM)
    operands = values if token is None else (*values, token)
    return pl.pallas_call(
        functools.partial(fence_kernel, len(values)),
        out_shape=[jax.ShapeDtypeStruct(v.shape, v.dtype) for v in values],
        in_specs=[inside] * len(operands),
        out_specs=[inside] * len(values),
        input_output_aliases={i: i for i in range(len(values))},
        compiler_params=pltpu.CompilerParams(vmem_limit_bytes=8 * 1024 * 1024),
        name="fence",
    )(*operands)


def edge_tile(after, before):
    width = after.shape[1]
    edge = lax.broadcasted_iota(jnp.int32, (EDGE, width), 0)
    tile = jnp.where(edge == 0, after, jnp.where(edge == EDGE - 1, before, 0.0))
    return tile.astype(jnp.bfloat16)


def halve_kernel(place_ref, shard_ref, out_ref):
    half = out_ref.shape[1]
    odd = lax.rem(place_ref[FIRST_HALF], 2)

    @pl.when(odd == 0)
    def _():
        out_ref[...] = shard_ref[:, pl.ds(0, half), :]

    @pl.when(odd == 1)
    def _():
        out_ref[...] = shard_ref[:, pl.ds(half, half), :]


def halve(place, shard):
    taps, rows, columns = shard.shape
    inside = pl.BlockSpec(memory_space=pltpu.VMEM)
    return pl.pallas_call(
        halve_kernel,
        out_shape=jax.ShapeDtypeStruct((taps, rows // 2, columns), shard.dtype),
        in_specs=[pl.BlockSpec(memory_space=pltpu.SMEM), inside],
        out_specs=inside,
        compiler_params=pltpu.CompilerParams(vmem_limit_bytes=8 * 1024 * 1024),
        name="halve",
    )(place, shard)


def order_kernel(place_ref, reverse_ref, *refs):
    move_refs, flipped_ref, token_ref = refs[:3], refs[3], refs[4]
    token_ref[...] = jnp.zeros_like(token_ref)
    rows, width = reverse_ref.shape
    part = width // PIECES
    begin = 0
    for move_ref, count in zip(move_refs, PARTS):
        size = count * part
        lane = lax.broadcasted_iota(jnp.int32, (1, size), 1)
        wanted = jnp.zeros((1, size), jnp.int32)
        for block in range(count):
            inside = (lane >= block * part) & (lane < (block + 1) * part)
            wanted = jnp.where(inside, lane + (place_ref[begin + block] - block) * part, wanted)
        source = lax.broadcasted_iota(jnp.int32, (width, size), 0)
        move_ref[...] = jnp.where(source == wanted, 1.0, 0.0).astype(jnp.bfloat16)
        begin += count
    row = lax.broadcasted_iota(jnp.int32, (rows, rows), 0)
    column = lax.broadcasted_iota(jnp.int32, (rows, rows), 1)
    flip = jnp.where(row + column == rows - 1, 1.0, 0.0).astype(jnp.bfloat16)
    flipped = jnp.dot(flip, reverse_ref[...], preferred_element_type=jnp.float32)
    flipped_ref[...] = flipped.astype(jnp.bfloat16)


def order(place, reverse_embed):
    rows, width = reverse_embed.shape
    part = width // PIECES
    inside = pl.BlockSpec(memory_space=pltpu.VMEM)
    outs = pl.pallas_call(
        order_kernel,
        out_shape=[jax.ShapeDtypeStruct((width, count * part), jnp.bfloat16) for count in PARTS]
        + [jax.ShapeDtypeStruct((rows, width), jnp.bfloat16), TOKEN],
        in_specs=[pl.BlockSpec(memory_space=pltpu.SMEM), inside],
        out_specs=[inside] * 5,
        compiler_params=pltpu.CompilerParams(vmem_limit_bytes=VMEM_LIMIT),
        cost_estimate=pl.CostEstimate(
            flops=16 * rows * width * width, bytes_accessed=8 * rows * width, transcendentals=0
        ),
        name="order",
    )(place, reverse_embed)
    return outs[:3], outs[3], outs[4]


def edge_tile(after, before):
    width = after.shape[1]
    edge = lax.broadcasted_iota(jnp.int32, (EDGE, width), 0)
    tile = jnp.where(edge == 0, after, jnp.where(edge == EDGE - 1, before, 0.0))
    return tile.astype(jnp.bfloat16)


def prepare_kernel(forward_ref, flipped_ref, low_ref, high_ref, *refs):
    move_refs, x_refs, y_refs, (away_ref, token_ref, edge_ref) = (
        refs[:3], refs[3:6], refs[6:9], refs[9:],
    )
    token_ref[...] = jnp.zeros_like(token_ref)
    rows = forward_ref.shape[0]
    kept = rows - AWAY
    low = low_ref[...].astype(jnp.float32)
    high = high_ref[...].astype(jnp.float32)
    next_row = flipped_ref[pl.ds(kept, EDGE), :].astype(jnp.float32)[0:1]
    past_row = flipped_ref[pl.ds(kept - EDGE, EDGE), :].astype(jnp.float32)[EDGE - 1 :]
    away_ref[:AWAY, :] = flipped_ref[pl.ds(kept, AWAY), :]
    away_ref[AWAY:, :] = edge_tile(low[1:2], past_row)
    edge_ref[:EDGE, :] = edge_tile(high[0:1], low[0:1])
    edge_ref[EDGE:, :] = edge_tile(next_row, high[1:2])
    for x_ref, y_ref, move_ref in zip(x_refs, y_refs, move_refs):
        edges = jnp.dot(edge_ref[...], move_ref[...], preferred_element_type=jnp.float32)
        edges = edges.astype(jnp.bfloat16)
        x_ref[:rows, :] = jnp.dot(
            forward_ref[...], move_ref[...], preferred_element_type=jnp.float32
        ).astype(jnp.bfloat16)
        x_ref[rows:, :] = edges[:EDGE]
        y_ref[:kept, :] = jnp.dot(
            flipped_ref[pl.ds(0, kept), :], move_ref[...], preferred_element_type=jnp.float32
        ).astype(jnp.bfloat16)
        y_ref[kept:, :] = edges[EDGE:]


def prepare(forward_embed, flipped, low, high, moves):
    rows, width = forward_embed.shape
    kept = rows - AWAY
    part = width // PIECES
    inside = pl.BlockSpec(memory_space=pltpu.VMEM)

    def stripes(height):
        return [jax.ShapeDtypeStruct((height, count * part), jnp.bfloat16) for count in PARTS]

    outs = pl.pallas_call(
        prepare_kernel,
        out_shape=stripes(rows + EDGE)
        + stripes(kept + EDGE)
        + [jax.ShapeDtypeStruct((AWAY + EDGE, width), jnp.bfloat16), TOKEN],
        in_specs=[inside] * 7,
        out_specs=[inside] * 8,
        scratch_shapes=[pltpu.VMEM((2 * EDGE, width), jnp.bfloat16)],
        compiler_params=pltpu.CompilerParams(vmem_limit_bytes=VMEM_LIMIT),
        cost_estimate=pl.CostEstimate(flops=1000, bytes_accessed=1000, transcendentals=0),
        name="prepare",
    )(forward_embed, flipped, low, high, *moves)
    return list(zip(outs[:3], outs[3:6])), outs[6], outs[7]


def convolve(x, flipped, blocks, columns):
    rows = x.shape[0] - EDGE
    total = None
    for tap in range(3):
        weight = jnp.concatenate([block[tap, :, columns] for block in blocks], axis=0)
        value = jnp.dot(x, weight, preferred_element_type=jnp.float32)
        shift = tap - 1 if flipped else 1 - tap
        if shift:
            value = pltpu.roll(value, shift % (rows + EDGE), 0)
        value = value[:rows]
        total = value if total is None else total + value
    return total


def partial_kernel(count, first, *refs):
    strands, blocks, refs = refs[:2], refs[2 : 2 + count], refs[2 + count :]
    out_refs, token_ref = refs[-3:-1], refs[-1]
    token_ref[...] = jnp.zeros_like(token_ref)
    @pl.loop(0, out_refs[0].shape[1] // TILE)
    def _(tile):
        columns = pl.ds(pl.multiple_of(tile * TILE, TILE), TILE)
        for strand in range(2):
            acc = convolve(strands[strand][...], strand == 1, blocks, columns)
            if not first:
                acc = acc + refs[strand][:, columns]
            out_refs[strand][:, columns] = acc


def partial_sum(strands, sources, prev):
    rows = [x.shape[0] - EDGE for x in strands]
    depth, channels = strands[0].shape[1], sources[0].shape[2]
    operands = [*strands, *sources] + ([] if prev is None else list(prev))
    inside = pl.BlockSpec(memory_space=pltpu.VMEM)
    last = len(operands)
    forward, reverse, token = pl.pallas_call(
        functools.partial(partial_kernel, len(sources), prev is None),
        out_shape=[jax.ShapeDtypeStruct((count, channels), jnp.float32) for count in rows]
        + [TOKEN],
        in_specs=[inside] * last,
        out_specs=[inside] * 3,
        input_output_aliases={} if prev is None else {last - 2: 0, last - 1: 1},
        compiler_params=pltpu.CompilerParams(vmem_limit_bytes=VMEM_LIMIT),
        cost_estimate=pl.CostEstimate(
            flops=6 * sum(rows) * depth * channels,
            bytes_accessed=6 * depth * channels,
            transcendentals=0,
        ),
        name="partial_sum",
    )(*operands)
    return (forward, reverse), token


def gelu(acc):
    return (0.5 * acc * (1.0 + lax.erf(acc * INV_SQRT2))).astype(jnp.bfloat16)


def predict(hidden_ref, head_ref, head_bias_ref, out_ref):
    rows = out_ref.shape[0]
    @pl.loop(0, rows // ROWS)
    def _(block):
        here = pl.ds(pl.multiple_of(block * ROWS, ROWS), ROWS)
        logits = jnp.dot(hidden_ref[here, :], head_ref[...], preferred_element_type=jnp.float32)
        logits = logits + head_bias_ref[...]
        tracks = jnp.maximum(logits, 0.0) + jnp.log1p(jnp.exp(-jnp.abs(logits)))
        out_ref[here, :] = tracks.astype(jnp.bfloat16)


def finish_kernel(flipped, count, x_ref, *refs):
    sources, refs = refs[:count], refs[count:]
    prev_ref, bias_ref, head_ref, head_bias_ref, out_ref, hidden_ref = refs
    @pl.loop(0, hidden_ref.shape[1] // TILE)
    def _(tile):
        here = pl.ds(pl.multiple_of(tile * TILE, TILE), TILE)
        acc = convolve(x_ref[...], flipped, sources, here)
        hidden_ref[:, here] = gelu(acc + prev_ref[:, here] + bias_ref[:, here])

    predict(hidden_ref, head_ref, head_bias_ref, out_ref)


def finish(flipped, x, sources, prev, bias, head, head_bias):
    rows, depth = x.shape[0] - EDGE, x.shape[1]
    channels, tracks = head.shape
    inside = pl.BlockSpec(memory_space=pltpu.VMEM)
    return pl.pallas_call(
        functools.partial(finish_kernel, flipped, len(sources)),
        out_shape=jax.ShapeDtypeStruct((rows, tracks), jnp.bfloat16),
        in_specs=[inside] * (len(sources) + 5),
        out_specs=inside,
        scratch_shapes=[pltpu.VMEM((rows, channels), jnp.bfloat16)],
        compiler_params=pltpu.CompilerParams(vmem_limit_bytes=VMEM_LIMIT),
        cost_estimate=pl.CostEstimate(
            flops=2 * rows * channels * (3 * depth + tracks),
            bytes_accessed=6 * depth * channels + 2 * channels * tracks,
            transcendentals=rows * channels,
        ),
        name="finish",
    )(x, *sources, prev, bias, head, head_bias[None])


def whole_kernel(sizes, away_ref, *refs):
    moves, refs = refs[: len(sizes)], refs[len(sizes) :]
    sources, refs = refs[: sum(sizes)], refs[sum(sizes) :]
    bias_ref, head_ref, head_bias_ref, out_ref, hidden_ref = refs
    stripes = [
        jnp.dot(away_ref[...], move[...], preferred_element_type=jnp.float32).astype(jnp.bfloat16)
        for move in moves
    ]
    @pl.loop(0, hidden_ref.shape[1] // TILE)
    def _(tile):
        here = pl.ds(pl.multiple_of(tile * TILE, TILE), TILE)
        acc, begin = bias_ref[:, here], 0
        for stripe, count in zip(stripes, sizes):
            acc = acc + convolve(stripe, True, sources[begin : begin + count], here)
            begin += count
        hidden_ref[:, here] = gelu(acc)

    predict(hidden_ref, head_ref, head_bias_ref, out_ref)


def whole(away, moves, sources, bias, head, head_bias):
    rows = away.shape[0] - EDGE
    channels, tracks = head.shape
    inside = pl.BlockSpec(memory_space=pltpu.VMEM)
    return pl.pallas_call(
        functools.partial(whole_kernel, SOURCES),
        out_shape=jax.ShapeDtypeStruct((rows, tracks), jnp.bfloat16),
        in_specs=[inside] * (len(moves) + len(sources) + 4),
        out_specs=inside,
        scratch_shapes=[pltpu.VMEM((rows, channels), jnp.bfloat16)],
        compiler_params=pltpu.CompilerParams(vmem_limit_bytes=VMEM_LIMIT),
        cost_estimate=pl.CostEstimate(
            flops=2 * rows * channels * (4 * channels + tracks),
            bytes_accessed=6 * channels * channels,
            transcendentals=rows * channels,
        ),
        name="whole",
    )(away, *moves, *sources, bias, head, head_bias[None])


def per_device(forward_embed, reverse_embed, conv_weight, conv_bias, head_weight, head_bias):
    own = conv_weight[0]
    x, y, core = lax.axis_index("x"), lax.axis_index("y_lo"), lax.axis_index("core")
    ends = XN * 2 * CN

    def seq(x_of, y_of, core_of):
        return (x_of % XN) * 4 + y_of * 2 + core_of

    step = 1 - 2 * core
    back, fore, far = x - step + XN, x + step + XN, x + 2
    other, over = 1 - core, 1 - y
    odd = lax.axis_index("z") % 2

    def both(*shards):
        return [2 * shard + half for shard in shards for half in range(2)]

    place = jnp.stack(
        both(
            seq(x, y, core), seq(x, y, other), seq(x, over, core), seq(x, over, other),
            seq(back, y, core), seq(fore, y, other),
            seq(back, over, core), seq(fore, over, other), seq(far, y, core), seq(far, y, other),
        )
        + [2 * seq(back, y, other) + odd, 2 * seq(fore, y, core) + odd]
        + [2 * seq(back, y, other) + 1 - odd, 2 * seq(fore, y, core) + 1 - odd]
        + both(
            seq(back, over, other), seq(fore, over, core),
            seq(far, over, core), seq(far, over, other),
        )
    ).astype(jnp.int32)

    with jax.named_scope("near"):
        near = x_shift(own)
    with jax.named_scope("across"):
        across = y_shift(own)
    with jax.named_scope("sibling"):
        sibling = core_swap(own)
    sibling_half = halve(place, sibling)
    with jax.named_scope("second"):
        second = x_shift(sibling_half)
    up = [(i, i + 1) for i in range(ends - 1)]
    down = [(b, a) for a, b in up]
    with jax.named_scope("low"):
        low = lax.ppermute(jnp.stack([forward_embed[-1], reverse_embed[-1]]), SEQ, up)
    with jax.named_scope("high"):
        high = lax.ppermute(jnp.stack([forward_embed[0], reverse_embed[0]]), SEQ, down)
    moves, flipped, token = order(place, reverse_embed)
    near, across, low, high = fence(token, near, across, low, high)

    with jax.named_scope("distant"):
        distant = x_shift(near)
    with jax.named_scope("near_over"):
        near_over = y_shift(near)
    with jax.named_scope("across_b"):
        across_b = core_swap(across)
    with jax.named_scope("near_b"):
        near_b = core_swap(near)
    (x_1, x_2, x_3), away, token = prepare(forward_embed, flipped, low, high, moves)
    shards_1 = [own, sibling, across, across_b, near, near_b]
    acc, token = partial_sum(x_1, shards_1, None)
    distant, near_over, across_b, second = fence(token, distant, near_over, across_b, second)
    shards_1[3] = across_b

    with jax.named_scope("second_z"):
        second_z = z_shift(second)
    with jax.named_scope("second_over"):
        second_over = x_shift(across_b)
    with jax.named_scope("distant_over"):
        distant_over = y_shift(distant)
    with jax.named_scope("near_over_b"):
        near_over_b = core_swap(near_over)
    with jax.named_scope("distant_b"):
        distant_b = core_swap(distant)
    with jax.named_scope("second_b"):
        second_b = core_swap(second)
    shards_2 = [near_over, near_over_b, distant, distant_b, second, second_b]
    acc, token = partial_sum(x_2, shards_2, acc)
    second_over, distant_over, second_z, away = fence(
        token, second_over, distant_over, second_z, away
    )

    mirror = [(i, ends - 1 - i) for i in range(ends)]
    with jax.named_scope("away"):
        away = lax.ppermute(away, SEQ, mirror)
    with jax.named_scope("second_over_b"):
        second_over_b = core_swap(second_over)
    with jax.named_scope("distant_over_b"):
        distant_over_b = core_swap(distant_over)
    with jax.named_scope("second_z_b"):
        second_z_b = core_swap(second_z)
    shards_3 = [second_z, second_z_b, second_over, second_over_b, distant_over, distant_over_b]
    rest = (conv_bias, head_weight, head_bias)
    reverse_tracks = finish(True, x_3[1], shards_3, acc[1], *rest)
    with jax.named_scope("mirrored"):
        mirrored = lax.ppermute(reverse_tracks, SEQ, mirror)
    forward_tracks = finish(False, x_3[0], shards_3, acc[0], *rest)
    away_tracks = whole(away, moves, shards_1 + shards_2 + shards_3, *rest)
    reverse = jnp.concatenate([mirrored, away_tracks])
    mean = 0.5 * (forward_tracks.astype(jnp.float32) + reverse.astype(jnp.float32))
    return mean.astype(jnp.bfloat16)


def solution(mesh):
    fine = Mesh(mesh.devices.reshape(2, 8, XN, 2, CN), AXES)
    return jax.shard_map(
        per_device,
        mesh=fine,
        in_specs=(
            P(AXES, None),
            P(AXES, None),
            P(None, None, SEQ, None),
            P(),
            P(),
            P(),
        ),
        out_specs=P(AXES, None),
        check_vma=False,
    )
```

```python
import functools

import jax
import jax.numpy as jnp
from jax import lax
from jax.experimental import pallas as pl
from jax.experimental.pallas import tpu as pltpu
from jax.sharding import Mesh
from jax.sharding import PartitionSpec as P

AXES = ("y_hi", "z", "x", "y_lo", "core")
SEQ = ("x", "y_lo", "core")
XN, YN, ZN, CN = 4, 4, 8, 2
VMEM_LIMIT = 24 * 1024 * 1024
EDGE = 16
TILE = 512
PARTS = (12, 8, 12)
SOURCES = (6, 4, 8)
PIECES = 32
FIRST_HALF = 20
ROWS = 128
AWAY = 128
TOKEN = jax.ShapeDtypeStruct((8, 128), jnp.float32)
INV_SQRT2 = 0.7071067811865476


def core_swap(value):
    return lax.ppermute(value, "core", [(0, 1), (1, 0)])


def x_shift(value):
    route = []
    for x in range(XN):
        route += [(x * 2, (x + 1) % XN * 2), (x * 2 + 1, (x - 1) % XN * 2 + 1)]
    return lax.ppermute(value, ("x", "core"), route)


def y_shift(value):
    route = []
    for y in range(YN):
        route += [(y * 2, (y + 1) % YN * 2), (y * 2 + 1, (y - 1) % YN * 2 + 1)]
    return lax.ppermute(value, ("y_hi", "y_lo", "core"), route)


def z_shift(value):
    route = []
    for z in range(ZN):
        route += [(z * 2, (z + 1) % ZN * 2), (z * 2 + 1, (z - 1) % ZN * 2 + 1)]
    return lax.ppermute(value, ("z", "core"), route)


def fence_kernel(count, *refs):
    for source, target in zip(refs[:count], refs[-count:]):
        target[...] = source[...]


def fence(token, *values):
    inside = pl.BlockSpec(memory_space=pltpu.VMEM)
    operands = values if token is None else (*values, token)
    return pl.pallas_call(
        functools.partial(fence_kernel, len(values)),
        out_shape=[jax.ShapeDtypeStruct(v.shape, v.dtype) for v in values],
        in_specs=[inside] * len(operands),
        out_specs=[inside] * len(values),
        input_output_aliases={i: i for i in range(len(values))},
        compiler_params=pltpu.CompilerParams(vmem_limit_bytes=8 * 1024 * 1024),
        name="fence",
    )(*operands)


def edge_tile(after, before):
    width = after.shape[1]
    edge = lax.broadcasted_iota(jnp.int32, (EDGE, width), 0)
    tile = jnp.where(edge == 0, after, jnp.where(edge == EDGE - 1, before, 0.0))
    return tile.astype(jnp.bfloat16)


def after_kernel(source_ref, token_ref, out_ref):
    out_ref[...] = source_ref[...]


def after(token, value):
    inside = pl.BlockSpec(memory_space=pltpu.VMEM)
    return pl.pallas_call(
        after_kernel,
        out_shape=jax.ShapeDtypeStruct(value.shape, value.dtype),
        in_specs=[inside] * 2,
        out_specs=inside,
        compiler_params=pltpu.CompilerParams(vmem_limit_bytes=8 * 1024 * 1024),
        name="after",
    )(value, token)


def halve_kernel(place_ref, shard_ref, out_ref):
    half = out_ref.shape[1]
    odd = lax.rem(place_ref[FIRST_HALF], 2)

    @pl.when(odd == 0)
    def _():
        out_ref[...] = shard_ref[:, pl.ds(0, half), :]

    @pl.when(odd == 1)
    def _():
        out_ref[...] = shard_ref[:, pl.ds(half, half), :]


def halve(place, shard):
    taps, rows, columns = shard.shape
    inside = pl.BlockSpec(memory_space=pltpu.VMEM)
    return pl.pallas_call(
        halve_kernel,
        out_shape=jax.ShapeDtypeStruct((taps, rows // 2, columns), shard.dtype),
        in_specs=[pl.BlockSpec(memory_space=pltpu.SMEM), inside],
        out_specs=inside,
        compiler_params=pltpu.CompilerParams(vmem_limit_bytes=8 * 1024 * 1024),
        name="halve",
    )(place, shard)


def order_kernel(place_ref, reverse_ref, *refs):
    move_refs, flipped_ref, token_ref = refs[:3], refs[3], refs[4]
    token_ref[...] = jnp.zeros_like(token_ref)
    rows, width = reverse_ref.shape
    part = width // PIECES
    begin = 0
    for move_ref, count in zip(move_refs, PARTS):
        size = count * part
        lane = lax.broadcasted_iota(jnp.int32, (1, size), 1)
        wanted = jnp.zeros((1, size), jnp.int32)
        for block in range(count):
            inside = (lane >= block * part) & (lane < (block + 1) * part)
            wanted = jnp.where(inside, lane + (place_ref[begin + block] - block) * part, wanted)
        source = lax.broadcasted_iota(jnp.int32, (width, size), 0)
        move_ref[...] = jnp.where(source == wanted, 1.0, 0.0).astype(jnp.bfloat16)
        begin += count
    row = lax.broadcasted_iota(jnp.int32, (rows, rows), 0)
    column = lax.broadcasted_iota(jnp.int32, (rows, rows), 1)
    flip = jnp.where(row + column == rows - 1, 1.0, 0.0).astype(jnp.bfloat16)
    flipped = jnp.dot(flip, reverse_ref[...], preferred_element_type=jnp.float32)
    flipped_ref[...] = flipped.astype(jnp.bfloat16)


def order(place, reverse_embed):
    rows, width = reverse_embed.shape
    part = width // PIECES
    inside = pl.BlockSpec(memory_space=pltpu.VMEM)
    outs = pl.pallas_call(
        order_kernel,
        out_shape=[jax.ShapeDtypeStruct((width, count * part), jnp.bfloat16) for count in PARTS]
        + [jax.ShapeDtypeStruct((rows, width), jnp.bfloat16), TOKEN],
        in_specs=[pl.BlockSpec(memory_space=pltpu.SMEM), inside],
        out_specs=[inside] * 5,
        compiler_params=pltpu.CompilerParams(vmem_limit_bytes=VMEM_LIMIT),
        cost_estimate=pl.CostEstimate(
            flops=16 * rows * width * width, bytes_accessed=8 * rows * width, transcendentals=0
        ),
        name="order",
    )(place, reverse_embed)
    return outs[:3], outs[3], outs[4]


def edge_tile(after, before):
    width = after.shape[1]
    edge = lax.broadcasted_iota(jnp.int32, (EDGE, width), 0)
    tile = jnp.where(edge == 0, after, jnp.where(edge == EDGE - 1, before, 0.0))
    return tile.astype(jnp.bfloat16)


def prepare_kernel(forward_ref, flipped_ref, low_ref, high_ref, *refs):
    move_refs, x_refs, y_refs, (away_ref, token_ref, edge_ref) = (
        refs[:3], refs[3:6], refs[6:9], refs[9:],
    )
    token_ref[...] = jnp.zeros_like(token_ref)
    rows = forward_ref.shape[0]
    kept = rows - AWAY
    low = low_ref[...].astype(jnp.float32)
    high = high_ref[...].astype(jnp.float32)
    next_row = flipped_ref[pl.ds(kept, EDGE), :].astype(jnp.float32)[0:1]
    past_row = flipped_ref[pl.ds(kept - EDGE, EDGE), :].astype(jnp.float32)[EDGE - 1 :]
    away_ref[:AWAY, :] = flipped_ref[pl.ds(kept, AWAY), :]
    away_ref[AWAY:, :] = edge_tile(low[1:2], past_row)
    edge_ref[:EDGE, :] = edge_tile(high[0:1], low[0:1])
    edge_ref[EDGE:, :] = edge_tile(next_row, high[1:2])
    for x_ref, y_ref, move_ref in zip(x_refs, y_refs, move_refs):
        edges = jnp.dot(edge_ref[...], move_ref[...], preferred_element_type=jnp.float32)
        edges = edges.astype(jnp.bfloat16)
        x_ref[:rows, :] = jnp.dot(
            forward_ref[...], move_ref[...], preferred_element_type=jnp.float32
        ).astype(jnp.bfloat16)
        x_ref[rows:, :] = edges[:EDGE]
        y_ref[:kept, :] = jnp.dot(
            flipped_ref[pl.ds(0, kept), :], move_ref[...], preferred_element_type=jnp.float32
        ).astype(jnp.bfloat16)
        y_ref[kept:, :] = edges[EDGE:]


def prepare(forward_embed, flipped, low, high, moves):
    rows, width = forward_embed.shape
    kept = rows - AWAY
    part = width // PIECES
    inside = pl.BlockSpec(memory_space=pltpu.VMEM)

    def stripes(height):
        return [jax.ShapeDtypeStruct((height, count * part), jnp.bfloat16) for count in PARTS]

    outs = pl.pallas_call(
        prepare_kernel,
        out_shape=stripes(rows + EDGE)
        + stripes(kept + EDGE)
        + [jax.ShapeDtypeStruct((AWAY + EDGE, width), jnp.bfloat16), TOKEN],
        in_specs=[inside] * 7,
        out_specs=[inside] * 8,
        scratch_shapes=[pltpu.VMEM((2 * EDGE, width), jnp.bfloat16)],
        compiler_params=pltpu.CompilerParams(vmem_limit_bytes=VMEM_LIMIT),
        cost_estimate=pl.CostEstimate(flops=1000, bytes_accessed=1000, transcendentals=0),
        name="prepare",
    )(forward_embed, flipped, low, high, *moves)
    return list(zip(outs[:3], outs[3:6])), outs[6], outs[7]


def convolve(x, flipped, blocks, columns):
    rows = x.shape[0] - EDGE
    total = None
    for tap in range(3):
        weight = jnp.concatenate([block[tap, :, columns] for block in blocks], axis=0)
        value = jnp.dot(x, weight, preferred_element_type=jnp.float32)
        shift = tap - 1 if flipped else 1 - tap
        if shift:
            value = pltpu.roll(value, shift % (rows + EDGE), 0)
        value = value[:rows]
        total = value if total is None else total + value
    return total


def partial_kernel(count, first, *refs):
    strands, blocks, refs = refs[:2], refs[2 : 2 + count], refs[2 + count :]
    out_refs, token_ref = refs[-3:-1], refs[-1]
    token_ref[...] = jnp.zeros_like(token_ref)
    @pl.loop(0, out_refs[0].shape[1] // TILE)
    def _(tile):
        columns = pl.ds(pl.multiple_of(tile * TILE, TILE), TILE)
        for strand in range(2):
            acc = convolve(strands[strand][...], strand == 1, blocks, columns)
            if not first:
                acc = acc + refs[strand][:, columns]
            out_refs[strand][:, columns] = acc


def partial_sum(strands, sources, prev):
    rows = [x.shape[0] - EDGE for x in strands]
    depth, channels = strands[0].shape[1], sources[0].shape[2]
    operands = [*strands, *sources] + ([] if prev is None else list(prev))
    inside = pl.BlockSpec(memory_space=pltpu.VMEM)
    last = len(operands)
    forward, reverse, token = pl.pallas_call(
        functools.partial(partial_kernel, len(sources), prev is None),
        out_shape=[jax.ShapeDtypeStruct((count, channels), jnp.float32) for count in rows]
        + [TOKEN],
        in_specs=[inside] * last,
        out_specs=[inside] * 3,
        input_output_aliases={} if prev is None else {last - 2: 0, last - 1: 1},
        compiler_params=pltpu.CompilerParams(vmem_limit_bytes=VMEM_LIMIT),
        cost_estimate=pl.CostEstimate(
            flops=6 * sum(rows) * depth * channels,
            bytes_accessed=6 * depth * channels,
            transcendentals=0,
        ),
        name="partial_sum",
    )(*operands)
    return (forward, reverse), token


def gelu(acc):
    return (0.5 * acc * (1.0 + lax.erf(acc * INV_SQRT2))).astype(jnp.bfloat16)


def predict(hidden_ref, head_ref, head_bias_ref, out_ref):
    rows = out_ref.shape[0]
    @pl.loop(0, rows // ROWS, unroll=True)
    def _(block):
        here = pl.ds(pl.multiple_of(block * ROWS, ROWS), ROWS)
        logits = jnp.dot(hidden_ref[here, :], head_ref[...], preferred_element_type=jnp.float32)
        logits = logits + head_bias_ref[...]
        tracks = jnp.maximum(logits, 0.0) + jnp.log1p(jnp.exp(-jnp.abs(logits)))
        out_ref[here, :] = tracks.astype(jnp.bfloat16)


def finish_kernel(flipped, count, x_ref, *refs):
    sources, refs = refs[:count], refs[count:]
    prev_ref, bias_ref, head_ref, head_bias_ref, out_ref, hidden_ref = refs
    @pl.loop(0, hidden_ref.shape[1] // TILE, unroll=True)
    def _(tile):
        here = pl.ds(pl.multiple_of(tile * TILE, TILE), TILE)
        acc = convolve(x_ref[...], flipped, sources, here)
        hidden_ref[:, here] = gelu(acc + prev_ref[:, here] + bias_ref[:, here])

    predict(hidden_ref, head_ref, head_bias_ref, out_ref)


def finish(flipped, x, sources, prev, bias, head, head_bias):
    rows, depth = x.shape[0] - EDGE, x.shape[1]
    channels, tracks = head.shape
    inside = pl.BlockSpec(memory_space=pltpu.VMEM)
    return pl.pallas_call(
        functools.partial(finish_kernel, flipped, len(sources)),
        out_shape=jax.ShapeDtypeStruct((rows, tracks), jnp.bfloat16),
        in_specs=[inside] * (len(sources) + 5),
        out_specs=inside,
        scratch_shapes=[pltpu.VMEM((rows, channels), jnp.bfloat16)],
        compiler_params=pltpu.CompilerParams(vmem_limit_bytes=VMEM_LIMIT),
        cost_estimate=pl.CostEstimate(
            flops=2 * rows * channels * (3 * depth + tracks),
            bytes_accessed=6 * depth * channels + 2 * channels * tracks,
            transcendentals=rows * channels,
        ),
        name="finish",
    )(x, *sources, prev, bias, head, head_bias[None])


def whole_kernel(sizes, away_ref, *refs):
    moves, refs = refs[: len(sizes)], refs[len(sizes) :]
    sources, refs = refs[: sum(sizes)], refs[sum(sizes) :]
    bias_ref, head_ref, head_bias_ref, out_ref, hidden_ref = refs
    stripes = [
        jnp.dot(away_ref[...], move[...], preferred_element_type=jnp.float32).astype(jnp.bfloat16)
        for move in moves
    ]
    @pl.loop(0, hidden_ref.shape[1] // TILE)
    def _(tile):
        here = pl.ds(pl.multiple_of(tile * TILE, TILE), TILE)
        acc, begin = bias_ref[:, here], 0
        for stripe, count in zip(stripes, sizes):
            acc = acc + convolve(stripe, True, sources[begin : begin + count], here)
            begin += count
        hidden_ref[:, here] = gelu(acc)

    predict(hidden_ref, head_ref, head_bias_ref, out_ref)


def whole(away, moves, sources, bias, head, head_bias):
    rows = away.shape[0] - EDGE
    channels, tracks = head.shape
    inside = pl.BlockSpec(memory_space=pltpu.VMEM)
    return pl.pallas_call(
        functools.partial(whole_kernel, SOURCES),
        out_shape=jax.ShapeDtypeStruct((rows, tracks), jnp.bfloat16),
        in_specs=[inside] * (len(moves) + len(sources) + 4),
        out_specs=inside,
        scratch_shapes=[pltpu.VMEM((rows, channels), jnp.bfloat16)],
        compiler_params=pltpu.CompilerParams(vmem_limit_bytes=VMEM_LIMIT),
        cost_estimate=pl.CostEstimate(
            flops=2 * rows * channels * (4 * channels + tracks),
            bytes_accessed=6 * channels * channels,
            transcendentals=rows * channels,
        ),
        name="whole",
    )(away, *moves, *sources, bias, head, head_bias[None])


def per_device(forward_embed, reverse_embed, conv_weight, conv_bias, head_weight, head_bias):
    own = conv_weight[0]
    x, y, core = lax.axis_index("x"), lax.axis_index("y_lo"), lax.axis_index("core")
    ends = XN * 2 * CN

    def seq(x_of, y_of, core_of):
        return (x_of % XN) * 4 + y_of * 2 + core_of

    step = 1 - 2 * core
    back, fore, far = x - step + XN, x + step + XN, x + 2
    other, over = 1 - core, 1 - y
    odd = lax.axis_index("z") % 2

    def both(*shards):
        return [2 * shard + half for shard in shards for half in range(2)]

    place = jnp.stack(
        both(
            seq(x, y, core), seq(x, y, other), seq(x, over, core), seq(x, over, other),
            seq(back, y, core), seq(fore, y, other),
            seq(back, over, core), seq(fore, over, other), seq(far, y, core), seq(far, y, other),
        )
        + [2 * seq(back, y, other) + odd, 2 * seq(fore, y, core) + odd]
        + [2 * seq(back, y, other) + 1 - odd, 2 * seq(fore, y, core) + 1 - odd]
        + both(
            seq(back, over, other), seq(fore, over, core),
            seq(far, over, core), seq(far, over, other),
        )
    ).astype(jnp.int32)

    with jax.named_scope("near"):
        near = x_shift(own)
    with jax.named_scope("across"):
        across = y_shift(own)
    with jax.named_scope("sibling"):
        sibling = core_swap(own)
    sibling_half = halve(place, sibling)
    with jax.named_scope("second"):
        second = x_shift(sibling_half)
    up = [(i, i + 1) for i in range(ends - 1)]
    down = [(b, a) for a, b in up]
    with jax.named_scope("low"):
        low = lax.ppermute(jnp.stack([forward_embed[-1], reverse_embed[-1]]), SEQ, up)
    with jax.named_scope("high"):
        high = lax.ppermute(jnp.stack([forward_embed[0], reverse_embed[0]]), SEQ, down)
    moves, flipped, token = order(place, reverse_embed)
    near, across, low, high = fence(token, near, across, low, high)

    with jax.named_scope("distant"):
        distant = x_shift(near)
    with jax.named_scope("near_over"):
        near_over = y_shift(near)
    with jax.named_scope("across_b"):
        across_b = core_swap(across)
    with jax.named_scope("near_b"):
        near_b = core_swap(near)
    (x_1, x_2, x_3), away, token = prepare(forward_embed, flipped, low, high, moves)
    shards_1 = [own, sibling, across, across_b, near, near_b]
    acc, token = partial_sum(x_1, shards_1, None)
    distant, near_over, across_b, second = fence(token, distant, near_over, across_b, second)
    shards_1[3] = across_b

    with jax.named_scope("second_z"):
        second_z = z_shift(second)
    with jax.named_scope("second_over"):
        second_over = x_shift(across_b)
    with jax.named_scope("distant_over"):
        distant_over = y_shift(distant)
    with jax.named_scope("near_over_b"):
        near_over_b = core_swap(near_over)
    with jax.named_scope("distant_b"):
        distant_b = core_swap(distant)
    shards_2 = [near_over, near_over_b, distant, distant_b]
    acc, token = partial_sum(x_2, shards_2, acc)
    with jax.named_scope("second_b"):
        second_b = core_swap(after(token, second))
    second_over, distant_over, second_z, second_b, away = fence(
        token, second_over, distant_over, second_z, second_b, away
    )

    mirror = [(i, ends - 1 - i) for i in range(ends)]
    with jax.named_scope("away"):
        away = lax.ppermute(away, SEQ, mirror)
    with jax.named_scope("second_over_b"):
        second_over_b = core_swap(second_over)
    with jax.named_scope("distant_over_b"):
        distant_over_b = core_swap(distant_over)
    with jax.named_scope("second_z_b"):
        second_z_b = core_swap(second_z)
    shards_3 = [second, second_b, second_z, second_z_b, second_over, second_over_b, distant_over, distant_over_b]
    rest = (conv_bias, head_weight, head_bias)
    reverse_tracks = finish(True, x_3[1], shards_3, acc[1], *rest)
    with jax.named_scope("mirrored"):
        mirrored = lax.ppermute(reverse_tracks, SEQ, mirror)
    forward_tracks = finish(False, x_3[0], shards_3, acc[0], *rest)
    away_tracks = whole(away, moves, shards_1 + shards_2 + shards_3, *rest)
    reverse = jnp.concatenate([mirrored, away_tracks])
    mean = 0.5 * (forward_tracks.astype(jnp.float32) + reverse.astype(jnp.float32))
    return mean.astype(jnp.bfloat16)


def solution(mesh):
    fine = Mesh(mesh.devices.reshape(2, 8, XN, 2, CN), AXES)
    return jax.shard_map(
        per_device,
        mesh=fine,
        in_specs=(
            P(AXES, None),
            P(AXES, None),
            P(None, None, SEQ, None),
            P(),
            P(),
            P(),
        ),
        out_specs=P(AXES, None),
        check_vma=False,
    )
```

```python
import functools

import jax
import jax.numpy as jnp
from jax import lax
from jax.experimental import pallas as pl
from jax.experimental.pallas import tpu as pltpu
from jax.sharding import Mesh
from jax.sharding import PartitionSpec as P

AXES = ("y_hi", "z", "x", "y_lo", "core")
SEQ = ("x", "y_lo", "core")
XN, YN, ZN, CN = 4, 4, 8, 2
VMEM_LIMIT = 24 * 1024 * 1024
EDGE = 16
TILE = 512
PARTS = (12, 8, 12)
SOURCES = (6, 4, 8)
PIECES = 32
FIRST_HALF = 20
ROWS = 128
AWAY = 128
TOKEN = jax.ShapeDtypeStruct((8, 128), jnp.float32)
INV_SQRT2 = 0.7071067811865476


def core_swap(value):
    return lax.ppermute(value, "core", [(0, 1), (1, 0)])


def x_shift(value):
    route = []
    for x in range(XN):
        route += [(x * 2, (x + 1) % XN * 2), (x * 2 + 1, (x - 1) % XN * 2 + 1)]
    return lax.ppermute(value, ("x", "core"), route)


def y_shift(value):
    route = []
    for y in range(YN):
        route += [(y * 2, (y + 1) % YN * 2), (y * 2 + 1, (y - 1) % YN * 2 + 1)]
    return lax.ppermute(value, ("y_hi", "y_lo", "core"), route)


def z_shift(value):
    route = []
    for z in range(ZN):
        route += [(z * 2, (z + 1) % ZN * 2), (z * 2 + 1, (z - 1) % ZN * 2 + 1)]
    return lax.ppermute(value, ("z", "core"), route)


def fence_kernel(count, *refs):
    for source, target in zip(refs[:count], refs[-count:]):
        target[...] = source[...]


def fence(token, *values):
    inside = pl.BlockSpec(memory_space=pltpu.VMEM)
    operands = values if token is None else (*values, token)
    return pl.pallas_call(
        functools.partial(fence_kernel, len(values)),
        out_shape=[jax.ShapeDtypeStruct(v.shape, v.dtype) for v in values],
        in_specs=[inside] * len(operands),
        out_specs=[inside] * len(values),
        input_output_aliases={i: i for i in range(len(values))},
        compiler_params=pltpu.CompilerParams(vmem_limit_bytes=8 * 1024 * 1024),
        name="fence",
    )(*operands)


def edge_tile(after, before):
    width = after.shape[1]
    edge = lax.broadcasted_iota(jnp.int32, (EDGE, width), 0)
    tile = jnp.where(edge == 0, after, jnp.where(edge == EDGE - 1, before, 0.0))
    return tile.astype(jnp.bfloat16)


def after_kernel(source_ref, token_ref, out_ref):
    out_ref[...] = source_ref[...]


def after(token, value):
    inside = pl.BlockSpec(memory_space=pltpu.VMEM)
    return pl.pallas_call(
        after_kernel,
        out_shape=jax.ShapeDtypeStruct(value.shape, value.dtype),
        in_specs=[inside] * 2,
        out_specs=inside,
        compiler_params=pltpu.CompilerParams(vmem_limit_bytes=8 * 1024 * 1024),
        name="after",
    )(value, token)


def halve_kernel(place_ref, shard_ref, out_ref):
    half = out_ref.shape[1]
    odd = lax.rem(place_ref[FIRST_HALF], 2)

    @pl.when(odd == 0)
    def _():
        out_ref[...] = shard_ref[:, pl.ds(0, half), :]

    @pl.when(odd == 1)
    def _():
        out_ref[...] = shard_ref[:, pl.ds(half, half), :]


def halve(place, shard):
    taps, rows, columns = shard.shape
    inside = pl.BlockSpec(memory_space=pltpu.VMEM)
    return pl.pallas_call(
        halve_kernel,
        out_shape=jax.ShapeDtypeStruct((taps, rows // 2, columns), shard.dtype),
        in_specs=[pl.BlockSpec(memory_space=pltpu.SMEM), inside],
        out_specs=inside,
        compiler_params=pltpu.CompilerParams(vmem_limit_bytes=8 * 1024 * 1024),
        name="halve",
    )(place, shard)


def order_kernel(place_ref, reverse_ref, *refs):
    move_refs, flipped_ref, token_ref = refs[:3], refs[3], refs[4]
    token_ref[...] = jnp.zeros_like(token_ref)
    rows, width = reverse_ref.shape
    part = width // PIECES
    begin = 0
    for move_ref, count in zip(move_refs, PARTS):
        size = count * part
        lane = lax.broadcasted_iota(jnp.int32, (1, size), 1)
        wanted = jnp.zeros((1, size), jnp.int32)
        for block in range(count):
            inside = (lane >= block * part) & (lane < (block + 1) * part)
            wanted = jnp.where(inside, lane + (place_ref[begin + block] - block) * part, wanted)
        source = lax.broadcasted_iota(jnp.int32, (width, size), 0)
        move_ref[...] = jnp.where(source == wanted, 1.0, 0.0).astype(jnp.bfloat16)
        begin += count
    row = lax.broadcasted_iota(jnp.int32, (rows, rows), 0)
    column = lax.broadcasted_iota(jnp.int32, (rows, rows), 1)
    flip = jnp.where(row + column == rows - 1, 1.0, 0.0).astype(jnp.bfloat16)
    flipped = jnp.dot(flip, reverse_ref[...], preferred_element_type=jnp.float32)
    flipped_ref[...] = flipped.astype(jnp.bfloat16)


def order(place, reverse_embed):
    rows, width = reverse_embed.shape
    part = width // PIECES
    inside = pl.BlockSpec(memory_space=pltpu.VMEM)
    outs = pl.pallas_call(
        order_kernel,
        out_shape=[jax.ShapeDtypeStruct((width, count * part), jnp.bfloat16) for count in PARTS]
        + [jax.ShapeDtypeStruct((rows, width), jnp.bfloat16), TOKEN],
        in_specs=[pl.BlockSpec(memory_space=pltpu.SMEM), inside],
        out_specs=[inside] * 5,
        compiler_params=pltpu.CompilerParams(vmem_limit_bytes=VMEM_LIMIT),
        cost_estimate=pl.CostEstimate(
            flops=16 * rows * width * width, bytes_accessed=8 * rows * width, transcendentals=0
        ),
        name="order",
    )(place, reverse_embed)
    return outs[:3], outs[3], outs[4]


def edge_tile(after, before):
    width = after.shape[1]
    edge = lax.broadcasted_iota(jnp.int32, (EDGE, width), 0)
    tile = jnp.where(edge == 0, after, jnp.where(edge == EDGE - 1, before, 0.0))
    return tile.astype(jnp.bfloat16)


def prepare_kernel(forward_ref, flipped_ref, low_ref, high_ref, *refs):
    move_refs, x_refs, y_refs, (away_ref, token_ref, edge_ref) = (
        refs[:3], refs[3:6], refs[6:9], refs[9:],
    )
    token_ref[...] = jnp.zeros_like(token_ref)
    rows = forward_ref.shape[0]
    kept = rows - AWAY
    low = low_ref[...].astype(jnp.float32)
    high = high_ref[...].astype(jnp.float32)
    next_row = flipped_ref[pl.ds(kept, EDGE), :].astype(jnp.float32)[0:1]
    past_row = flipped_ref[pl.ds(kept - EDGE, EDGE), :].astype(jnp.float32)[EDGE - 1 :]
    away_ref[:AWAY, :] = flipped_ref[pl.ds(kept, AWAY), :]
    away_ref[AWAY:, :] = edge_tile(low[1:2], past_row)
    edge_ref[:EDGE, :] = edge_tile(high[0:1], low[0:1])
    edge_ref[EDGE:, :] = edge_tile(next_row, high[1:2])
    for x_ref, y_ref, move_ref in zip(x_refs, y_refs, move_refs):
        edges = jnp.dot(edge_ref[...], move_ref[...], preferred_element_type=jnp.float32)
        edges = edges.astype(jnp.bfloat16)
        x_ref[:rows, :] = jnp.dot(
            forward_ref[...], move_ref[...], preferred_element_type=jnp.float32
        ).astype(jnp.bfloat16)
        x_ref[rows:, :] = edges[:EDGE]
        y_ref[:kept, :] = jnp.dot(
            flipped_ref[pl.ds(0, kept), :], move_ref[...], preferred_element_type=jnp.float32
        ).astype(jnp.bfloat16)
        y_ref[kept:, :] = edges[EDGE:]


def prepare(forward_embed, flipped, low, high, moves):
    rows, width = forward_embed.shape
    kept = rows - AWAY
    part = width // PIECES
    inside = pl.BlockSpec(memory_space=pltpu.VMEM)

    def stripes(height):
        return [jax.ShapeDtypeStruct((height, count * part), jnp.bfloat16) for count in PARTS]

    outs = pl.pallas_call(
        prepare_kernel,
        out_shape=stripes(rows + EDGE)
        + stripes(kept + EDGE)
        + [jax.ShapeDtypeStruct((AWAY + EDGE, width), jnp.bfloat16), TOKEN],
        in_specs=[inside] * 7,
        out_specs=[inside] * 8,
        scratch_shapes=[pltpu.VMEM((2 * EDGE, width), jnp.bfloat16)],
        compiler_params=pltpu.CompilerParams(vmem_limit_bytes=VMEM_LIMIT),
        cost_estimate=pl.CostEstimate(flops=1000, bytes_accessed=1000, transcendentals=0),
        name="prepare",
    )(forward_embed, flipped, low, high, *moves)
    return list(zip(outs[:3], outs[3:6])), outs[6], outs[7]


def convolve(x, flipped, blocks, columns):
    rows = x.shape[0] - EDGE
    total = None
    for tap in range(3):
        weight = jnp.concatenate([block[tap, :, columns] for block in blocks], axis=0)
        value = jnp.dot(x, weight, preferred_element_type=jnp.float32)
        shift = tap - 1 if flipped else 1 - tap
        if shift:
            value = pltpu.roll(value, shift % (rows + EDGE), 0)
        value = value[:rows]
        total = value if total is None else total + value
    return total


def partial_kernel(count, first, *refs):
    strands, blocks, refs = refs[:2], refs[2 : 2 + count], refs[2 + count :]
    out_refs, token_ref = refs[-3:-1], refs[-1]
    token_ref[...] = jnp.zeros_like(token_ref)
    @pl.loop(0, out_refs[0].shape[1] // TILE)
    def _(tile):
        columns = pl.ds(pl.multiple_of(tile * TILE, TILE), TILE)
        for strand in range(2):
            acc = convolve(strands[strand][...], strand == 1, blocks, columns)
            if not first:
                acc = acc + refs[strand][:, columns]
            out_refs[strand][:, columns] = acc


def partial_sum(strands, sources, prev):
    rows = [x.shape[0] - EDGE for x in strands]
    depth, channels = strands[0].shape[1], sources[0].shape[2]
    operands = [*strands, *sources] + ([] if prev is None else list(prev))
    inside = pl.BlockSpec(memory_space=pltpu.VMEM)
    last = len(operands)
    forward, reverse, token = pl.pallas_call(
        functools.partial(partial_kernel, len(sources), prev is None),
        out_shape=[jax.ShapeDtypeStruct((count, channels), jnp.float32) for count in rows]
        + [TOKEN],
        in_specs=[inside] * last,
        out_specs=[inside] * 3,
        input_output_aliases={} if prev is None else {last - 2: 0, last - 1: 1},
        compiler_params=pltpu.CompilerParams(vmem_limit_bytes=VMEM_LIMIT),
        cost_estimate=pl.CostEstimate(
            flops=6 * sum(rows) * depth * channels,
            bytes_accessed=6 * depth * channels,
            transcendentals=0,
        ),
        name="partial_sum",
    )(*operands)
    return (forward, reverse), token


def gelu(acc):
    return (0.5 * acc * (1.0 + lax.erf(acc * INV_SQRT2))).astype(jnp.bfloat16)


def predict(hidden_ref, head_ref, head_bias_ref, out_ref):
    rows = out_ref.shape[0]
    @pl.loop(0, rows // ROWS, unroll=True)
    def _(block):
        here = pl.ds(pl.multiple_of(block * ROWS, ROWS), ROWS)
        logits = jnp.dot(hidden_ref[here, :], head_ref[...], preferred_element_type=jnp.float32)
        logits = logits + head_bias_ref[...]
        tracks = jnp.maximum(logits, 0.0) + jnp.log1p(jnp.exp(-jnp.abs(logits)))
        out_ref[here, :] = tracks.astype(jnp.bfloat16)


def finish_kernel(flipped, count, x_ref, *refs):
    sources, refs = refs[:count], refs[count:]
    prev_ref, bias_ref, head_ref, head_bias_ref, out_ref, hidden_ref = refs
    @pl.loop(0, hidden_ref.shape[1] // TILE, unroll=True)
    def _(tile):
        here = pl.ds(pl.multiple_of(tile * TILE, TILE), TILE)
        acc = convolve(x_ref[...], flipped, sources, here)
        hidden_ref[:, here] = gelu(acc + prev_ref[:, here] + bias_ref[:, here])

    predict(hidden_ref, head_ref, head_bias_ref, out_ref)


def finish(flipped, x, sources, prev, bias, head, head_bias):
    rows, depth = x.shape[0] - EDGE, x.shape[1]
    channels, tracks = head.shape
    inside = pl.BlockSpec(memory_space=pltpu.VMEM)
    return pl.pallas_call(
        functools.partial(finish_kernel, flipped, len(sources)),
        out_shape=jax.ShapeDtypeStruct((rows, tracks), jnp.bfloat16),
        in_specs=[inside] * (len(sources) + 5),
        out_specs=inside,
        scratch_shapes=[pltpu.VMEM((rows, channels), jnp.bfloat16)],
        compiler_params=pltpu.CompilerParams(vmem_limit_bytes=VMEM_LIMIT),
        cost_estimate=pl.CostEstimate(
            flops=2 * rows * channels * (3 * depth + tracks),
            bytes_accessed=6 * depth * channels + 2 * channels * tracks,
            transcendentals=rows * channels,
        ),
        name="finish",
    )(x, *sources, prev, bias, head, head_bias[None])


def whole_kernel(sizes, forward_ref, away_ref, *refs):
    moves, refs = refs[: len(sizes)], refs[len(sizes) :]
    sources, refs = refs[: sum(sizes)], refs[sum(sizes) :]
    bias_ref, head_ref, head_bias_ref, out_ref, hidden_ref = refs
    stripes = [
        jnp.dot(away_ref[...], move[...], preferred_element_type=jnp.float32).astype(jnp.bfloat16)
        for move in moves
    ]
    @pl.loop(0, hidden_ref.shape[1] // TILE)
    def _(tile):
        here = pl.ds(pl.multiple_of(tile * TILE, TILE), TILE)
        acc, begin = bias_ref[:, here], 0
        for stripe, count in zip(stripes, sizes):
            acc = acc + convolve(stripe, True, sources[begin : begin + count], here)
            begin += count
        hidden_ref[:, here] = gelu(acc)

    predict(hidden_ref, head_ref, head_bias_ref, out_ref)


def whole(forward_tracks, away, moves, sources, bias, head, head_bias):
    rows = away.shape[0] - EDGE
    channels, tracks = head.shape
    inside = pl.BlockSpec(memory_space=pltpu.VMEM)
    return pl.pallas_call(
        functools.partial(whole_kernel, SOURCES),
        out_shape=jax.ShapeDtypeStruct((rows, tracks), jnp.bfloat16),
        in_specs=[inside] * (len(moves) + len(sources) + 5),
        out_specs=inside,
        scratch_shapes=[pltpu.VMEM((rows, channels), jnp.bfloat16)],
        compiler_params=pltpu.CompilerParams(vmem_limit_bytes=VMEM_LIMIT),
        cost_estimate=pl.CostEstimate(
            flops=2 * rows * channels * (4 * channels + tracks),
            bytes_accessed=6 * channels * channels,
            transcendentals=rows * channels,
        ),
        name="whole",
    )(forward_tracks, away, *moves, *sources, bias, head, head_bias[None])


def per_device(forward_embed, reverse_embed, conv_weight, conv_bias, head_weight, head_bias):
    own = conv_weight[0]
    x, y, core = lax.axis_index("x"), lax.axis_index("y_lo"), lax.axis_index("core")
    ends = XN * 2 * CN

    def seq(x_of, y_of, core_of):
        return (x_of % XN) * 4 + y_of * 2 + core_of

    step = 1 - 2 * core
    back, fore, far = x - step + XN, x + step + XN, x + 2
    other, over = 1 - core, 1 - y
    odd = lax.axis_index("z") % 2

    def both(*shards):
        return [2 * shard + half for shard in shards for half in range(2)]

    place = jnp.stack(
        both(
            seq(x, y, core), seq(x, y, other), seq(x, over, core), seq(x, over, other),
            seq(back, y, core), seq(fore, y, other),
            seq(back, over, core), seq(fore, over, other), seq(far, y, core), seq(far, y, other),
        )
        + [2 * seq(back, y, other) + odd, 2 * seq(fore, y, core) + odd]
        + [2 * seq(back, y, other) + 1 - odd, 2 * seq(fore, y, core) + 1 - odd]
        + both(
            seq(back, over, other), seq(fore, over, core),
            seq(far, over, core), seq(far, over, other),
        )
    ).astype(jnp.int32)

    with jax.named_scope("near"):
        near = x_shift(own)
    with jax.named_scope("across"):
        across = y_shift(own)
    with jax.named_scope("sibling"):
        sibling = core_swap(own)
    sibling_half = halve(place, sibling)
    with jax.named_scope("second"):
        second = x_shift(sibling_half)
    up = [(i, i + 1) for i in range(ends - 1)]
    down = [(b, a) for a, b in up]
    with jax.named_scope("low"):
        low = lax.ppermute(jnp.stack([forward_embed[-1], reverse_embed[-1]]), SEQ, up)
    with jax.named_scope("high"):
        high = lax.ppermute(jnp.stack([forward_embed[0], reverse_embed[0]]), SEQ, down)
    moves, flipped, token = order(place, reverse_embed)
    near, across, low, high = fence(token, near, across, low, high)

    with jax.named_scope("distant"):
        distant = x_shift(near)
    with jax.named_scope("near_over"):
        near_over = y_shift(near)
    with jax.named_scope("across_b"):
        across_b = core_swap(across)
    with jax.named_scope("near_b"):
        near_b = core_swap(near)
    (x_1, x_2, x_3), away, token = prepare(forward_embed, flipped, low, high, moves)
    shards_1 = [own, sibling, across, across_b, near, near_b]
    acc, token = partial_sum(x_1, shards_1, None)
    distant, near_over, across_b, second = fence(token, distant, near_over, across_b, second)
    shards_1[3] = across_b

    with jax.named_scope("second_z"):
        second_z = z_shift(second)
    with jax.named_scope("second_over"):
        second_over = x_shift(across_b)
    with jax.named_scope("distant_over"):
        distant_over = y_shift(distant)
    with jax.named_scope("near_over_b"):
        near_over_b = core_swap(near_over)
    with jax.named_scope("distant_b"):
        distant_b = core_swap(distant)
    shards_2 = [near_over, near_over_b, distant, distant_b]
    acc, token = partial_sum(x_2, shards_2, acc)
    with jax.named_scope("second_b"):
        second_b = core_swap(after(token, second))
    with jax.named_scope("second_z_b"):
        second_z_b = core_swap(after(token, second_z))
    second_over, distant_over, second_z_b, second_b, away = fence(
        token, second_over, distant_over, second_z_b, second_b, away
    )

    mirror = [(i, ends - 1 - i) for i in range(ends)]
    with jax.named_scope("away"):
        away = lax.ppermute(away, SEQ, mirror)
    with jax.named_scope("second_over_b"):
        second_over_b = core_swap(second_over)
    with jax.named_scope("distant_over_b"):
        distant_over_b = core_swap(distant_over)
    shards_3 = [second, second_b, second_z, second_z_b, second_over, second_over_b, distant_over, distant_over_b]
    rest = (conv_bias, head_weight, head_bias)
    reverse_tracks = finish(True, x_3[1], shards_3, acc[1], *rest)
    with jax.named_scope("mirrored"):
        mirrored = lax.ppermute(reverse_tracks, SEQ, mirror)
    forward_tracks = finish(False, x_3[0], shards_3, acc[0], *rest)
    away_tracks = whole(forward_tracks, away, moves, shards_1 + shards_2 + shards_3, *rest)
    reverse = jnp.concatenate([mirrored, away_tracks])
    mean = 0.5 * (forward_tracks.astype(jnp.float32) + reverse.astype(jnp.float32))
    return mean.astype(jnp.bfloat16)


def solution(mesh):
    fine = Mesh(mesh.devices.reshape(2, 8, XN, 2, CN), AXES)
    return jax.shard_map(
        per_device,
        mesh=fine,
        in_specs=(
            P(AXES, None),
            P(AXES, None),
            P(None, None, SEQ, None),
            P(),
            P(),
            P(),
        ),
        out_specs=P(AXES, None),
        check_vma=False,
    )
```

```python
import functools

import jax
import jax.numpy as jnp
from jax import lax
from jax.experimental import pallas as pl
from jax.experimental.pallas import tpu as pltpu
from jax.sharding import Mesh
from jax.sharding import PartitionSpec as P

AXES = ("y_hi", "z", "x", "y_lo", "core")
SEQ = ("x", "y_lo", "core")
XN, YN, ZN, CN = 4, 4, 8, 2
VMEM_LIMIT = 24 * 1024 * 1024
EDGE = 16
TILE = 512
PARTS = (12, 8, 12)
SOURCES = (6, 4, 8)
PIECES = 32
FIRST_HALF = 20
ROWS = 96
AWAY = 96
TOKEN = jax.ShapeDtypeStruct((8, 128), jnp.float32)
INV_SQRT2 = 0.7071067811865476


def core_swap(value):
    return lax.ppermute(value, "core", [(0, 1), (1, 0)])


def x_shift(value):
    route = []
    for x in range(XN):
        route += [(x * 2, (x + 1) % XN * 2), (x * 2 + 1, (x - 1) % XN * 2 + 1)]
    return lax.ppermute(value, ("x", "core"), route)


def y_shift(value):
    route = []
    for y in range(YN):
        route += [(y * 2, (y + 1) % YN * 2), (y * 2 + 1, (y - 1) % YN * 2 + 1)]
    return lax.ppermute(value, ("y_hi", "y_lo", "core"), route)


def z_shift(value):
    route = []
    for z in range(ZN):
        route += [(z * 2, (z + 1) % ZN * 2), (z * 2 + 1, (z - 1) % ZN * 2 + 1)]
    return lax.ppermute(value, ("z", "core"), route)


def fence_kernel(count, *refs):
    for source, target in zip(refs[:count], refs[-count:]):
        target[...] = source[...]


def fence(token, *values):
    inside = pl.BlockSpec(memory_space=pltpu.VMEM)
    operands = values if token is None else (*values, token)
    return pl.pallas_call(
        functools.partial(fence_kernel, len(values)),
        out_shape=[jax.ShapeDtypeStruct(v.shape, v.dtype) for v in values],
        in_specs=[inside] * len(operands),
        out_specs=[inside] * len(values),
        input_output_aliases={i: i for i in range(len(values))},
        compiler_params=pltpu.CompilerParams(vmem_limit_bytes=8 * 1024 * 1024),
        name="fence",
    )(*operands)


def edge_tile(after, before):
    width = after.shape[1]
    edge = lax.broadcasted_iota(jnp.int32, (EDGE, width), 0)
    tile = jnp.where(edge == 0, after, jnp.where(edge == EDGE - 1, before, 0.0))
    return tile.astype(jnp.bfloat16)


def after_kernel(source_ref, token_ref, out_ref):
    out_ref[...] = source_ref[...]


def after(token, value):
    inside = pl.BlockSpec(memory_space=pltpu.VMEM)
    return pl.pallas_call(
        after_kernel,
        out_shape=jax.ShapeDtypeStruct(value.shape, value.dtype),
        in_specs=[inside] * 2,
        out_specs=inside,
        compiler_params=pltpu.CompilerParams(vmem_limit_bytes=8 * 1024 * 1024),
        name="after",
    )(value, token)


def halve_kernel(place_ref, shard_ref, out_ref):
    half = out_ref.shape[1]
    odd = lax.rem(place_ref[FIRST_HALF], 2)

    @pl.when(odd == 0)
    def _():
        out_ref[...] = shard_ref[:, pl.ds(0, half), :]

    @pl.when(odd == 1)
    def _():
        out_ref[...] = shard_ref[:, pl.ds(half, half), :]


def halve(place, shard):
    taps, rows, columns = shard.shape
    inside = pl.BlockSpec(memory_space=pltpu.VMEM)
    return pl.pallas_call(
        halve_kernel,
        out_shape=jax.ShapeDtypeStruct((taps, rows // 2, columns), shard.dtype),
        in_specs=[pl.BlockSpec(memory_space=pltpu.SMEM), inside],
        out_specs=inside,
        compiler_params=pltpu.CompilerParams(vmem_limit_bytes=8 * 1024 * 1024),
        name="halve",
    )(place, shard)


def order_kernel(place_ref, reverse_ref, *refs):
    move_refs, flipped_ref, token_ref = refs[:3], refs[3], refs[4]
    token_ref[...] = jnp.zeros_like(token_ref)
    rows, width = reverse_ref.shape
    part = width // PIECES
    begin = 0
    for move_ref, count in zip(move_refs, PARTS):
        size = count * part
        lane = lax.broadcasted_iota(jnp.int32, (1, size), 1)
        wanted = jnp.zeros((1, size), jnp.int32)
        for block in range(count):
            inside = (lane >= block * part) & (lane < (block + 1) * part)
            wanted = jnp.where(inside, lane + (place_ref[begin + block] - block) * part, wanted)
        source = lax.broadcasted_iota(jnp.int32, (width, size), 0)
        move_ref[...] = jnp.where(source == wanted, 1.0, 0.0).astype(jnp.bfloat16)
        begin += count
    row = lax.broadcasted_iota(jnp.int32, (rows, rows), 0)
    column = lax.broadcasted_iota(jnp.int32, (rows, rows), 1)
    flip = jnp.where(row + column == rows - 1, 1.0, 0.0).astype(jnp.bfloat16)
    flipped = jnp.dot(flip, reverse_ref[...], preferred_element_type=jnp.float32)
    flipped_ref[...] = flipped.astype(jnp.bfloat16)


def order(place, reverse_embed):
    rows, width = reverse_embed.shape
    part = width // PIECES
    inside = pl.BlockSpec(memory_space=pltpu.VMEM)
    outs = pl.pallas_call(
        order_kernel,
        out_shape=[jax.ShapeDtypeStruct((width, count * part), jnp.bfloat16) for count in PARTS]
        + [jax.ShapeDtypeStruct((rows, width), jnp.bfloat16), TOKEN],
        in_specs=[pl.BlockSpec(memory_space=pltpu.SMEM), inside],
        out_specs=[inside] * 5,
        compiler_params=pltpu.CompilerParams(vmem_limit_bytes=VMEM_LIMIT),
        cost_estimate=pl.CostEstimate(
            flops=16 * rows * width * width, bytes_accessed=8 * rows * width, transcendentals=0
        ),
        name="order",
    )(place, reverse_embed)
    return outs[:3], outs[3], outs[4]


def edge_tile(after, before):
    width = after.shape[1]
    edge = lax.broadcasted_iota(jnp.int32, (EDGE, width), 0)
    tile = jnp.where(edge == 0, after, jnp.where(edge == EDGE - 1, before, 0.0))
    return tile.astype(jnp.bfloat16)


def prepare_kernel(forward_ref, flipped_ref, low_ref, high_ref, *refs):
    move_refs, x_refs, y_refs, (away_ref, token_ref, edge_ref) = (
        refs[:3], refs[3:6], refs[6:9], refs[9:],
    )
    token_ref[...] = jnp.zeros_like(token_ref)
    rows = forward_ref.shape[0]
    kept = rows - AWAY
    low = low_ref[...].astype(jnp.float32)
    high = high_ref[...].astype(jnp.float32)
    next_row = flipped_ref[pl.ds(kept, EDGE), :].astype(jnp.float32)[0:1]
    past_row = flipped_ref[pl.ds(kept - EDGE, EDGE), :].astype(jnp.float32)[EDGE - 1 :]
    away_ref[:AWAY, :] = flipped_ref[pl.ds(kept, AWAY), :]
    away_ref[AWAY:, :] = edge_tile(low[1:2], past_row)
    edge_ref[:EDGE, :] = edge_tile(high[0:1], low[0:1])
    edge_ref[EDGE:, :] = edge_tile(next_row, high[1:2])
    for x_ref, y_ref, move_ref in zip(x_refs, y_refs, move_refs):
        edges = jnp.dot(edge_ref[...], move_ref[...], preferred_element_type=jnp.float32)
        edges = edges.astype(jnp.bfloat16)
        x_ref[:rows, :] = jnp.dot(
            forward_ref[...], move_ref[...], preferred_element_type=jnp.float32
        ).astype(jnp.bfloat16)
        x_ref[rows:, :] = edges[:EDGE]
        y_ref[:kept, :] = jnp.dot(
            flipped_ref[pl.ds(0, kept), :], move_ref[...], preferred_element_type=jnp.float32
        ).astype(jnp.bfloat16)
        y_ref[kept:, :] = edges[EDGE:]


def prepare(forward_embed, flipped, low, high, moves):
    rows, width = forward_embed.shape
    kept = rows - AWAY
    part = width // PIECES
    inside = pl.BlockSpec(memory_space=pltpu.VMEM)

    def stripes(height):
        return [jax.ShapeDtypeStruct((height, count * part), jnp.bfloat16) for count in PARTS]

    outs = pl.pallas_call(
        prepare_kernel,
        out_shape=stripes(rows + EDGE)
        + stripes(kept + EDGE)
        + [jax.ShapeDtypeStruct((AWAY + EDGE, width), jnp.bfloat16), TOKEN],
        in_specs=[inside] * 7,
        out_specs=[inside] * 8,
        scratch_shapes=[pltpu.VMEM((2 * EDGE, width), jnp.bfloat16)],
        compiler_params=pltpu.CompilerParams(vmem_limit_bytes=VMEM_LIMIT),
        cost_estimate=pl.CostEstimate(flops=1000, bytes_accessed=1000, transcendentals=0),
        name="prepare",
    )(forward_embed, flipped, low, high, *moves)
    return list(zip(outs[:3], outs[3:6])), outs[6], outs[7]


def convolve(x, flipped, blocks, columns):
    rows = x.shape[0] - EDGE
    total = None
    for tap in range(3):
        weight = jnp.concatenate([block[tap, :, columns] for block in blocks], axis=0)
        value = jnp.dot(x, weight, preferred_element_type=jnp.float32)
        shift = tap - 1 if flipped else 1 - tap
        if shift:
            value = pltpu.roll(value, shift % (rows + EDGE), 0)
        value = value[:rows]
        total = value if total is None else total + value
    return total


def partial_kernel(count, first, *refs):
    strands, blocks, refs = refs[:2], refs[2 : 2 + count], refs[2 + count :]
    out_refs, token_ref = refs[-3:-1], refs[-1]
    token_ref[...] = jnp.zeros_like(token_ref)
    @pl.loop(0, out_refs[0].shape[1] // TILE)
    def _(tile):
        columns = pl.ds(pl.multiple_of(tile * TILE, TILE), TILE)
        for strand in range(2):
            acc = convolve(strands[strand][...], strand == 1, blocks, columns)
            if not first:
                acc = acc + refs[strand][:, columns]
            out_refs[strand][:, columns] = acc


def partial_sum(strands, sources, prev):
    rows = [x.shape[0] - EDGE for x in strands]
    depth, channels = strands[0].shape[1], sources[0].shape[2]
    operands = [*strands, *sources] + ([] if prev is None else list(prev))
    inside = pl.BlockSpec(memory_space=pltpu.VMEM)
    last = len(operands)
    forward, reverse, token = pl.pallas_call(
        functools.partial(partial_kernel, len(sources), prev is None),
        out_shape=[jax.ShapeDtypeStruct((count, channels), jnp.float32) for count in rows]
        + [TOKEN],
        in_specs=[inside] * last,
        out_specs=[inside] * 3,
        input_output_aliases={} if prev is None else {last - 2: 0, last - 1: 1},
        compiler_params=pltpu.CompilerParams(vmem_limit_bytes=VMEM_LIMIT),
        cost_estimate=pl.CostEstimate(
            flops=6 * sum(rows) * depth * channels,
            bytes_accessed=6 * depth * channels,
            transcendentals=0,
        ),
        name="partial_sum",
    )(*operands)
    return (forward, reverse), token


def gelu(acc):
    return (0.5 * acc * (1.0 + lax.erf(acc * INV_SQRT2))).astype(jnp.bfloat16)


def predict(hidden_ref, head_ref, head_bias_ref, out_ref):
    rows = out_ref.shape[0]
    @pl.loop(0, rows // ROWS, unroll=True)
    def _(block):
        here = pl.ds(pl.multiple_of(block * ROWS, ROWS), ROWS)
        logits = jnp.dot(hidden_ref[here, :], head_ref[...], preferred_element_type=jnp.float32)
        logits = logits + head_bias_ref[...]
        tracks = jnp.maximum(logits, 0.0) + jnp.log1p(jnp.exp(-jnp.abs(logits)))
        out_ref[here, :] = tracks.astype(jnp.bfloat16)


def finish_kernel(flipped, count, x_ref, *refs):
    sources, refs = refs[:count], refs[count:]
    prev_ref, bias_ref, head_ref, head_bias_ref, out_ref, hidden_ref = refs
    @pl.loop(0, hidden_ref.shape[1] // TILE, unroll=True)
    def _(tile):
        here = pl.ds(pl.multiple_of(tile * TILE, TILE), TILE)
        acc = convolve(x_ref[...], flipped, sources, here)
        hidden_ref[:, here] = gelu(acc + prev_ref[:, here] + bias_ref[:, here])

    predict(hidden_ref, head_ref, head_bias_ref, out_ref)


def finish(flipped, x, sources, prev, bias, head, head_bias):
    rows, depth = x.shape[0] - EDGE, x.shape[1]
    channels, tracks = head.shape
    inside = pl.BlockSpec(memory_space=pltpu.VMEM)
    return pl.pallas_call(
        functools.partial(finish_kernel, flipped, len(sources)),
        out_shape=jax.ShapeDtypeStruct((rows, tracks), jnp.bfloat16),
        in_specs=[inside] * (len(sources) + 5),
        out_specs=inside,
        scratch_shapes=[pltpu.VMEM((rows, channels), jnp.bfloat16)],
        compiler_params=pltpu.CompilerParams(vmem_limit_bytes=VMEM_LIMIT),
        cost_estimate=pl.CostEstimate(
            flops=2 * rows * channels * (3 * depth + tracks),
            bytes_accessed=6 * depth * channels + 2 * channels * tracks,
            transcendentals=rows * channels,
        ),
        name="finish",
    )(x, *sources, prev, bias, head, head_bias[None])


def whole_kernel(sizes, away_ref, *refs):
    moves, refs = refs[: len(sizes)], refs[len(sizes) :]
    sources, refs = refs[: sum(sizes)], refs[sum(sizes) :]
    bias_ref, head_ref, head_bias_ref, out_ref, hidden_ref = refs
    stripes = [
        jnp.dot(away_ref[...], move[...], preferred_element_type=jnp.float32).astype(jnp.bfloat16)
        for move in moves
    ]
    @pl.loop(0, hidden_ref.shape[1] // TILE)
    def _(tile):
        here = pl.ds(pl.multiple_of(tile * TILE, TILE), TILE)
        acc, begin = bias_ref[:, here], 0
        for stripe, count in zip(stripes, sizes):
            acc = acc + convolve(stripe, True, sources[begin : begin + count], here)
            begin += count
        hidden_ref[:, here] = gelu(acc)

    predict(hidden_ref, head_ref, head_bias_ref, out_ref)


def whole(away, moves, sources, bias, head, head_bias):
    rows = away.shape[0] - EDGE
    channels, tracks = head.shape
    inside = pl.BlockSpec(memory_space=pltpu.VMEM)
    return pl.pallas_call(
        functools.partial(whole_kernel, SOURCES),
        out_shape=jax.ShapeDtypeStruct((rows, tracks), jnp.bfloat16),
        in_specs=[inside] * (len(moves) + len(sources) + 4),
        out_specs=inside,
        scratch_shapes=[pltpu.VMEM((rows, channels), jnp.bfloat16)],
        compiler_params=pltpu.CompilerParams(vmem_limit_bytes=VMEM_LIMIT),
        cost_estimate=pl.CostEstimate(
            flops=2 * rows * channels * (4 * channels + tracks),
            bytes_accessed=6 * channels * channels,
            transcendentals=rows * channels,
        ),
        name="whole",
    )(away, *moves, *sources, bias, head, head_bias[None])


def per_device(forward_embed, reverse_embed, conv_weight, conv_bias, head_weight, head_bias):
    own = conv_weight[0]
    x, y, core = lax.axis_index("x"), lax.axis_index("y_lo"), lax.axis_index("core")
    ends = XN * 2 * CN

    def seq(x_of, y_of, core_of):
        return (x_of % XN) * 4 + y_of * 2 + core_of

    step = 1 - 2 * core
    back, fore, far = x - step + XN, x + step + XN, x + 2
    other, over = 1 - core, 1 - y
    odd = lax.axis_index("z") % 2

    def both(*shards):
        return [2 * shard + half for shard in shards for half in range(2)]

    place = jnp.stack(
        both(
            seq(x, y, core), seq(x, y, other), seq(x, over, core), seq(x, over, other),
            seq(back, y, core), seq(fore, y, other),
            seq(back, over, core), seq(fore, over, other), seq(far, y, core), seq(far, y, other),
        )
        + [2 * seq(back, y, other) + odd, 2 * seq(fore, y, core) + odd]
        + [2 * seq(back, y, other) + 1 - odd, 2 * seq(fore, y, core) + 1 - odd]
        + both(
            seq(back, over, other), seq(fore, over, core),
            seq(far, over, core), seq(far, over, other),
        )
    ).astype(jnp.int32)

    with jax.named_scope("near"):
        near = x_shift(own)
    with jax.named_scope("across"):
        across = y_shift(own)
    with jax.named_scope("sibling"):
        sibling = core_swap(own)
    sibling_half = halve(place, sibling)
    with jax.named_scope("second"):
        second = x_shift(sibling_half)
    up = [(i, i + 1) for i in range(ends - 1)]
    down = [(b, a) for a, b in up]
    with jax.named_scope("low"):
        low = lax.ppermute(jnp.stack([forward_embed[-1], reverse_embed[-1]]), SEQ, up)
    with jax.named_scope("high"):
        high = lax.ppermute(jnp.stack([forward_embed[0], reverse_embed[0]]), SEQ, down)
    moves, flipped, token = order(place, reverse_embed)
    near, across, low, high = fence(token, near, across, low, high)

    with jax.named_scope("distant"):
        distant = x_shift(near)
    with jax.named_scope("near_over"):
        near_over = y_shift(near)
    with jax.named_scope("across_b"):
        across_b = core_swap(across)
    with jax.named_scope("near_b"):
        near_b = core_swap(near)
    (x_1, x_2, x_3), away, token = prepare(forward_embed, flipped, low, high, moves)
    shards_1 = [own, sibling, across, across_b, near, near_b]
    acc, token = partial_sum(x_1, shards_1, None)
    distant, near_over, across_b, second = fence(token, distant, near_over, across_b, second)
    shards_1[3] = across_b

    with jax.named_scope("second_z"):
        second_z = z_shift(second)
    with jax.named_scope("second_over"):
        second_over = x_shift(across_b)
    with jax.named_scope("distant_over"):
        distant_over = y_shift(distant)
    with jax.named_scope("near_over_b"):
        near_over_b = core_swap(near_over)
    with jax.named_scope("distant_b"):
        distant_b = core_swap(distant)
    shards_2 = [near_over, near_over_b, distant, distant_b]
    acc, token = partial_sum(x_2, shards_2, acc)
    with jax.named_scope("second_b"):
        second_b = core_swap(after(token, second))
    second_over, distant_over, second_z, second_b, away = fence(
        token, second_over, distant_over, second_z, second_b, away
    )

    mirror = [(i, ends - 1 - i) for i in range(ends)]
    with jax.named_scope("away"):
        away = lax.ppermute(away, SEQ, mirror)
    with jax.named_scope("second_over_b"):
        second_over_b = core_swap(second_over)
    with jax.named_scope("distant_over_b"):
        distant_over_b = core_swap(distant_over)
    with jax.named_scope("second_z_b"):
        second_z_b = core_swap(second_z)
    shards_3 = [second, second_b, second_z, second_z_b, second_over, second_over_b, distant_over, distant_over_b]
    rest = (conv_bias, head_weight, head_bias)
    reverse_tracks = finish(True, x_3[1], shards_3, acc[1], *rest)
    with jax.named_scope("mirrored"):
        mirrored = lax.ppermute(reverse_tracks, SEQ, mirror)
    forward_tracks = finish(False, x_3[0], shards_3, acc[0], *rest)
    away_tracks = whole(away, moves, shards_1 + shards_2 + shards_3, *rest)
    reverse = jnp.concatenate([mirrored, away_tracks])
    mean = 0.5 * (forward_tracks.astype(jnp.float32) + reverse.astype(jnp.float32))
    return mean.astype(jnp.bfloat16)


def solution(mesh):
    fine = Mesh(mesh.devices.reshape(2, 8, XN, 2, CN), AXES)
    return jax.shard_map(
        per_device,
        mesh=fine,
        in_specs=(
            P(AXES, None),
            P(AXES, None),
            P(None, None, SEQ, None),
            P(),
            P(),
            P(),
        ),
        out_specs=P(AXES, None),
        check_vma=False,
    )
```
